512 devices in a mesh: wide: 64 (over y, z), narrow: 8 (over x, core).
Axes of the slice: x: 4, y: 4, z: 16, core: 2. Of those that a mesh axis runs over, the one named last changes fastest.
Arguments:
- right_side: float32 [16, 512, 1024], P(None, 'wide', 'narrow'), may hold values from -8 to 8
- capacity: float32 [16, 512, 1024], P(None, 'wide', 'narrow'), may hold values from 0.1 to 2
- phase: int32 [16, 512, 1024], P(None, 'wide', 'narrow'), may hold values from 0 to 2
- mold_flags: int32 [16, 512, 1024], P(None, 'wide', 'narrow'), may hold values 0 or 1
Outputs:
- adjoint_field: float32 [16, 512, 1024], P(None, 'wide', 'narrow')
- residual: float32 [16, 512, 1024], P(None, 'wide', 'narrow')
The draws below stay inside these ranges and needn't reach their ends.
All inputs are finite; a program needn't handle non-finite values. No bound on the sum of `mold_flags` on one device may be relied on, other than what follows from the above.
Results may differ from the reference program's by a relative error of at most 0.0003.
Values sent between devices are 32-bit elements; how exact they have to be, the bound alone decides.
No kernel may reach another device: no remote copies, remote signals or barrier semaphores. Data moves between devices by JAX's collectives and lax.ppermute only.
A program may use at most 64 MiB of HBM per device.

```python
import math
import jax
import jax.numpy as jnp

NZ = 16
LEVELS = 4
COARSE_SWEEPS = 4
ITERS = 2
NX = 512
NY = 1024


def plant(result, rng, low, high):
    longest = result.shape.index(max(result.shape))
    spots = []
    for shift in (0, 1):
        where = [jax.random.randint(jax.random.fold_in(rng, axis), (), 0, length) for axis, length in enumerate(result.shape)]
        where[longest] = (where[longest] + shift) % result.shape[longest]
        spots.append(tuple(where))
    return result.at[spots[0]].set(low).at[spots[1]].set(high)


def level_of(rng, extent, split, smallest, top_value):
    def one(position, blocks):
        draws = jax.random.uniform(jax.random.fold_in(jax.random.fold_in(rng, 6), position), (blocks,), jnp.float32, smallest / len(split), top_value / len(split))
        return jnp.repeat(jnp.exp(draws), extent[position] // blocks).reshape((-1,) + (1,) * (len(extent) - position - 1))

    gain = one(*split[0])
    for cut in split[1:]:
        gain = gain * one(*cut)
    return gain


def bell_draw(stream_key, shape, scale, most, cuts=(), dtype=jnp.bfloat16):
    factor_of = level_of(stream_key, shape, cuts, -0.22, 0.18) if cuts else 1.0
    values = jax.random.normal(stream_key, shape, jnp.float32) * scale * factor_of
    return jnp.minimum(jnp.maximum(values, -most), most).astype(dtype)


def setup_inputs(seed: int = 0) -> dict:
    key_list = jax.random.split(jax.random.key(seed), 5)
    return {
        "right_side": bell_draw(key_list[0], (NZ, NX, NY), 1.0, 8.0, ((1, 64), (2, 8)), jnp.float32),
        "capacity": jnp.clip(jnp.exp(math.log(2.0) - 2.9957323 * jax.random.uniform(key_list[1], (NZ, NX, NY), jnp.float32) ** level_of(key_list[1], (NZ, NX, NY), ((1, 64), (2, 8)), -0.2, 0.2)), 0.1, 2.0),
        "phase": plant(jax.random.randint(key_list[2], (NZ, NX, NY), 0, 3), jax.random.fold_in(key_list[2], 1), 0, 2).astype(jnp.int32),
        "mold_flags": plant((jax.random.randint(key_list[3], (NZ, NX, NY), 0, 4) < 1).astype(jnp.int32), jax.random.fold_in(key_list[3], 1), 0, 1),
    }


OMEGA = 0.8


def restrict(field):
    zc, xc, yc = field.shape
    return field.reshape(zc // 2, 2, xc // 2, 2, yc // 2, 2).mean(axis=(1, 3, 5))


def prolong(field):
    return jnp.repeat(jnp.repeat(jnp.repeat(field, 2, 0), 2, 1), 2, 2)


def operate(field, extra, scale):
    padded = jnp.pad(field, 1)
    beside = padded[2:, 1:-1, 1:-1] + padded[:-2, 1:-1, 1:-1]
    beside = beside + padded[1:-1, 2:, 1:-1] + padded[1:-1, :-2, 1:-1]
    beside = beside + padded[1:-1, 1:-1, 2:] + padded[1:-1, 1:-1, :-2]
    return scale * (6.0 * field - beside) + extra * field


def vcycle(level, source, diags):
    scale = 0.25 ** level
    inverse = OMEGA / (6.0 * scale + diags[level])
    correct = inverse * source
    if level == LEVELS - 1:
        for sweep in range(COARSE_SWEEPS - 1):
            correct = correct + inverse * (source - operate(correct, diags[level], scale))
        line_total = jnp.sum(source, axis=1, keepdims=True)
        line_weight = jnp.sum(diags[level], axis=1, keepdims=True)
        return correct + line_total / line_weight
    left = source - operate(correct, diags[level], scale)
    correct = correct + prolong(vcycle(level + 1, restrict(left), diags))
    return correct + inverse * (source - operate(correct, diags[level], scale))


def reference(right_side, capacity, phase, mold_flags):
    weight = jnp.where(phase == 1, jnp.float32(4.0), jnp.float32(1.0))
    base = 0.05 * capacity * weight + 0.5 * mold_flags.astype(jnp.float32)
    diags = [base]
    for level in range(1, LEVELS):
        diags.append(restrict(diags[-1]))
    adjoint_field = jnp.zeros_like(right_side)
    residual = right_side
    precond = vcycle(0, residual, diags)
    rho = jnp.sum(residual * precond)
    direction = precond
    for step in range(ITERS):
        image = operate(direction, base, 1.0)
        alpha = rho / jnp.sum(direction * image)
        adjoint_field = adjoint_field + alpha * direction
        residual = residual - alpha * image
        if step + 1 < ITERS:
            precond = vcycle(0, residual, diags)
            rho_next = jnp.sum(residual * precond)
            direction = precond + (rho_next / rho) * direction
            rho = rho_next
    return adjoint_field, residual
```

```python
import jax
import jax.numpy as jnp
from jax import lax
from jax.sharding import PartitionSpec as P

LEVELS = 4
COARSE_SWEEPS = 4
ITERS = 2


OMEGA = 0.8


def gathered(array, axis):
    peers = lax.axis_size(axis)
    slots = jnp.broadcast_to(array[None], (peers,) + array.shape)
    return lax.all_to_all(slots, axis, 0, 0)


def gather_rows(array):
    parts = gathered(array, "wide")
    peers, zc, xc, yc = parts.shape
    return jnp.transpose(parts, (1, 0, 2, 3)).reshape(zc, peers * xc, yc)


def with_halo(array, sides, width):
    for axis, dim in sides:
        peers, length = (lax.axis_size(axis), array.shape[dim])
        up = [(i, (i + 1) % peers) for i in range(peers - 1)]
        down = [(j, i) for i, j in up]
        last = lax.slice_in_dim(array, length - width, length, axis=dim)
        first = lax.slice_in_dim(array, 0, width, axis=dim)
        before = lax.ppermute(last, axis, up)
        after = lax.ppermute(first, axis, down)
        array = jnp.concatenate([before, array, after], axis=dim)
    return array


def restrict(field):
    zc, xc, yc = field.shape
    return field.reshape(zc // 2, 2, xc // 2, 2, yc // 2, 2).mean(axis=(1, 3, 5))


def prolong(field):
    return jnp.repeat(jnp.repeat(jnp.repeat(field, 2, 0), 2, 1), 2, 2)


def operate(field, extra, scale, spread):
    if spread:
        padded = with_halo(field, (("wide", 1), ("narrow", 2)), 1)
        padded = jnp.pad(padded, ((1, 1), (0, 0), (0, 0)))
    else:
        padded = with_halo(field, (("narrow", 2),), 1)
        padded = jnp.pad(padded, ((1, 1), (1, 1), (0, 0)))
    beside = padded[2:, 1:-1, 1:-1] + padded[:-2, 1:-1, 1:-1]
    beside = beside + padded[1:-1, 2:, 1:-1] + padded[1:-1, :-2, 1:-1]
    beside = beside + padded[1:-1, 1:-1, 2:] + padded[1:-1, 1:-1, :-2]
    return scale * (6.0 * field - beside) + extra * field


def vcycle(level, source, diags, collect):
    scale = 0.25**level
    spread = level < collect
    inverse = OMEGA / (6.0 * scale + diags[level])
    correct = inverse * source
    if level == LEVELS - 1:
        for sweep in range(COARSE_SWEEPS - 1):
            correct = correct + inverse * (source - operate(correct, diags[level], scale, spread))
        line_total = jnp.sum(source, axis=1, keepdims=True)
        line_weight = jnp.sum(diags[level], axis=1, keepdims=True)
        return correct + line_total / line_weight
    left = restrict(source - operate(correct, diags[level], scale, spread))
    if level + 1 == collect:
        width = left.shape[1]
        whole = gather_rows(left)
        coarse = vcycle(level + 1, whole, diags, collect)
        coarse = lax.dynamic_slice_in_dim(coarse, lax.axis_index("wide") * width, width, 1)
    else:
        coarse = vcycle(level + 1, left, diags, collect)
    correct = correct + prolong(coarse)
    return correct + inverse * (source - operate(correct, diags[level], scale, spread))


def inner_sum(first, second):
    part = jnp.sum(first * second).reshape(1)
    part = jnp.sum(gathered(part, "narrow"), axis=0)
    return jnp.sum(gathered(part, "wide"))


def on_device(right_side, capacity, phase, mold_flags):
    collect = 2
    weight = jnp.where(phase == 1, jnp.float32(4.0), jnp.float32(1.0))
    base = 0.05 * capacity * weight + 0.5 * mold_flags.astype(jnp.float32)
    diags = [base]
    for level in range(1, LEVELS):
        lower = restrict(diags[-1])
        if level == collect:
            lower = gather_rows(lower)
        diags.append(lower)
    adjoint_field = jnp.zeros_like(right_side)
    residual = right_side
    precond = vcycle(0, residual, diags, collect)
    rho = inner_sum(residual, precond)
    direction = precond
    for step in range(ITERS):
        image = operate(direction, base, 1.0, True)
        alpha = rho / inner_sum(direction, image)
        adjoint_field = adjoint_field + alpha * direction
        residual = residual - alpha * image
        if step + 1 < ITERS:
            precond = vcycle(0, residual, diags, collect)
            rho_next = inner_sum(residual, precond)
            direction = precond + rho_next / rho * direction
            rho = rho_next
    return (adjoint_field, residual)


def solution(mesh):
    in_specs = (
        P(None, "wide", "narrow"),
        P(None, "wide", "narrow"),
        P(None, "wide", "narrow"),
        P(None, "wide", "narrow"),
    )
    out_specs = (P(None, "wide", "narrow"), P(None, "wide", "narrow"))
    return jax.shard_map(
        on_device, mesh=mesh, in_specs=in_specs, out_specs=out_specs, check_vma=False
    )
```

```python
import functools

import jax
import jax.numpy as jnp
from jax import lax
from jax.experimental import pallas as pl
from jax.experimental.pallas import tpu as pltpu
from jax.sharding import PartitionSpec as P

OMEGA = 0.8
HALO = 5
OWN = 8
EXT = OWN + 2 * HALO
LANES = 256
F32 = jnp.float32


def iota(shape, dim):
    return lax.broadcasted_iota(jnp.int32, shape, dim)


def roll(value, shift, axis):
    return pltpu.roll(value, shift % value.shape[axis], axis)


def swap(value, width, axis):
    at = iota(value.shape, axis)
    lower = (at // width) % 2 == 0
    return jnp.where(lower, roll(value, -width, axis), roll(value, width, axis))


def along_y(value, width):
    axis = value.ndim - 1
    return roll(value, width, axis) + roll(value, -width, axis)


def apply_fine(even, odd, extra_even, extra_odd):
    e, o = even[1:-1], odd[1:-1]
    k = iota(e.shape, 1)
    by_e = o + jnp.where(k > 0, roll(o, 1, 1), 0.0) + even[2:] + even[:-2] + along_y(e, 1)
    by_o = e + jnp.where(k < 7, roll(e, -1, 1), 0.0) + odd[2:] + odd[:-2] + along_y(o, 1)
    return 6.0 * e - by_e + extra_even * e, 6.0 * o - by_o + extra_odd * o


def restrict_fine(even, odd):
    both = even + odd
    both = jnp.sum(both.reshape((both.shape[0] // 2, 2) + both.shape[1:]), axis=1)
    return 0.125 * (both + swap(both, 1, 2))


def double_rows(value):
    wide = jnp.broadcast_to(value[:, None], (value.shape[0], 2) + value.shape[1:])
    return wide.reshape((2 * value.shape[0],) + value.shape[1:])


def apply_one(value, extra):
    v = value[1:-1]
    k = iota(v.shape, 1)
    beside = jnp.where(k > 0, roll(v, 1, 1), 0.0) + jnp.where(k < 7, roll(v, -1, 1), 0.0)
    beside = beside + value[2:] + value[:-2] + along_y(v, 2)
    return 0.25 * (6.0 * v - beside) + extra * v


def pack_two(value, first_lane):
    pairs = jnp.sum(value.reshape((2, 2) + value.shape[1:]), axis=1)
    pairs = pairs + swap(pairs, 1, 1)
    rows = jnp.where(iota(pairs.shape[1:], 0) % 2 == 0, pairs[0], pairs[1])
    shape = (LANES, 128)
    matrix = jnp.where(iota(shape, 0) // 4 + first_lane == iota(shape, 1), 0.0625, 0.0)
    return jnp.dot(rows, matrix.astype(F32), precision=lax.Precision.HIGHEST)


def split_two(ref, wide):
    return [[ref[pl.ds(2 * z + x, wide, stride=8), :] for z in range(4)] for x in range(2)]


def add(terms):
    return functools.reduce(lambda a, b: a + b, terms)


def before(value):
    return jnp.where(iota(value.shape, 0) > 0, roll(value, 1, 0), 0.0)


def after(value):
    last = value.shape[0] - 1
    return jnp.where(iota(value.shape, 0) < last, roll(value, -1, 0), 0.0)


def each(function, *lists):
    return [[function(*(a[x][z] for a in lists)) for z in range(4)] for x in range(2)]


def apply_two(v, d):
    out = [[], []]
    for x in range(2):
        for z in range(4):
            terms = [along_y(v[x][z], 1), v[1 - x][z]]
            terms += [before(v[1][z])] if x == 0 else [after(v[0][z])]
            terms += [v[x][k] for k in (z - 1, z + 1) if 0 <= k < 4]
            out[x].append(0.0625 * (6.0 * v[x][z] - add(terms)) + d[x][z] * v[x][z])
    return out


def restrict_two(v):
    out = []
    for z in range(2):
        total = v[0][2 * z] + v[0][2 * z + 1] + v[1][2 * z] + v[1][2 * z + 1]
        out.append(0.125 * (total + swap(total, 1, 1)))
    return out


def apply_three(v, d):
    out = []
    for z in range(2):
        beside = before(v[z]) + after(v[z]) + v[1 - z] + along_y(v[z], 2)
        out.append(0.015625 * (6.0 * v[z] - beside) + d[z] * v[z])
    return out


def solve_coarse(r2, d2, mine, narrow):
    shape = r2[0][0].shape
    lane = iota(shape, 1) % 64
    column = 32 * mine + jnp.where(lane < 48, lane, lane - 64)
    inside = (column >= 0) & (column < 32 * narrow)
    i2 = each(lambda d: jnp.where(inside, OMEGA / (0.375 + d), 0.0), d2)
    c2 = each(lambda i, r: i * r, i2, r2)
    left = each(lambda r, a: r - a, r2, apply_two(c2, d2))
    r3, d3 = restrict_two(left), restrict_two(d2)
    i3 = [jnp.where(inside, OMEGA / (0.09375 + d), 0.0) for d in d3]
    e3 = [i * r for i, r in zip(i3, r3)]
    for _ in range(3):
        a3 = apply_three(e3, d3)
        e3 = [e + i * (r - a) for e, i, r, a in zip(e3, i3, r3, a3)]
    one = inside[:1]
    for z in range(2):
        weight = jnp.where(one, jnp.sum(d3[z], axis=0, keepdims=True), 1.0)
        line = jnp.where(one, jnp.sum(r3[z], axis=0, keepdims=True) / weight, 0.0)
        e3[z] = e3[z] + line
    e2 = [[c2[x][z] + e3[z // 2] for z in range(4)] for x in range(2)]
    return each(lambda e, i, r, a: e + i * (r - a), e2, i2, r2, apply_two(e2, d2))


def rise(e2, scratch, at, r1, d1, i1):
    wide = e2[0][0].shape[0]
    blank = jnp.zeros((8, 128), F32)
    for x in range(2):
        for z in range(4):
            scratch[2 * z + x, 0:8, :] = blank
            scratch[2 * z + x, 8 + wide : 16 + wide, :] = blank
            scratch[2 * z + x, 8 : 8 + wide, :] = e2[x][z]
    pair = iota((8, 128), 0) // 2
    rows = []
    for x, step in ((1, -1), (0, 0), (1, 0), (0, 1)):
        tile = blank
        for z in range(4):
            line = scratch[2 * z + x, pl.ds(at + (8 + step), 1), :]
            tile = jnp.where(pair == z, jnp.broadcast_to(line, (8, 128)), tile)
        rows.append(tile)
    shape = (128, LANES)
    matrix = jnp.where(iota(shape, 0) == iota(shape, 1) // 4, 1.0, 0.0).astype(F32)
    spread = jnp.dot(jnp.concatenate(rows, 0), matrix, precision=lax.Precision.HIGHEST)
    e1 = i1 * r1 + double_rows(spread.reshape(4, 8, LANES))
    return e1[1:-1] + i1[1:-1] * (r1[1:-1] - apply_one(e1, d1[1:-1]))


def finish(e1, source, extra, inverse):
    up = double_rows(e1)
    e = [inverse[p, 3:15] * source[p, 3:15] + up for p in range(2)]
    a = apply_fine(e[0], e[1], extra[0, 4:14], extra[1, 4:14])
    z = [e[p][1:-1] + inverse[p, 4:14] * (source[p, 4:14] - a[p]) for p in range(2)]
    q = apply_fine(z[0], z[1], extra[0, 5:13], extra[1, 5:13])
    return [v[1:-1] for v in z], q


def descend(source, extra, inverse):
    c = [i * s for i, s in zip(inverse, source)]
    a = apply_fine(c[0], c[1], extra[0][1:-1], extra[1][1:-1])
    left = [source[p][1:-1] - a[p] for p in range(2)]
    return restrict_fine(left[0], left[1])


def leave_one(r1, d1, i1):
    c1 = (i1 * r1)[1:7]
    return r1[2:6] - apply_one(c1, d1[2:6])


def total(a, b):
    return jnp.sum(jnp.sum(a[0] * b[0] + a[1] * b[1], axis=0), keepdims=True)


def place(values, shape, first):
    lane = iota(shape, len(shape) - 1)
    out = jnp.zeros(shape, F32)
    for i, v in enumerate(values):
        out = jnp.where(lane == first + i, v, out)
    return out


def prepare_kernel(right, capacity, phase, flags, own, low, high):
    half = iota((8, 128), 1) < 64
    for p in range(2):
        for x in range(OWN):
            rows = pl.ds(x + 8 * p, 8, stride=16)
            r = right[rows, :]
            weight = jnp.where(phase[rows, :] == 1, 4.0, 1.0)
            d = 0.05 * capacity[rows, :] * weight + 0.5 * flags[rows, :].astype(F32)
            first = jnp.where(half, r, roll(d, 64, 1))
            second = jnp.where(half, roll(r, 64, 1), d)
            for side, value in ((0, first), (1, second)):
                own[side, p, x] = value
                if x < HALO:
                    low[side, p, x] = value
                if x >= OWN - HALO:
                    high[side, p, x - (OWN - HALO)] = value


def down_kernel(wide, narrow, a, b, from_left, from_right, r0, d0, i0, r1, d1, i1, send):
    me_w, me_n = lax.axis_index("wide"), lax.axis_index("narrow")
    shape = (EXT, 8, 128)
    half = iota(shape, 2) < 64
    fine = (EXT, 8, LANES)
    lane, row = iota(fine, 2), iota(fine, 0)
    column = 128 * me_n + jnp.where(lane < 192, lane, lane - 256)
    line = 8 * me_w - HALO + row
    inside = (column >= 0) & (column < 128 * narrow) & (line >= 0) & (line < 8 * wide)
    source, extra, inverse = [], [], []
    for p in range(2):
        fa, fb, fl, fr = a[p], b[p], from_left[p], from_right[p]
        own_r = jnp.where(half, fa, roll(fb, 64, 2))
        own_d = jnp.where(half, roll(fa, 64, 2), fb)
        far_r = jnp.where(half, fr, roll(fl, 64, 2))
        far_d = jnp.where(half, roll(fr, 64, 2), fl)
        source.append(jnp.concatenate([own_r, far_r], axis=2))
        extra.append(jnp.concatenate([own_d, far_d], axis=2))
        inverse.append(jnp.where(inside, OMEGA / (6.0 + extra[p]), 0.0))
        r0[p] = source[p]
        d0[p] = extra[p]
        i0[p] = inverse[p]
    vr1 = descend(source, extra, inverse)
    vd1 = restrict_fine(extra[0][1:-1], extra[1][1:-1])
    line = 4 * me_w - 2 + iota(vd1.shape, 0)
    inside = (column[:8] >= 0) & (column[:8] < 128 * narrow) & (line >= 0) & (line < 4 * wide)
    vi1 = jnp.where(inside, OMEGA / (1.5 + vd1), 0.0)
    r1[...] = vr1
    d1[...] = vd1
    i1[...] = vi1
    send[...] = pack_two(leave_one(vr1, vd1, vi1), 0) + pack_two(vd1[2:6], 64)


def both_halves(tile):
    half = iota(tile.shape, 1) < 64
    other = roll(tile, 64, 1)
    return jnp.where(half, tile, other), jnp.where(half, other, tile)


def up_kernel(wide, narrow, got, r0, d0, i0, r1, d1, i1, z, q, low, high, sums, scratch):
    me_w, me_n = lax.axis_index("wide"), lax.axis_index("narrow")
    tiles = split_two(got, wide)
    r2 = each(lambda t: both_halves(t)[0], tiles)
    d2 = each(lambda t: both_halves(t)[1], tiles)
    e2 = solve_coarse(r2, d2, me_n, narrow)
    e1 = rise(e2, scratch, me_w, r1[...], d1[...], i1[...])
    vz, vq = finish(e1, r0, d0, i0)
    for p in range(2):
        z[p] = vz[p][:, :, :128]
        q[p] = vq[p]
        low[p] = vq[p][:HALO]
        high[p] = vq[p][OWN - HALO :]
    mine = [v[:, :, :128] for v in vz]
    image = [v[:, :, :128] for v in vq]
    residual = [r0[p, HALO : HALO + OWN, :, :128] for p in range(2)]
    sums[...] = place([total(residual, mine), total(mine, image)], (8, 128), 64)


def down_again_kernel(q, low, high, d0, i0, d1, i1, sums, source, r1, send):
    full, extra, inverse = [], [], []
    for p in range(2):
        full.append(jnp.concatenate([low[p], q[p], high[p]], axis=0))
        extra.append(d0[p])
        inverse.append(i0[p])
        source[p] = full[p]
    vr1 = descend(full, extra, inverse)
    r1[...] = vr1
    send[...] = pack_two(leave_one(vr1, d1[...], i1[...]), 0) + sums[...]


def window_kernel(narrow, got, send):
    me = lax.axis_index("narrow")
    lane = iota((8, 128), 1)
    right = got[jnp.minimum(me + 1, narrow - 1)]
    left = got[jnp.maximum(me - 1, 0)]
    tile = jnp.where(lane < 32, got[me], jnp.where(lane < 48, roll(right, 32, 1), roll(left, 32, 1)))
    scalars = jnp.sum(got[...], axis=0)
    send[...] = jnp.where(lane < 64, tile, scalars)


def up_again_kernel(wide, narrow, got, first, source, r0, d0, i0, r1, d1, i1, z0, z1, image1, res1, sums, known, scratch):
    me_w, me_n = lax.axis_index("wide"), lax.axis_index("narrow")
    r2 = each(lambda t: both_halves(t)[0], split_two(got, wide))
    d2 = each(lambda t: both_halves(t)[1], split_two(first, wide))
    e2 = solve_coarse(r2, d2, me_n, narrow)
    e1 = rise(e2, scratch, me_w, r1[...], d1[...], i1[...])
    vw, vy = finish(e1, source, d0, i0)
    scalars = jnp.sum(got[pl.ds(0, wide, stride=8), :], axis=0, keepdims=True)
    lane = iota((1, 128), 1)
    rho = jnp.sum(jnp.where(lane == 64, scalars, 0.0), keepdims=True)
    curve = jnp.sum(jnp.where(lane == 65, scalars, 0.0), keepdims=True)
    alpha = (rho / curve).reshape(1, 1, 1)
    own = slice(HALO, HALO + OWN)
    vz0 = [z0[p] for p in range(2)]
    vq0 = [source[p, own, :, :128] for p in range(2)]
    vz1 = [vz0[p] - alpha * vw[p][:, :, :128] for p in range(2)]
    vi1 = [vq0[p] - alpha * vy[p][:, :, :128] for p in range(2)]
    vr1 = [r0[p, own, :, :128] - alpha * vq0[p] for p in range(2)]
    for p in range(2):
        z1[p] = vz1[p]
        image1[p] = vi1[p]
        res1[p] = vr1[p]
    cross = total(vz1, vq0) + total(vz0, vi1)
    sums[...] = place([total(vr1, vz1), total(vz1, vi1), cross], (1, 128), 0)
    known[...] = place([rho, curve], (1, 128), 0)


def last_kernel(got, known, z0, source, z1, image1, res1, field, residual):
    scalars = jnp.sum(got[...], axis=0, keepdims=True)
    lane = iota((1, 128), 1)

    def pick(vector, at):
        return jnp.sum(jnp.where(lane == at, vector, 0.0), keepdims=True)

    rho, curve = pick(known[...], 0), pick(known[...], 1)
    rho_next, square, cross = (pick(scalars, i) for i in range(3))
    alpha = rho / curve
    beta = rho_next / rho
    alpha_next = rho_next / (square + beta * cross + beta * beta * curve)
    for p in range(2):
        for x in range(OWN):
            rows = pl.ds(x + 8 * p, 8, stride=16)
            z, q = z0[p, x], source[p, HALO + x, :, :128]
            field[rows, :] = alpha * z + alpha_next * (z1[p, x] + beta * z)
            residual[rows, :] = res1[p, x] - alpha_next * (image1[p, x] + beta * q)


def call(kernel, outs, *args, scratch=()):
    return pl.pallas_call(
        kernel,
        out_shape=tuple(jax.ShapeDtypeStruct(s, F32) for s in outs),
        in_specs=[pl.BlockSpec(memory_space=pltpu.VMEM)] * len(args),
        out_specs=tuple(pl.BlockSpec(memory_space=pltpu.VMEM) for _ in outs),
        scratch_shapes=scratch,
        compiler_params=pltpu.CompilerParams(vmem_limit_bytes=40 * 1024 * 1024),
    )(*args)


def gathered(array, axis):
    peers = lax.axis_size(axis)
    slots = jnp.broadcast_to(array[None], (peers,) + array.shape)
    return lax.all_to_all(slots, axis, 0, 0)


def to_next(array, axis):
    n = lax.axis_size(axis)
    return lax.ppermute(array, axis, [(i, i + 1) for i in range(n - 1)])


def to_previous(array, axis):
    n = lax.axis_size(axis)
    return lax.ppermute(array, axis, [(i + 1, i) for i in range(n - 1)])


def on_device(right_side, capacity, phase, mold_flags):
    wide, narrow = lax.axis_size("wide"), lax.axis_size("narrow")
    flat = [v.reshape(128, 128) for v in (right_side, capacity, phase, mold_flags)]
    edge = (2, 2, HALO, 8, 128)
    own, low, high = call(prepare_kernel, [(2, 2, OWN, 8, 128), edge, edge], *flat)
    below, above = to_next(high, "wide"), to_previous(low, "wide")
    a = jnp.concatenate([below[0], own[0], above[0]], axis=1)
    b = jnp.concatenate([below[1], own[1], above[1]], axis=1)
    from_left, from_right = to_next(b, "narrow"), to_previous(a, "narrow")
    fine, coarse = (2, EXT, 8, LANES), (8, 8, LANES)
    r0, d0, i0, r1, d1, i1, send = call(
        functools.partial(down_kernel, wide, narrow),
        [fine, fine, fine, coarse, coarse, coarse, (8, 128)],
        a, b, from_left, from_right,
    )
    first = gathered(send, "wide").reshape(8 * wide, 128)
    block = (2, OWN, 8, 128)
    band = (2, HALO, 8, LANES)
    scratch = [pltpu.VMEM((8, wide + 16, 128), F32)]
    z0, q0, low, high, sums = call(
        functools.partial(up_kernel, wide, narrow),
        [block, (2, OWN, 8, LANES), band, band, (8, 128)],
        first, r0, d0, i0, r1, d1, i1,
        scratch=scratch,
    )
    below, above = to_next(high, "wide"), to_previous(low, "wide")
    source, r1, send = call(
        down_again_kernel, [fine, coarse, (8, 128)], q0, below, above, d0, i0, d1, i1, sums
    )
    (send,) = call(functools.partial(window_kernel, narrow), [(8, 128)], gathered(send, "narrow"))
    second = gathered(send, "wide").reshape(8 * wide, 128)
    z1, image1, res1, sums, known = call(
        functools.partial(up_again_kernel, wide, narrow),
        [block, block, block, (1, 128), (1, 128)],
        second, first, source, r0, d0, i0, r1, d1, i1, z0,
        scratch=scratch,
    )
    sums = jnp.sum(gathered(sums, "narrow"), axis=0)
    third = gathered(sums, "wide").reshape(wide, 128)
    field, residual = call(
        last_kernel, [(128, 128), (128, 128)], third, known, z0, source, z1, image1, res1
    )
    return field.reshape(right_side.shape), residual.reshape(right_side.shape)


def solution(mesh):
    spec = P(None, "wide", "narrow")
    return jax.shard_map(
        on_device, mesh=mesh, in_specs=(spec,) * 4, out_specs=(spec, spec), check_vma=False
    )
```

```python
import functools

import jax
import jax.numpy as jnp
from jax import lax
from jax.experimental import pallas as pl
from jax.experimental.pallas import tpu as pltpu
from jax.sharding import PartitionSpec as P

OMEGA = 0.8
HALO = 5
OWN = 8
EXT = OWN + 2 * HALO
LANES = 256
F32 = jnp.float32
DEEP = 16
SUMS = 44


def iota(shape, dim):
    return lax.broadcasted_iota(jnp.int32, shape, dim)


def roll(value, shift, axis):
    return pltpu.roll(value, shift % value.shape[axis], axis)


def swap(value, width, axis):
    at = iota(value.shape, axis)
    lower = (at // width) % 2 == 0
    return jnp.where(lower, roll(value, -width, axis), roll(value, width, axis))


def along_y(value, width):
    axis = value.ndim - 1
    return roll(value, width, axis) + roll(value, -width, axis)


def apply_fine(even, odd, extra_even, extra_odd):
    e, o = even[1:-1], odd[1:-1]
    k = iota(e.shape, 1)
    by_e = o + jnp.where(k > 0, roll(o, 1, 1), 0.0) + even[2:] + even[:-2] + along_y(e, 1)
    by_o = e + jnp.where(k < 7, roll(e, -1, 1), 0.0) + odd[2:] + odd[:-2] + along_y(o, 1)
    return 6.0 * e - by_e + extra_even * e, 6.0 * o - by_o + extra_odd * o


def restrict_fine(even, odd):
    both = even + odd
    both = jnp.sum(both.reshape((both.shape[0] // 2, 2) + both.shape[1:]), axis=1)
    return 0.125 * (both + swap(both, 1, 2))


def double_rows(value):
    wide = jnp.broadcast_to(value[:, None], (value.shape[0], 2) + value.shape[1:])
    return wide.reshape((2 * value.shape[0],) + value.shape[1:])


def apply_one(value, extra):
    v = value[1:-1]
    k = iota(v.shape, 1)
    beside = jnp.where(k > 0, roll(v, 1, 1), 0.0) + jnp.where(k < 7, roll(v, -1, 1), 0.0)
    beside = beside + value[2:] + value[:-2] + along_y(v, 2)
    return 0.25 * (6.0 * v - beside) + extra * v


def pack_two(value, first_lane):
    pairs = jnp.sum(value.reshape((2, 2) + value.shape[1:]), axis=1)
    pairs = pairs + swap(pairs, 1, 1)
    rows = jnp.where(iota(pairs.shape[1:], 0) % 2 == 0, pairs[0], pairs[1])
    shape = (LANES, 128)
    matrix = jnp.where(iota(shape, 0) // 4 + first_lane == iota(shape, 1), 0.0625, 0.0)
    return jnp.dot(rows, matrix.astype(F32), precision=lax.Precision.HIGHEST)


def pack_rows(value, scratch):
    pairs = jnp.sum(value.reshape((2, 2) + value.shape[1:]), axis=1)
    pairs = pairs + swap(pairs, 1, 1)
    shape = (LANES, 128)
    out = jnp.zeros((8, 128), F32)
    for x in range(2):
        matrix = jnp.where(iota(shape, 0) // 4 + 64 * x == iota(shape, 1), 0.0625, 0.0)
        out = out + jnp.dot(pairs[x], matrix.astype(F32), precision=lax.Precision.HIGHEST)
    scratch[...] = out
    return scratch[pl.ds(0, 4, stride=2), :]


def split_two(ref, wide):
    return [[ref[pl.ds(2 * z + x, wide, stride=8), :] for z in range(4)] for x in range(2)]


def add(terms):
    return functools.reduce(lambda a, b: a + b, terms)


def before(value):
    return jnp.where(iota(value.shape, 0) > 0, roll(value, 1, 0), 0.0)


def after(value):
    last = value.shape[0] - 1
    return jnp.where(iota(value.shape, 0) < last, roll(value, -1, 0), 0.0)


def each(function, *lists):
    return [[function(*(a[x][z] for a in lists)) for z in range(4)] for x in range(2)]


def apply_two(v, d):
    out = [[], []]
    for x in range(2):
        for z in range(4):
            terms = [along_y(v[x][z], 1), v[1 - x][z]]
            terms += [before(v[1][z])] if x == 0 else [after(v[0][z])]
            terms += [v[x][k] for k in (z - 1, z + 1) if 0 <= k < 4]
            out[x].append(0.0625 * (6.0 * v[x][z] - add(terms)) + d[x][z] * v[x][z])
    return out


def restrict_two(v):
    out = []
    for z in range(2):
        total = v[0][2 * z] + v[0][2 * z + 1] + v[1][2 * z] + v[1][2 * z + 1]
        out.append(0.125 * (total + swap(total, 1, 1)))
    return out


def apply_three(v, d):
    out = []
    for z in range(2):
        beside = before(v[z]) + after(v[z]) + v[1 - z] + along_y(v[z], 2)
        out.append(0.015625 * (6.0 * v[z] - beside) + d[z] * v[z])
    return out


def solve_coarse(r2, d2, mine, narrow):
    shape = r2[0][0].shape
    lane = iota(shape, 1) % 64
    column = 32 * mine + jnp.where(lane < 48, lane, lane - 64)
    inside = (column >= 0) & (column < 32 * narrow)
    i2 = each(lambda d: jnp.where(inside, OMEGA / (0.375 + d), 0.0), d2)
    c2 = each(lambda i, r: i * r, i2, r2)
    left = each(lambda r, a: r - a, r2, apply_two(c2, d2))
    r3, d3 = restrict_two(left), restrict_two(d2)
    i3 = [jnp.where(inside, OMEGA / (0.09375 + d), 0.0) for d in d3]
    e3 = [i * r for i, r in zip(i3, r3)]
    for _ in range(3):
        a3 = apply_three(e3, d3)
        e3 = [e + i * (r - a) for e, i, r, a in zip(e3, i3, r3, a3)]
    one = inside[:1]
    for z in range(2):
        weight = jnp.where(one, jnp.sum(d3[z], axis=0, keepdims=True), 1.0)
        line = jnp.where(one, jnp.sum(r3[z], axis=0, keepdims=True) / weight, 0.0)
        e3[z] = e3[z] + line
    e2 = [[c2[x][z] + e3[z // 2] for z in range(4)] for x in range(2)]
    return each(lambda e, i, r, a: e + i * (r - a), e2, i2, r2, apply_two(e2, d2))


def rise(e2, scratch, at, r1, d1, i1):
    wide = e2[0][0].shape[0]
    blank = jnp.zeros((8, 128), F32)
    for x in range(2):
        for z in range(4):
            scratch[2 * z + x, 0:8, :] = blank
            scratch[2 * z + x, 8 + wide : 16 + wide, :] = blank
            scratch[2 * z + x, 8 : 8 + wide, :] = e2[x][z]
    pair = iota((8, 128), 0) // 2
    rows = []
    for x, step in ((1, -1), (0, 0), (1, 0), (0, 1)):
        tile = blank
        for z in range(4):
            line = scratch[2 * z + x, pl.ds(at + (8 + step), 1), :]
            tile = jnp.where(pair == z, jnp.broadcast_to(line, (8, 128)), tile)
        rows.append(tile)
    shape = (128, LANES)
    matrix = jnp.where(iota(shape, 0) == iota(shape, 1) // 4, 1.0, 0.0).astype(F32)
    spread = jnp.dot(jnp.concatenate(rows, 0), matrix, precision=lax.Precision.HIGHEST)
    e1 = i1 * r1 + double_rows(spread.reshape(4, 8, LANES))
    return e1[1:-1] + i1[1:-1] * (r1[1:-1] - apply_one(e1, d1[1:-1]))


def finish(e1, source, extra, inverse):
    up = double_rows(e1)
    e = [inverse[p, 3:15] * source[p, 3:15] + up for p in range(2)]
    a = apply_fine(e[0], e[1], extra[0, 4:14], extra[1, 4:14])
    z = [e[p][1:-1] + inverse[p, 4:14] * (source[p, 4:14] - a[p]) for p in range(2)]
    q = apply_fine(z[0], z[1], extra[0, 5:13], extra[1, 5:13])
    return [v[1:-1] for v in z], q


def descend(source, extra, inverse):
    c = [i * s for i, s in zip(inverse, source)]
    a = apply_fine(c[0], c[1], extra[0][1:-1], extra[1][1:-1])
    left = [source[p][1:-1] - a[p] for p in range(2)]
    return restrict_fine(left[0], left[1])


def leave_one(r1, d1, i1):
    c1 = (i1 * r1)[1:7]
    return r1[2:6] - apply_one(c1, d1[2:6])


def total(a, b):
    return jnp.sum(jnp.sum(a[0] * b[0] + a[1] * b[1], axis=0), keepdims=True)


def place(values, shape, first):
    lane = iota(shape, len(shape) - 1)
    out = jnp.zeros(shape, F32)
    for i, v in enumerate(values):
        out = jnp.where(lane == first + i, v, out)
    return out


def prepare_kernel(right_in, capacity_in, phase_in, flags_in, own, low, high, right, capacity, phase, flags, done):
    pairs = ((right_in, right), (capacity_in, capacity), (phase_in, phase), (flags_in, flags))
    copies = [pltpu.make_async_copy(a, b, done.at[i]) for i, (a, b) in enumerate(pairs)]
    for copy in copies:
        copy.start()
    for copy in copies:
        copy.wait()
    half = iota((8, 128), 1) < 64
    for p in range(2):
        for x in range(OWN):
            rows = pl.ds(x + 8 * p, 8, stride=16)
            r = right[rows, :]
            weight = jnp.where(phase[rows, :] == 1, 4.0, 1.0)
            d = 0.05 * capacity[rows, :] * weight + 0.5 * flags[rows, :].astype(F32)
            first = jnp.where(half, r, roll(d, 64, 1))
            second = jnp.where(half, roll(r, 64, 1), d)
            for side, value in ((0, first), (1, second)):
                own[side, p, x] = value
                if x < HALO:
                    low[side, p, x] = value
                if x >= OWN - HALO:
                    high[side, p, x - (OWN - HALO)] = value


def down_kernel(wide, narrow, a, b, from_left, from_right, r0, d0, i0, r1, d1, i1, send):
    me_w, me_n = lax.axis_index("wide"), lax.axis_index("narrow")
    shape = (EXT, 8, 128)
    half = iota(shape, 2) < 64
    fine = (EXT, 8, LANES)
    lane, row = iota(fine, 2), iota(fine, 0)
    column = 128 * me_n + jnp.where(lane < 192, lane, lane - 256)
    line = 8 * me_w - HALO + row
    inside = (column >= 0) & (column < 128 * narrow) & (line >= 0) & (line < 8 * wide)
    source, extra, inverse = [], [], []
    for p in range(2):
        fa, fb, fl, fr = a[p], b[p], from_left[p], from_right[p]
        own_r = jnp.where(half, fa, roll(fb, 64, 2))
        own_d = jnp.where(half, roll(fa, 64, 2), fb)
        far_r = jnp.where(half, fr, roll(fl, 64, 2))
        far_d = jnp.where(half, roll(fr, 64, 2), fl)
        source.append(jnp.concatenate([own_r, far_r], axis=2))
        extra.append(jnp.concatenate([own_d, far_d], axis=2))
        inverse.append(jnp.where(inside, OMEGA / (6.0 + extra[p]), 0.0))
        r0[p] = source[p]
        d0[p] = extra[p]
        i0[p] = inverse[p]
    vr1 = descend(source, extra, inverse)
    vd1 = restrict_fine(extra[0][1:-1], extra[1][1:-1])
    line = 4 * me_w - 2 + iota(vd1.shape, 0)
    inside = (column[:8] >= 0) & (column[:8] < 128 * narrow) & (line >= 0) & (line < 4 * wide)
    vi1 = jnp.where(inside, OMEGA / (1.5 + vd1), 0.0)
    r1[...] = vr1
    d1[...] = vd1
    i1[...] = vi1
    send[...] = pack_two(leave_one(vr1, vd1, vi1), 0) + pack_two(vd1[2:6], 64)


def both_halves(tile):
    half = iota(tile.shape, 1) < 64
    other = roll(tile, 64, 1)
    return jnp.where(half, tile, other), jnp.where(half, other, tile)


def up_kernel(wide, narrow, got, r0, d0, i0, r1, d1, i1, z, q, low, high, sums, scratch):
    me_w, me_n = lax.axis_index("wide"), lax.axis_index("narrow")
    tiles = split_two(got, wide)
    r2 = each(lambda t: both_halves(t)[0], tiles)
    d2 = each(lambda t: both_halves(t)[1], tiles)
    e2 = solve_coarse(r2, d2, me_n, narrow)
    e1 = rise(e2, scratch, me_w, r1[...], d1[...], i1[...])
    vz, vq = finish(e1, r0, d0, i0)
    for p in range(2):
        z[p] = vz[p][:, :, :128]
        q[p] = vq[p]
        low[p] = vq[p][:HALO]
        high[p] = vq[p][OWN - HALO :]
    mine = [v[:, :, :128] for v in vz]
    image = [v[:, :, :128] for v in vq]
    residual = [r0[p, HALO : HALO + OWN, :, :128] for p in range(2)]
    sums[...] = place([total(residual, mine), total(mine, image)], (8, 128), SUMS)


def down_again_kernel(q, low, high, d0, i0, d1, i1, sums, source, r1, send, scratch):
    full, extra, inverse = [], [], []
    for p in range(2):
        full.append(jnp.concatenate([low[p], q[p], high[p]], axis=0))
        extra.append(d0[p])
        inverse.append(i0[p])
        source[p] = full[p]
    vr1 = descend(full, extra, inverse)
    r1[...] = vr1
    rows = pack_rows(leave_one(vr1, d1[...], i1[...]), scratch)
    lane = iota(rows.shape, 1)
    send[...] = jnp.where((lane == SUMS) | (lane == SUMS + 1), sums[0:4, :], rows)


def window_kernel(narrow, got, send, own, right, left):
    me = lax.axis_index("narrow")
    for y in range(got.shape[0] // narrow):
        rows = slice(4 * y, 4 * y + 4)
        own[rows, :] = got[y * narrow + me]
        right[rows, :] = got[y * narrow + jnp.minimum(me + 1, narrow - 1)]
        left[rows, :] = got[y * narrow + jnp.maximum(me - 1, 0)]
    lane = iota(own.shape, 1)
    cell = lane % 64
    halo = jnp.where(cell < 48, roll(right[...], 32, 1), roll(left[...], 32, 1))
    tile = jnp.where(cell < 32, own[...], halo)
    scalars = jnp.sum(jnp.sum(got[...], axis=0), axis=0, keepdims=True) * 0.25
    send[...] = jnp.where((lane == SUMS) | (lane == SUMS + 1), scalars, tile)


def split_deep(ref, wide):
    sides = [[], []]
    across = wide // DEEP
    for z in range(4):
        rows = [ref[pl.ds(4 * y + z, DEEP, stride=4 * across), :] for y in range(across)]
        for side, value in zip(sides, both_halves(jnp.concatenate(rows, 0))):
            side.append(value)
    return sides


def up_again_kernel(wide, narrow, got, first, source, r0, d0, i0, r1, d1, i1, z0, z1, image1, res1, sums, known, scratch):
    me_w, me_n = lax.axis_index("wide"), lax.axis_index("narrow")
    r2 = split_deep(got, wide)
    d2 = each(lambda t: both_halves(t)[1], split_two(first, wide))
    e2 = solve_coarse(r2, d2, me_n, narrow)
    e1 = rise(e2, scratch, me_w, r1[...], d1[...], i1[...])
    vw, vy = finish(e1, source, d0, i0)
    stride = 4 * (wide // DEEP)
    scalars = jnp.sum(got[pl.ds(0, DEEP, stride=stride), :], axis=0, keepdims=True)
    lane = iota((1, 128), 1)
    rho = jnp.sum(jnp.where(lane == SUMS, scalars, 0.0), keepdims=True)
    curve = jnp.sum(jnp.where(lane == SUMS + 1, scalars, 0.0), keepdims=True)
    alpha = (rho / curve).reshape(1, 1, 1)
    own = slice(HALO, HALO + OWN)
    vz0 = [z0[p] for p in range(2)]
    vq0 = [source[p, own, :, :128] for p in range(2)]
    vz1 = [vz0[p] - alpha * vw[p][:, :, :128] for p in range(2)]
    vi1 = [vq0[p] - alpha * vy[p][:, :, :128] for p in range(2)]
    vr1 = [r0[p, own, :, :128] - alpha * vq0[p] for p in range(2)]
    for p in range(2):
        z1[p] = vz1[p]
        image1[p] = vi1[p]
        res1[p] = vr1[p]
    cross = total(vz1, vq0) + total(vz0, vi1)
    sums[...] = place([total(vr1, vz1), total(vz1, vi1), cross], (1, 128), 0)
    known[...] = place([rho, curve], (1, 128), 0)


def last_kernel(got, known, z0, source, z1, image1, res1, field, residual):
    scalars = jnp.sum(got[...], axis=0, keepdims=True)
    lane = iota((1, 128), 1)

    def pick(vector, at):
        return jnp.sum(jnp.where(lane == at, vector, 0.0), keepdims=True)

    rho, curve = pick(known[...], 0), pick(known[...], 1)
    rho_next, square, cross = (pick(scalars, i) for i in range(3))
    alpha = rho / curve
    beta = rho_next / rho
    alpha_next = rho_next / (square + beta * cross + beta * beta * curve)
    for p in range(2):
        for x in range(OWN):
            rows = pl.ds(x + 8 * p, 8, stride=16)
            z, q = z0[p, x], source[p, HALO + x, :, :128]
            field[rows, :] = alpha * z + alpha_next * (z1[p, x] + beta * z)
            residual[rows, :] = res1[p, x] - alpha_next * (image1[p, x] + beta * q)


def call(kernel, outs, *args, scratch=(), space=pltpu.VMEM):
    return pl.pallas_call(
        kernel,
        out_shape=tuple(jax.ShapeDtypeStruct(s, F32) for s in outs),
        in_specs=[pl.BlockSpec(memory_space=space)] * len(args),
        out_specs=tuple(pl.BlockSpec(memory_space=pltpu.VMEM) for _ in outs),
        scratch_shapes=scratch,
        compiler_params=pltpu.CompilerParams(vmem_limit_bytes=40 * 1024 * 1024),
    )(*args)


def gathered(array, axis, groups=None):
    peers = lax.axis_size(axis) if groups is None else len(groups[0])
    slots = jnp.broadcast_to(array[None], (peers,) + array.shape)
    return lax.all_to_all(slots, axis, 0, 0, axis_index_groups=groups)


def to_next(array, axis):
    n = lax.axis_size(axis)
    return lax.ppermute(array, axis, [(i, i + 1) for i in range(n - 1)])


def to_previous(array, axis):
    n = lax.axis_size(axis)
    return lax.ppermute(array, axis, [(i + 1, i) for i in range(n - 1)])


def on_device(right_side, capacity, phase, mold_flags):
    wide, narrow = lax.axis_size("wide"), lax.axis_size("narrow")
    flat = [v.reshape(128, 128) for v in (right_side, capacity, phase, mold_flags)]
    edge = (2, 2, HALO, 8, 128)
    staged = [pltpu.VMEM((128, 128), v.dtype) for v in flat]
    own, low, high = call(
        prepare_kernel,
        [(2, 2, OWN, 8, 128), edge, edge],
        *flat,
        scratch=staged + [pltpu.SemaphoreType.DMA((4,))],
        space=pl.ANY,
    )
    below, above = to_next(high, "wide"), to_previous(low, "wide")
    a = jnp.concatenate([below[0], own[0], above[0]], axis=1)
    b = jnp.concatenate([below[1], own[1], above[1]], axis=1)
    from_left, from_right = to_next(b, "narrow"), to_previous(a, "narrow")
    fine, coarse = (2, EXT, 8, LANES), (8, 8, LANES)
    r0, d0, i0, r1, d1, i1, send = call(
        functools.partial(down_kernel, wide, narrow),
        [fine, fine, fine, coarse, coarse, coarse, (8, 128)],
        a, b, from_left, from_right,
    )
    first = gathered(send, "wide").reshape(8 * wide, 128)
    block = (2, OWN, 8, 128)
    band = (2, HALO, 8, LANES)
    scratch = [pltpu.VMEM((8, wide + 16, 128), F32)]
    z0, q0, low, high, sums = call(
        functools.partial(up_kernel, wide, narrow),
        [block, (2, OWN, 8, LANES), band, band, (8, 128)],
        first, r0, d0, i0, r1, d1, i1,
        scratch=scratch,
    )
    below, above = to_next(high, "wide"), to_previous(low, "wide")
    source, r1, send = call(
        down_again_kernel,
        [fine, coarse, (4, 128)],
        q0, below, above, d0, i0, d1, i1, sums,
        scratch=[pltpu.VMEM((8, 128), F32)],
    )
    across = wide // DEEP
    near = [
        [(DEEP * y + z) * narrow + n for y in range(across) for n in range(narrow)]
        for z in range(DEEP)
    ]
    far = [[DEEP * y + z for z in range(DEEP)] for y in range(across)]
    rows = (4 * across, 128)
    (send,) = call(
        functools.partial(window_kernel, narrow),
        [rows],
        gathered(send, ("wide", "narrow"), near),
        scratch=[pltpu.VMEM(rows, F32)] * 3,
    )
    second = gathered(send, "wide", far).reshape(DEEP * 4 * across, 128)
    z1, image1, res1, sums, known = call(
        functools.partial(up_again_kernel, wide, narrow),
        [block, block, block, (1, 128), (1, 128)],
        second, first, source, r0, d0, i0, r1, d1, i1, z0,
        scratch=scratch,
    )
    sums = jnp.sum(gathered(sums, "narrow"), axis=0)
    third = gathered(sums, "wide").reshape(wide, 128)
    field, residual = call(
        last_kernel, [(128, 128), (128, 128)], third, known, z0, source, z1, image1, res1
    )
    return field.reshape(right_side.shape), residual.reshape(right_side.shape)


def solution(mesh):
    spec = P(None, "wide", "narrow")
    return jax.shard_map(
        on_device, mesh=mesh, in_specs=(spec,) * 4, out_specs=(spec, spec), check_vma=False
    )
```

```python
import functools

import jax
import jax.numpy as jnp
from jax import lax
from jax.experimental import pallas as pl
from jax.experimental.pallas import tpu as pltpu
from jax.sharding import PartitionSpec as P

OMEGA = 0.8
HALO = 5
OWN = 8
EXT = OWN + 2 * HALO
LANES = 256
F32 = jnp.float32
DEEP = 16
SUMS = 44


def iota(shape, dim):
    return lax.broadcasted_iota(jnp.int32, shape, dim)


def roll(value, shift, axis):
    return pltpu.roll(value, shift % value.shape[axis], axis)


def swap(value, width, axis):
    at = iota(value.shape, axis)
    lower = (at // width) % 2 == 0
    return jnp.where(lower, roll(value, -width, axis), roll(value, width, axis))


def along_y(value, width):
    axis = value.ndim - 1
    return roll(value, width, axis) + roll(value, -width, axis)


def apply_fine(even, odd, extra_even, extra_odd):
    e, o = even[1:-1], odd[1:-1]
    k = iota(e.shape, 1)
    by_e = o + jnp.where(k > 0, roll(o, 1, 1), 0.0) + even[2:] + even[:-2] + along_y(e, 1)
    by_o = e + jnp.where(k < 7, roll(e, -1, 1), 0.0) + odd[2:] + odd[:-2] + along_y(o, 1)
    return 6.0 * e - by_e + extra_even * e, 6.0 * o - by_o + extra_odd * o


def restrict_fine(even, odd):
    both = even + odd
    both = jnp.sum(both.reshape((both.shape[0] // 2, 2) + both.shape[1:]), axis=1)
    return 0.125 * (both + swap(both, 1, 2))


def double_rows(value):
    wide = jnp.broadcast_to(value[:, None], (value.shape[0], 2) + value.shape[1:])
    return wide.reshape((2 * value.shape[0],) + value.shape[1:])


def apply_one(value, extra):
    v = value[1:-1]
    k = iota(v.shape, 1)
    beside = jnp.where(k > 0, roll(v, 1, 1), 0.0) + jnp.where(k < 7, roll(v, -1, 1), 0.0)
    beside = beside + value[2:] + value[:-2] + along_y(v, 2)
    return 0.25 * (6.0 * v - beside) + extra * v


def pack_two(value, first_lane):
    pairs = jnp.sum(value.reshape((2, 2) + value.shape[1:]), axis=1)
    pairs = pairs + swap(pairs, 1, 1)
    rows = jnp.where(iota(pairs.shape[1:], 0) % 2 == 0, pairs[0], pairs[1])
    shape = (LANES, 128)
    matrix = jnp.where(iota(shape, 0) // 4 + first_lane == iota(shape, 1), 0.0625, 0.0)
    return jnp.dot(rows, matrix.astype(F32), precision=lax.Precision.HIGHEST)


def pack_rows(value, scratch):
    pairs = jnp.sum(value.reshape((2, 2) + value.shape[1:]), axis=1)
    pairs = pairs + swap(pairs, 1, 1)
    shape = (LANES, 128)
    out = jnp.zeros((8, 128), F32)
    for x in range(2):
        matrix = jnp.where(iota(shape, 0) // 4 + 64 * x == iota(shape, 1), 0.0625, 0.0)
        out = out + jnp.dot(pairs[x], matrix.astype(F32), precision=lax.Precision.HIGHEST)
    scratch[...] = out
    return scratch[pl.ds(0, 4, stride=2), :]


def split_two(ref, wide):
    return [[ref[pl.ds(2 * z + x, wide, stride=8), :] for z in range(4)] for x in range(2)]


def add(terms):
    return functools.reduce(lambda a, b: a + b, terms)


def before(value):
    return jnp.where(iota(value.shape, 0) > 0, roll(value, 1, 0), 0.0)


def after(value):
    last = value.shape[0] - 1
    return jnp.where(iota(value.shape, 0) < last, roll(value, -1, 0), 0.0)


def each(function, *lists):
    return [[function(*(a[x][z] for a in lists)) for z in range(4)] for x in range(2)]


def apply_two(v, d):
    out = [[], []]
    for x in range(2):
        for z in range(4):
            terms = [along_y(v[x][z], 1), v[1 - x][z]]
            terms += [before(v[1][z])] if x == 0 else [after(v[0][z])]
            terms += [v[x][k] for k in (z - 1, z + 1) if 0 <= k < 4]
            out[x].append(0.0625 * (6.0 * v[x][z] - add(terms)) + d[x][z] * v[x][z])
    return out


def restrict_two(v):
    out = []
    for z in range(2):
        total = v[0][2 * z] + v[0][2 * z + 1] + v[1][2 * z] + v[1][2 * z + 1]
        out.append(0.125 * (total + swap(total, 1, 1)))
    return out


def apply_three(v, d):
    out = []
    for z in range(2):
        beside = before(v[z]) + after(v[z]) + v[1 - z] + along_y(v[z], 2)
        out.append(0.015625 * (6.0 * v[z] - beside) + d[z] * v[z])
    return out


def solve_coarse(r2, d2, mine, narrow):
    shape = r2[0][0].shape
    lane = iota(shape, 1) % 64
    column = 32 * mine + jnp.where(lane < 48, lane, lane - 64)
    inside = (column >= 0) & (column < 32 * narrow)
    i2 = each(lambda d: jnp.where(inside, OMEGA / (0.375 + d), 0.0), d2)
    c2 = each(lambda i, r: i * r, i2, r2)
    left = each(lambda r, a: r - a, r2, apply_two(c2, d2))
    r3, d3 = restrict_two(left), restrict_two(d2)
    i3 = [jnp.where(inside, OMEGA / (0.09375 + d), 0.0) for d in d3]
    e3 = [i * r for i, r in zip(i3, r3)]
    for _ in range(3):
        a3 = apply_three(e3, d3)
        e3 = [e + i * (r - a) for e, i, r, a in zip(e3, i3, r3, a3)]
    one = inside[:1]
    for z in range(2):
        weight = jnp.where(one, jnp.sum(d3[z], axis=0, keepdims=True), 1.0)
        line = jnp.where(one, jnp.sum(r3[z], axis=0, keepdims=True) / weight, 0.0)
        e3[z] = e3[z] + line
    e2 = [[c2[x][z] + e3[z // 2] for z in range(4)] for x in range(2)]
    return each(lambda e, i, r, a: e + i * (r - a), e2, i2, r2, apply_two(e2, d2))


def rise(e2, scratch, at, reach, r1, d1, i1):
    wide = e2[0][0].shape[0]
    blank = jnp.zeros((8, 128), F32)
    for x in range(2):
        for z in range(4):
            scratch[2 * z + x, 0:8, :] = blank
            scratch[2 * z + x, 8 + wide : 16 + wide, :] = blank
            scratch[2 * z + x, 8 : 8 + wide, :] = e2[x][z]
    pair = iota((8, 128), 0) // 2
    rows = []
    for row in range(-reach, 2 + reach):
        x, step = row % 2, row // 2
        tile = blank
        for z in range(4):
            line = scratch[2 * z + x, pl.ds(at + (8 + step), 1), :]
            tile = jnp.where(pair == z, jnp.broadcast_to(line, (8, 128)), tile)
        rows.append(tile)
    shape = (128, LANES)
    matrix = jnp.where(iota(shape, 0) == iota(shape, 1) // 4, 1.0, 0.0).astype(F32)
    spread = jnp.dot(jnp.concatenate(rows, 0), matrix, precision=lax.Precision.HIGHEST)
    e1 = i1 * r1 + double_rows(spread.reshape(len(rows), 8, LANES))
    return e1[1:-1] + i1[1:-1] * (r1[1:-1] - apply_one(e1, d1[1:-1]))


def rows_of(pair, first, stop):
    return [pair[p][first:stop] for p in range(2)]


def finish(up, source, extra, inverse):
    e = [inverse[p] * source[p] + up for p in range(2)]
    a = apply_fine(e[0], e[1], extra[0][1:-1], extra[1][1:-1])
    z = [e[p][1:-1] + inverse[p][1:-1] * (source[p][1:-1] - a[p]) for p in range(2)]
    q = apply_fine(z[0], z[1], extra[0][2:-2], extra[1][2:-2])
    return z, q


def descend(source, extra, inverse):
    c = [i * s for i, s in zip(inverse, source)]
    a = apply_fine(c[0], c[1], extra[0][1:-1], extra[1][1:-1])
    left = [source[p][1:-1] - a[p] for p in range(2)]
    return restrict_fine(left[0], left[1])


def leave_one(r1, d1, i1):
    return r1[1:-1] - apply_one(i1 * r1, d1[1:-1])


def invert_one(d1, first, me_w, me_n, wide, narrow):
    lane = iota(d1.shape, 2)
    column = 128 * me_n + jnp.where(lane < 192, lane, lane - 256)
    line = 4 * me_w + first + iota(d1.shape, 0)
    inside = (column >= 0) & (column < 128 * narrow) & (line >= 0) & (line < 4 * wide)
    return jnp.where(inside, OMEGA / (1.5 + d1), 0.0)


def total(a, b):
    return jnp.sum(jnp.sum(a[0] * b[0] + a[1] * b[1], axis=0), keepdims=True)


def place(values, shape, first):
    lane = iota(shape, len(shape) - 1)
    out = jnp.zeros(shape, F32)
    for i, v in enumerate(values):
        out = jnp.where(lane == first + i, v, out)
    return out


def prepare_kernel(right_in, capacity_in, phase_in, flags_in, own, low, high, right, capacity, phase, flags, done):
    pairs = ((right_in, right), (capacity_in, capacity), (phase_in, phase), (flags_in, flags))
    copies = [pltpu.make_async_copy(a, b, done.at[i]) for i, (a, b) in enumerate(pairs)]
    for copy in copies:
        copy.start()
    for copy in copies:
        copy.wait()
    half = iota((8, 128), 1) < 64
    for p in range(2):
        for x in range(OWN):
            rows = pl.ds(x + 8 * p, 8, stride=16)
            r = right[rows, :]
            weight = jnp.where(phase[rows, :] == 1, 4.0, 1.0)
            d = 0.05 * capacity[rows, :] * weight + 0.5 * flags[rows, :].astype(F32)
            first = jnp.where(half, r, roll(d, 64, 1))
            second = jnp.where(half, roll(r, 64, 1), d)
            for side, value in ((0, first), (1, second)):
                own[side, p, x] = value
                if x < HALO:
                    low[side, p, x] = value
                if x >= OWN - HALO:
                    high[side, p, x - (OWN - HALO)] = value


def down_kernel(wide, narrow, a, b, from_left, from_right, r0, d0, i0, one, send):
    me_w, me_n = lax.axis_index("wide"), lax.axis_index("narrow")
    shape = (EXT, 8, 128)
    half = iota(shape, 2) < 64
    fine = (EXT, 8, LANES)
    lane, row = iota(fine, 2), iota(fine, 0)
    column = 128 * me_n + jnp.where(lane < 192, lane, lane - 256)
    line = 8 * me_w - HALO + row
    inside = (column >= 0) & (column < 128 * narrow) & (line >= 0) & (line < 8 * wide)
    source, extra, inverse = [], [], []
    for p in range(2):
        fa, fb, fl, fr = a[p], b[p], from_left[p], from_right[p]
        own_r = jnp.where(half, fa, roll(fb, 64, 2))
        own_d = jnp.where(half, roll(fa, 64, 2), fb)
        far_r = jnp.where(half, fr, roll(fl, 64, 2))
        far_d = jnp.where(half, roll(fr, 64, 2), fl)
        source.append(jnp.concatenate([own_r, far_r], axis=2))
        extra.append(jnp.concatenate([own_d, far_d], axis=2))
        inverse.append(jnp.where(inside, OMEGA / (6.0 + extra[p]), 0.0))
        r0[p] = source[p]
        d0[p] = extra[p]
        i0[p] = inverse[p]
    vr1 = descend(source, extra, inverse)[1:7]
    vd1 = restrict_fine(extra[0][3:15], extra[1][3:15])
    vi1 = invert_one(vd1, -1, me_w, me_n, wide, narrow)
    one[0] = vr1[1:5]
    one[1] = vd1[1:5]
    send[...] = pack_two(leave_one(vr1, vd1, vi1), 0) + pack_two(vd1[1:5], 64)


def both_halves(tile):
    half = iota(tile.shape, 1) < 64
    other = roll(tile, 64, 1)
    return jnp.where(half, tile, other), jnp.where(half, other, tile)


def turn_kernel(wide, narrow, got, r0, d0, i0, one, below, above, z, q, r1, d1, i1, low, high, send, scratch, small):
    me_w, me_n = lax.axis_index("wide"), lax.axis_index("narrow")
    tiles = split_two(got, wide)
    r2 = each(lambda t: both_halves(t)[0], tiles)
    d2 = each(lambda t: both_halves(t)[1], tiles)
    e2 = solve_coarse(r2, d2, me_n, narrow)
    vr1 = jnp.concatenate([below[0], one[0], above[0]], axis=0)
    vd1 = jnp.concatenate([below[1], one[1], above[1]], axis=0)
    vi1 = invert_one(vd1, -4, me_w, me_n, wide, narrow)
    e1 = rise(e2, scratch, me_w, 2, vr1, vd1, vi1)
    up = double_rows(e1)[1:-1]
    source, extra, inverse = (rows_of(ref, 0, EXT) for ref in (r0, d0, i0))
    vz, vq = finish(up, source, extra, inverse)
    own_z = [v[4:12, :, :128] for v in vz]
    own_q = [v[3:11, :, :128] for v in vq]
    own_r = [v[HALO : HALO + OWN, :, :128] for v in source]
    for p in range(2):
        z[p] = own_z[p]
        q[p] = vq[p]
    below_two = descend(vq, rows_of(d0, 2, 16), rows_of(i0, 2, 16))
    r1[...] = below_two
    d1[...] = vd1[2:10]
    i1[...] = vi1[2:10]
    low[...] = below_two[2:3]
    high[...] = below_two[3:4]
    rows = pack_rows(leave_one(below_two, vd1[3:9], vi1[3:9]), small)
    sums = place([total(own_r, own_z), total(own_z, own_q)], rows.shape, SUMS)
    lane = iota(rows.shape, 1)
    send[...] = jnp.where((lane == SUMS) | (lane == SUMS + 1), sums, rows)


def window_kernel(narrow, got, send, own, right, left):
    me = lax.axis_index("narrow")
    for y in range(got.shape[0] // narrow):
        rows = slice(4 * y, 4 * y + 4)
        own[rows, :] = got[y * narrow + me]
        right[rows, :] = got[y * narrow + jnp.minimum(me + 1, narrow - 1)]
        left[rows, :] = got[y * narrow + jnp.maximum(me - 1, 0)]
    lane = iota(own.shape, 1)
    cell = lane % 64
    halo = jnp.where(cell < 48, roll(right[...], 32, 1), roll(left[...], 32, 1))
    tile = jnp.where(cell < 32, own[...], halo)
    scalars = jnp.sum(jnp.sum(got[...], axis=0), axis=0, keepdims=True) * 0.25
    send[...] = jnp.where((lane == SUMS) | (lane == SUMS + 1), scalars, tile)


def split_deep(ref, wide):
    sides = [[], []]
    across = wide // DEEP
    for z in range(4):
        rows = [ref[pl.ds(4 * y + z, DEEP, stride=4 * across), :] for y in range(across)]
        for side, value in zip(sides, both_halves(jnp.concatenate(rows, 0))):
            side.append(value)
    return sides


def up_again_kernel(wide, narrow, got, first, source, r0, d0, i0, below, r1, above, d1, i1, z0, z1, image1, res1, sums, known, scratch):
    me_w, me_n = lax.axis_index("wide"), lax.axis_index("narrow")
    r2 = split_deep(got, wide)
    d2 = each(lambda t: both_halves(t)[1], split_two(first, wide))
    e2 = solve_coarse(r2, d2, me_n, narrow)
    vr1 = jnp.concatenate([below[...], r1[...], above[...]], axis=0)
    e1 = rise(e2, scratch, me_w, 1, vr1, d1[...], i1[...])
    extra, inverse = rows_of(d0, 3, 15), rows_of(i0, 3, 15)
    vw, vy = finish(double_rows(e1), rows_of(source, 1, 13), extra, inverse)
    vw = [v[1:-1] for v in vw]
    stride = 4 * (wide // DEEP)
    scalars = jnp.sum(got[pl.ds(0, DEEP, stride=stride), :], axis=0, keepdims=True)
    lane = iota((1, 128), 1)
    rho = jnp.sum(jnp.where(lane == SUMS, scalars, 0.0), keepdims=True)
    curve = jnp.sum(jnp.where(lane == SUMS + 1, scalars, 0.0), keepdims=True)
    alpha = (rho / curve).reshape(1, 1, 1)
    own = slice(HALO, HALO + OWN)
    vz0 = [z0[p] for p in range(2)]
    vq0 = [source[p, 3:11, :, :128] for p in range(2)]
    vz1 = [vz0[p] - alpha * vw[p][:, :, :128] for p in range(2)]
    vi1 = [vq0[p] - alpha * vy[p][:, :, :128] for p in range(2)]
    vr1 = [r0[p, own, :, :128] - alpha * vq0[p] for p in range(2)]
    for p in range(2):
        z1[p] = vz1[p]
        image1[p] = vi1[p]
        res1[p] = vr1[p]
    cross = total(vz1, vq0) + total(vz0, vi1)
    sums[...] = place([total(vr1, vz1), total(vz1, vi1), cross], (1, 128), 0)
    known[...] = place([rho, curve], (1, 128), 0)


def last_kernel(got, known, z0, source, z1, image1, res1, field, residual):
    scalars = jnp.sum(got[...], axis=0, keepdims=True)
    lane = iota((1, 128), 1)

    def pick(vector, at):
        return jnp.sum(jnp.where(lane == at, vector, 0.0), keepdims=True)

    rho, curve = pick(known[...], 0), pick(known[...], 1)
    rho_next, square, cross = (pick(scalars, i) for i in range(3))
    alpha = rho / curve
    beta = rho_next / rho
    alpha_next = rho_next / (square + beta * cross + beta * beta * curve)
    for p in range(2):
        for x in range(OWN):
            rows = pl.ds(x + 8 * p, 8, stride=16)
            z, q = z0[p, x], source[p, 3 + x, :, :128]
            field[rows, :] = alpha * z + alpha_next * (z1[p, x] + beta * z)
            residual[rows, :] = res1[p, x] - alpha_next * (image1[p, x] + beta * q)


def call(kernel, outs, *args, scratch=(), space=pltpu.VMEM, limit=40):
    return pl.pallas_call(
        kernel,
        out_shape=tuple(jax.ShapeDtypeStruct(s, F32) for s in outs),
        in_specs=[pl.BlockSpec(memory_space=space)] * len(args),
        out_specs=tuple(pl.BlockSpec(memory_space=pltpu.VMEM) for _ in outs),
        scratch_shapes=scratch,
        compiler_params=pltpu.CompilerParams(vmem_limit_bytes=limit * 1024 * 1024),
    )(*args)


def gathered(array, axis, groups=None):
    peers = lax.axis_size(axis) if groups is None else len(groups[0])
    slots = jnp.broadcast_to(array[None], (peers,) + array.shape)
    return lax.all_to_all(slots, axis, 0, 0, axis_index_groups=groups)


def to_next(array, axis):
    n = lax.axis_size(axis)
    return lax.ppermute(array, axis, [(i, i + 1) for i in range(n - 1)])


def to_previous(array, axis):
    n = lax.axis_size(axis)
    return lax.ppermute(array, axis, [(i + 1, i) for i in range(n - 1)])


def on_device(right_side, capacity, phase, mold_flags):
    wide, narrow = lax.axis_size("wide"), lax.axis_size("narrow")
    flat = [v.reshape(128, 128) for v in (right_side, capacity, phase, mold_flags)]
    edge = (2, 2, HALO, 8, 128)
    staged = [pltpu.VMEM((128, 128), v.dtype) for v in flat]
    own, low, high = call(
        prepare_kernel,
        [(2, 2, OWN, 8, 128), edge, edge],
        *flat,
        scratch=staged + [pltpu.SemaphoreType.DMA((4,))],
        space=pl.ANY,
        limit=63,
    )
    below, above = to_next(high, "wide"), to_previous(low, "wide")
    a = jnp.concatenate([below[0], own[0], above[0]], axis=1)
    b = jnp.concatenate([below[1], own[1], above[1]], axis=1)
    from_left, from_right = to_next(b, "narrow"), to_previous(a, "narrow")
    fine = (2, EXT, 8, LANES)
    r0, d0, i0, one, send = call(
        functools.partial(down_kernel, wide, narrow),
        [fine, fine, fine, (2, 4, 8, LANES), (8, 128)],
        a, b, from_left, from_right,
    )
    below, above = to_next(one, "wide"), to_previous(one, "wide")
    first = gathered(send, "wide").reshape(8 * wide, 128)
    block, coarse, line = (2, OWN, 8, 128), (8, 8, LANES), (1, 8, LANES)
    scratch = [pltpu.VMEM((8, wide + 16, 128), F32)]
    z0, source, r1, d1, i1, low, high, send = call(
        functools.partial(turn_kernel, wide, narrow),
        [block, (2, 14, 8, LANES), (6, 8, LANES), coarse, coarse, line, line, (4, 128)],
        first, r0, d0, i0, one, below, above,
        scratch=scratch + [pltpu.VMEM((8, 128), F32)],
    )
    below, above = to_next(high, "wide"), to_previous(low, "wide")
    across = wide // DEEP
    near = [
        [(DEEP * y + z) * narrow + n for y in range(across) for n in range(narrow)]
        for z in range(DEEP)
    ]
    far = [[DEEP * y + z for z in range(DEEP)] for y in range(across)]
    rows = (4 * across, 128)
    (send,) = call(
        functools.partial(window_kernel, narrow),
        [rows],
        gathered(send, ("wide", "narrow"), near),
        scratch=[pltpu.VMEM(rows, F32)] * 3,
    )
    second = gathered(send, "wide", far).reshape(DEEP * 4 * across, 128)
    z1, image1, res1, sums, known = call(
        functools.partial(up_again_kernel, wide, narrow),
        [block, block, block, (1, 128), (1, 128)],
        second, first, source, r0, d0, i0, below, r1, above, d1, i1, z0,
        scratch=scratch,
    )
    sums = jnp.sum(gathered(sums, "narrow"), axis=0)
    third = gathered(sums, "wide").reshape(wide, 128)
    field, residual = call(
        last_kernel, [(128, 128), (128, 128)], third, known, z0, source, z1, image1, res1
    )
    return field.reshape(right_side.shape), residual.reshape(right_side.shape)


def solution(mesh):
    spec = P(None, "wide", "narrow")
    return jax.shard_map(
        on_device, mesh=mesh, in_specs=(spec,) * 4, out_specs=(spec, spec), check_vma=False
    )
```

```python
import functools

import jax
import jax.numpy as jnp
from jax import lax
from jax.experimental import pallas as pl
from jax.experimental.pallas import tpu as pltpu
from jax.sharding import PartitionSpec as P

OMEGA = 0.8
HALO = 5
OWN = 8
EXT = OWN + 2 * HALO
LANES = 256
F32 = jnp.float32
SUMS = 44


def iota(shape, dim):
    return lax.broadcasted_iota(jnp.int32, shape, dim)


def roll(value, shift, axis):
    return pltpu.roll(value, shift % value.shape[axis], axis)


def swap(value, width, axis):
    at = iota(value.shape, axis)
    lower = (at // width) % 2 == 0
    return jnp.where(lower, roll(value, -width, axis), roll(value, width, axis))


def along_y(value, width):
    axis = value.ndim - 1
    return roll(value, width, axis) + roll(value, -width, axis)


def apply_fine(even, odd, extra_even, extra_odd):
    e, o = even[1:-1], odd[1:-1]
    k = iota(e.shape, 1)
    by_e = o + jnp.where(k > 0, roll(o, 1, 1), 0.0) + even[2:] + even[:-2] + along_y(e, 1)
    by_o = e + jnp.where(k < 7, roll(e, -1, 1), 0.0) + odd[2:] + odd[:-2] + along_y(o, 1)
    return 6.0 * e - by_e + extra_even * e, 6.0 * o - by_o + extra_odd * o


def restrict_fine(even, odd):
    both = even + odd
    both = jnp.sum(both.reshape((both.shape[0] // 2, 2) + both.shape[1:]), axis=1)
    return 0.125 * (both + swap(both, 1, 2))


def double_rows(value):
    wide = jnp.broadcast_to(value[:, None], (value.shape[0], 2) + value.shape[1:])
    return wide.reshape((2 * value.shape[0],) + value.shape[1:])


def apply_one(value, extra):
    v = value[1:-1]
    k = iota(v.shape, 1)
    beside = jnp.where(k > 0, roll(v, 1, 1), 0.0) + jnp.where(k < 7, roll(v, -1, 1), 0.0)
    beside = beside + value[2:] + value[:-2] + along_y(v, 2)
    return 0.25 * (6.0 * v - beside) + extra * v


def pack_two(value, first_lane):
    pairs = jnp.sum(value.reshape((2, 2) + value.shape[1:]), axis=1)
    pairs = pairs + swap(pairs, 1, 1)
    rows = jnp.where(iota(pairs.shape[1:], 0) % 2 == 0, pairs[0], pairs[1])
    shape = (LANES, 128)
    matrix = jnp.where(iota(shape, 0) // 4 + first_lane == iota(shape, 1), 0.0625, 0.0)
    return jnp.dot(rows, matrix.astype(F32), precision=lax.Precision.HIGHEST)


def pack_rows(value, scratch):
    pairs = jnp.sum(value.reshape((2, 2) + value.shape[1:]), axis=1)
    pairs = pairs + swap(pairs, 1, 1)
    shape = (LANES, 128)
    out = jnp.zeros((8, 128), F32)
    for x in range(2):
        matrix = jnp.where(iota(shape, 0) // 4 + 64 * x == iota(shape, 1), 0.0625, 0.0)
        out = out + jnp.dot(pairs[x], matrix.astype(F32), precision=lax.Precision.HIGHEST)
    scratch[...] = out
    return scratch[pl.ds(0, 4, stride=2), :]


def split_two(ref, wide):
    return [[ref[pl.ds(2 * z + x, wide, stride=8), :] for z in range(4)] for x in range(2)]


def add(terms):
    return functools.reduce(lambda a, b: a + b, terms)


def before(value):
    return jnp.where(iota(value.shape, 0) > 0, roll(value, 1, 0), 0.0)


def after(value):
    last = value.shape[0] - 1
    return jnp.where(iota(value.shape, 0) < last, roll(value, -1, 0), 0.0)


def each(function, *lists):
    return [[function(*(a[x][z] for a in lists)) for z in range(4)] for x in range(2)]


def apply_two(v, d):
    out = [[], []]
    for x in range(2):
        for z in range(4):
            terms = [along_y(v[x][z], 1), v[1 - x][z]]
            terms += [before(v[1][z])] if x == 0 else [after(v[0][z])]
            terms += [v[x][k] for k in (z - 1, z + 1) if 0 <= k < 4]
            out[x].append(0.0625 * (6.0 * v[x][z] - add(terms)) + d[x][z] * v[x][z])
    return out


def restrict_two(v):
    out = []
    for z in range(2):
        total = v[0][2 * z] + v[0][2 * z + 1] + v[1][2 * z] + v[1][2 * z + 1]
        out.append(0.125 * (total + swap(total, 1, 1)))
    return out


def apply_three(v, d):
    out = []
    for z in range(2):
        beside = before(v[z]) + after(v[z]) + v[1 - z] + along_y(v[z], 2)
        out.append(0.015625 * (6.0 * v[z] - beside) + d[z] * v[z])
    return out


def solve_coarse(r2, d2, mine, narrow):
    shape = r2[0][0].shape
    lane = iota(shape, 1) % 64
    column = 32 * mine + jnp.where(lane < 48, lane, lane - 64)
    inside = (column >= 0) & (column < 32 * narrow)
    i2 = each(lambda d: jnp.where(inside, OMEGA / (0.375 + d), 0.0), d2)
    c2 = each(lambda i, r: i * r, i2, r2)
    left = each(lambda r, a: r - a, r2, apply_two(c2, d2))
    r3, d3 = restrict_two(left), restrict_two(d2)
    i3 = [jnp.where(inside, OMEGA / (0.09375 + d), 0.0) for d in d3]
    e3 = [i * r for i, r in zip(i3, r3)]
    for _ in range(3):
        a3 = apply_three(e3, d3)
        e3 = [e + i * (r - a) for e, i, r, a in zip(e3, i3, r3, a3)]
    one = inside[:1]
    for z in range(2):
        weight = jnp.where(one, jnp.sum(d3[z], axis=0, keepdims=True), 1.0)
        line = jnp.where(one, jnp.sum(r3[z], axis=0, keepdims=True) / weight, 0.0)
        e3[z] = e3[z] + line
    e2 = [[c2[x][z] + e3[z // 2] for z in range(4)] for x in range(2)]
    return each(lambda e, i, r, a: e + i * (r - a), e2, i2, r2, apply_two(e2, d2))


def rise(e2, scratch, at, reach, r1, d1, i1):
    wide = e2[0][0].shape[0]
    blank = jnp.zeros((8, 128), F32)
    for x in range(2):
        for z in range(4):
            scratch[2 * z + x, 0:8, :] = blank
            scratch[2 * z + x, 8 + wide : 16 + wide, :] = blank
            scratch[2 * z + x, 8 : 8 + wide, :] = e2[x][z]
    pair = iota((8, 128), 0) // 2
    rows = []
    for row in range(-reach, 2 + reach):
        x, step = row % 2, row // 2
        tile = blank
        for z in range(4):
            line = scratch[2 * z + x, pl.ds(at + (8 + step), 1), :]
            tile = jnp.where(pair == z, jnp.broadcast_to(line, (8, 128)), tile)
        rows.append(tile)
    shape = (128, LANES)
    matrix = jnp.where(iota(shape, 0) == iota(shape, 1) // 4, 1.0, 0.0).astype(F32)
    spread = jnp.dot(jnp.concatenate(rows, 0), matrix, precision=lax.Precision.HIGHEST)
    e1 = i1 * r1 + double_rows(spread.reshape(len(rows), 8, LANES))
    return e1[1:-1] + i1[1:-1] * (r1[1:-1] - apply_one(e1, d1[1:-1]))


def rows_of(pair, first, stop):
    return [pair[p][first:stop] for p in range(2)]


def finish(up, source, extra, inverse):
    e = [inverse[p] * source[p] + up for p in range(2)]
    a = apply_fine(e[0], e[1], extra[0][1:-1], extra[1][1:-1])
    z = [e[p][1:-1] + inverse[p][1:-1] * (source[p][1:-1] - a[p]) for p in range(2)]
    q = apply_fine(z[0], z[1], extra[0][2:-2], extra[1][2:-2])
    return z, q


def descend(source, extra, inverse):
    c = [i * s for i, s in zip(inverse, source)]
    a = apply_fine(c[0], c[1], extra[0][1:-1], extra[1][1:-1])
    left = [source[p][1:-1] - a[p] for p in range(2)]
    return restrict_fine(left[0], left[1])


def leave_one(r1, d1, i1):
    return r1[1:-1] - apply_one(i1 * r1, d1[1:-1])


def invert_one(d1, first, me_w, me_n, wide, narrow):
    lane = iota(d1.shape, 2)
    column = 128 * me_n + jnp.where(lane < 192, lane, lane - 256)
    line = 4 * me_w + first + iota(d1.shape, 0)
    inside = (column >= 0) & (column < 128 * narrow) & (line >= 0) & (line < 4 * wide)
    return jnp.where(inside, OMEGA / (1.5 + d1), 0.0)


def total(a, b):
    return jnp.sum(jnp.sum(a[0] * b[0] + a[1] * b[1], axis=0), keepdims=True)


def place(values, shape, first):
    lane = iota(shape, len(shape) - 1)
    out = jnp.zeros(shape, F32)
    for i, v in enumerate(values):
        out = jnp.where(lane == first + i, v, out)
    return out


def prepare_kernel(right_in, capacity_in, phase_in, flags_in, own, low, high, right, capacity, phase, flags, done):
    pairs = ((right_in, right), (capacity_in, capacity), (phase_in, phase), (flags_in, flags))
    copies = [pltpu.make_async_copy(a, b, done.at[i]) for i, (a, b) in enumerate(pairs)]
    for copy in copies:
        copy.start()
    for copy in copies:
        copy.wait()
    half = iota((8, 128), 1) < 64
    for p in range(2):
        for x in range(OWN):
            rows = pl.ds(x + 8 * p, 8, stride=16)
            r = right[rows, :]
            weight = jnp.where(phase[rows, :] == 1, 4.0, 1.0)
            d = 0.05 * capacity[rows, :] * weight + 0.5 * flags[rows, :].astype(F32)
            first = jnp.where(half, r, roll(d, 64, 1))
            second = jnp.where(half, roll(r, 64, 1), d)
            for side, value in ((0, first), (1, second)):
                own[side, p, x] = value
                if x < HALO:
                    low[side, p, x] = value
                if x >= OWN - HALO:
                    high[side, p, x - (OWN - HALO)] = value


def down_kernel(wide, narrow, a, b, from_left, from_right, r0, d0, i0, one, send):
    me_w, me_n = lax.axis_index("wide"), lax.axis_index("narrow")
    shape = (EXT, 8, 128)
    half = iota(shape, 2) < 64
    fine = (EXT, 8, LANES)
    lane, row = iota(fine, 2), iota(fine, 0)
    column = 128 * me_n + jnp.where(lane < 192, lane, lane - 256)
    line = 8 * me_w - HALO + row
    inside = (column >= 0) & (column < 128 * narrow) & (line >= 0) & (line < 8 * wide)
    source, extra, inverse = [], [], []
    for p in range(2):
        fa, fb, fl, fr = a[p], b[p], from_left[p], from_right[p]
        own_r = jnp.where(half, fa, roll(fb, 64, 2))
        own_d = jnp.where(half, roll(fa, 64, 2), fb)
        far_r = jnp.where(half, fr, roll(fl, 64, 2))
        far_d = jnp.where(half, roll(fr, 64, 2), fl)
        source.append(jnp.concatenate([own_r, far_r], axis=2))
        extra.append(jnp.concatenate([own_d, far_d], axis=2))
        inverse.append(jnp.where(inside, OMEGA / (6.0 + extra[p]), 0.0))
        r0[p] = source[p]
        d0[p] = extra[p]
        i0[p] = inverse[p]
    vr1 = descend(source, extra, inverse)[1:7]
    vd1 = restrict_fine(extra[0][3:15], extra[1][3:15])
    vi1 = invert_one(vd1, -1, me_w, me_n, wide, narrow)
    one[0] = vr1[1:5]
    one[1] = vd1[1:5]
    send[...] = pack_two(leave_one(vr1, vd1, vi1), 0) + pack_two(vd1[1:5], 64)


def both_halves(tile):
    half = iota(tile.shape, 1) < 64
    other = roll(tile, 64, 1)
    return jnp.where(half, tile, other), jnp.where(half, other, tile)


def turn_kernel(wide, narrow, got, r0, d0, i0, one, below, above, z, q, r1, d1, i1, low, high, send, scratch, small):
    me_w, me_n = lax.axis_index("wide"), lax.axis_index("narrow")
    tiles = split_two(got, wide)
    r2 = each(lambda t: both_halves(t)[0], tiles)
    d2 = each(lambda t: both_halves(t)[1], tiles)
    e2 = solve_coarse(r2, d2, me_n, narrow)
    vr1 = jnp.concatenate([below[0], one[0], above[0]], axis=0)
    vd1 = jnp.concatenate([below[1], one[1], above[1]], axis=0)
    vi1 = invert_one(vd1, -4, me_w, me_n, wide, narrow)
    e1 = rise(e2, scratch, me_w, 2, vr1, vd1, vi1)
    up = double_rows(e1)[1:-1]
    source, extra, inverse = (rows_of(ref, 0, EXT) for ref in (r0, d0, i0))
    vz, vq = finish(up, source, extra, inverse)
    own_z = [v[4:12, :, :128] for v in vz]
    own_q = [v[3:11, :, :128] for v in vq]
    own_r = [v[HALO : HALO + OWN, :, :128] for v in source]
    for p in range(2):
        z[p] = own_z[p]
        q[p] = vq[p]
    below_two = descend(vq, rows_of(d0, 2, 16), rows_of(i0, 2, 16))
    r1[...] = below_two
    d1[...] = vd1[2:10]
    i1[...] = vi1[2:10]
    low[...] = below_two[2:3]
    high[...] = below_two[3:4]
    rows = pack_rows(leave_one(below_two, vd1[3:9], vi1[3:9]), small)
    sums = place([total(own_r, own_z), total(own_z, own_q)], rows.shape, SUMS)
    lane = iota(rows.shape, 1)
    send[0:4, :] = jnp.where((lane == SUMS) | (lane == SUMS + 1), sums, rows)
    send[4:8, :] = jnp.zeros(rows.shape, F32)


def window_kernel(own, right, left, send):
    lane = iota(own.shape, 1)
    cell = lane % 64
    halo = jnp.where(cell < 48, roll(right[...], 32, 1), roll(left[...], 32, 1))
    keep = (cell < 32) | (lane == SUMS) | (lane == SUMS + 1)
    send[...] = jnp.where(keep, own[...], halo)[0:4]


def split_rows(ref, wide):
    sides = [[], []]
    for z in range(4):
        for side, value in zip(sides, both_halves(ref[pl.ds(z, wide, stride=4), :])):
            side.append(value)
    return sides


def up_again_kernel(wide, narrow, got, first, source, r0, d0, i0, below, r1, above, d1, i1, z0, w0, y0, sums, scratch):
    me_w, me_n = lax.axis_index("wide"), lax.axis_index("narrow")
    r2 = split_rows(got, wide)
    d2 = each(lambda t: both_halves(t)[1], split_two(first, wide))
    e2 = solve_coarse(r2, d2, me_n, narrow)
    vr1 = jnp.concatenate([below[...], r1[...], above[...]], axis=0)
    e1 = rise(e2, scratch, me_w, 1, vr1, d1[...], i1[...])
    extra, inverse = rows_of(d0, 3, 15), rows_of(i0, 3, 15)
    vw, vy = finish(double_rows(e1), rows_of(source, 1, 13), extra, inverse)
    w = [v[1:-1, :, :128] for v in vw]
    y = [v[:, :, :128] for v in vy]
    scalars = jnp.sum(got[pl.ds(0, wide, stride=4), :], axis=0, keepdims=True)
    lane = iota((1, 128), 1)
    rho = jnp.sum(jnp.where(lane == SUMS, scalars, 0.0), keepdims=True)
    curve = jnp.sum(jnp.where(lane == SUMS + 1, scalars, 0.0), keepdims=True)
    ratio = rho / jnp.where(curve > 0.0, curve, 1.0)
    shift = jnp.where(curve > 0.0, jnp.minimum(jnp.maximum(ratio, 0.0), 8.0), 0.0)
    s = shift.reshape(1, 1, 1)
    z = [z0[p] for p in range(2)]
    q = [source[p, 3:11, :, :128] for p in range(2)]
    r = [r0[p, HALO : HALO + OWN, :, :128] for p in range(2)]
    for p in range(2):
        w0[p] = w[p]
        y0[p] = y[p]
    rs = [r[p] - s * q[p] for p in range(2)]
    zs = [z[p] - s * w[p] for p in range(2)]
    ys = [q[p] - s * y[p] for p in range(2)]
    values = [
        shift,
        total(r, z),
        total(z, q),
        total(rs, zs),
        total(rs, w) + total(q, zs),
        total(q, w),
        total(zs, ys),
        total(w, ys) + total(zs, y),
        total(w, y),
        total(zs, q) + total(z, ys),
        total(w, q) + total(z, y),
    ]
    sums[...] = place(values, (1, 128), 0)


def last_kernel(got, z0, source, w0, y0, r0, field, residual):
    lane = iota(got.shape, 1)

    def pick(at):
        return jnp.sum(jnp.where(lane == at, got[...], 0.0), axis=1, keepdims=True)

    def whole(columns):
        return jnp.sum(columns, axis=0, keepdims=True)

    shift, g = pick(0), [pick(i) for i in range(1, 11)]
    rho, curve = whole(g[0]), whole(g[1])
    alpha = rho / curve
    t = alpha - shift
    rho_next = whole(g[2] - t * (g[3] - t * g[4]))
    square = whole(g[5] - t * (g[6] - t * g[7]))
    cross = whole(g[8] - t * g[9])
    beta = rho_next / rho
    alpha_next = rho_next / (square + beta * cross + beta * beta * curve)
    for p in range(2):
        for x in range(OWN):
            rows = pl.ds(x + 8 * p, 8, stride=16)
            z, q = z0[p, x], source[p, 3 + x, :, :128]
            step = (z - alpha * w0[p, x]) + beta * z
            image = (q - alpha * y0[p, x]) + beta * q
            field[rows, :] = alpha * z + alpha_next * step
            residual[rows, :] = (r0[p, HALO + x, :, :128] - alpha * q) - alpha_next * image


def call(kernel, outs, *args, scratch=(), space=pltpu.VMEM, limit=40):
    return pl.pallas_call(
        kernel,
        out_shape=tuple(jax.ShapeDtypeStruct(s, F32) for s in outs),
        in_specs=[pl.BlockSpec(memory_space=space)] * len(args),
        out_specs=tuple(pl.BlockSpec(memory_space=pltpu.VMEM) for _ in outs),
        scratch_shapes=scratch,
        compiler_params=pltpu.CompilerParams(vmem_limit_bytes=limit * 1024 * 1024),
    )(*args)


def gathered(array, axis):
    peers = lax.axis_size(axis)
    slots = jnp.broadcast_to(array[None], (peers,) + array.shape)
    return lax.all_to_all(slots, axis, 0, 0)


def to_next(array, axis):
    n = lax.axis_size(axis)
    return lax.ppermute(array, axis, [(i, i + 1) for i in range(n - 1)])


def to_previous(array, axis):
    n = lax.axis_size(axis)
    return lax.ppermute(array, axis, [(i + 1, i) for i in range(n - 1)])


def around(array, axis, step):
    n = lax.axis_size(axis)
    return lax.ppermute(array, axis, [(i, (i + step) % n) for i in range(n)])


def on_device(right_side, capacity, phase, mold_flags):
    wide, narrow = lax.axis_size("wide"), lax.axis_size("narrow")
    flat = [v.reshape(128, 128) for v in (right_side, capacity, phase, mold_flags)]
    edge = (2, 2, HALO, 8, 128)
    staged = [pltpu.VMEM((128, 128), v.dtype) for v in flat]
    own, low, high = call(
        prepare_kernel,
        [(2, 2, OWN, 8, 128), edge, edge],
        *flat,
        scratch=staged + [pltpu.SemaphoreType.DMA((4,))],
        space=pl.ANY,
        limit=63,
    )
    below, above = to_next(high, "wide"), to_previous(low, "wide")
    a = jnp.concatenate([below[0], own[0], above[0]], axis=1)
    b = jnp.concatenate([below[1], own[1], above[1]], axis=1)
    from_left, from_right = around(b, "narrow", 1), around(a, "narrow", -1)
    fine = (2, EXT, 8, LANES)
    r0, d0, i0, one, send = call(
        functools.partial(down_kernel, wide, narrow),
        [fine, fine, fine, (2, 4, 8, LANES), (8, 128)],
        a, b, from_left, from_right,
    )
    below, above = to_next(one, "wide"), to_previous(one, "wide")
    first = gathered(send, "wide").reshape(8 * wide, 128)
    block, coarse, line = (2, OWN, 8, 128), (8, 8, LANES), (1, 8, LANES)
    scratch = [pltpu.VMEM((8, wide + 16, 128), F32)]
    z0, source, r1, d1, i1, low, high, send = call(
        functools.partial(turn_kernel, wide, narrow),
        [block, (2, 14, 8, LANES), (6, 8, LANES), coarse, coarse, line, line, (8, 128)],
        first, r0, d0, i0, one, below, above,
        scratch=scratch + [pltpu.VMEM((8, 128), F32)],
    )
    below, above = to_next(high, "wide"), to_previous(low, "wide")
    from_left, from_right = around(send, "narrow", 1), around(send, "narrow", -1)
    (send,) = call(window_kernel, [(4, 128)], send, from_right, from_left)
    second = gathered(send, "wide").reshape(4 * wide, 128)
    w0, y0, sums = call(
        functools.partial(up_again_kernel, wide, narrow),
        [block, block, (1, 128)],
        second, first, source, r0, d0, i0, below, r1, above, d1, i1, z0,
        scratch=scratch,
    )
    parts = gathered(sums, "wide")
    first_lane = jnp.arange(128) == 0
    sums = jnp.where(first_lane, parts[0], jnp.sum(parts, axis=0))
    third = gathered(sums, "narrow").reshape(narrow, 128)
    field, residual = call(
        last_kernel, [(128, 128), (128, 128)], third, z0, source, w0, y0, r0
    )
    return field.reshape(right_side.shape), residual.reshape(right_side.shape)


def solution(mesh):
    spec = P(None, "wide", "narrow")
    return jax.shard_map(
        on_device, mesh=mesh, in_specs=(spec,) * 4, out_specs=(spec, spec), check_vma=False
    )
```

```python
import functools

import jax
import jax.numpy as jnp
from jax import lax
from jax.experimental import pallas as pl
from jax.experimental.pallas import tpu as pltpu
from jax.sharding import PartitionSpec as P

OMEGA = 0.8
HALO = 5
OWN = 8
EXT = OWN + 2 * HALO
LANES = 256
F32 = jnp.float32
DEEP = 16
SUMS = 44


def iota(shape, dim):
    return lax.broadcasted_iota(jnp.int32, shape, dim)


def roll(value, shift, axis):
    return pltpu.roll(value, shift % value.shape[axis], axis)


def swap(value, width, axis):
    at = iota(value.shape, axis)
    lower = (at // width) % 2 == 0
    return jnp.where(lower, roll(value, -width, axis), roll(value, width, axis))


def along_y(value, width):
    axis = value.ndim - 1
    return roll(value, width, axis) + roll(value, -width, axis)


def apply_fine(even, odd, extra_even, extra_odd):
    e, o = even[1:-1], odd[1:-1]
    k = iota(e.shape, 1)
    by_e = o + jnp.where(k > 0, roll(o, 1, 1), 0.0) + even[2:] + even[:-2] + along_y(e, 1)
    by_o = e + jnp.where(k < 7, roll(e, -1, 1), 0.0) + odd[2:] + odd[:-2] + along_y(o, 1)
    return 6.0 * e - by_e + extra_even * e, 6.0 * o - by_o + extra_odd * o


def restrict_fine(even, odd):
    both = even + odd
    both = jnp.sum(both.reshape((both.shape[0] // 2, 2) + both.shape[1:]), axis=1)
    return 0.125 * (both + swap(both, 1, 2))


def double_rows(value):
    wide = jnp.broadcast_to(value[:, None], (value.shape[0], 2) + value.shape[1:])
    return wide.reshape((2 * value.shape[0],) + value.shape[1:])


def apply_one(value, extra):
    v = value[1:-1]
    k = iota(v.shape, 1)
    beside = jnp.where(k > 0, roll(v, 1, 1), 0.0) + jnp.where(k < 7, roll(v, -1, 1), 0.0)
    beside = beside + value[2:] + value[:-2] + along_y(v, 2)
    return 0.25 * (6.0 * v - beside) + extra * v


def pack_two(value, first_lane):
    pairs = jnp.sum(value.reshape((2, 2) + value.shape[1:]), axis=1)
    pairs = pairs + swap(pairs, 1, 1)
    rows = jnp.where(iota(pairs.shape[1:], 0) % 2 == 0, pairs[0], pairs[1])
    shape = (LANES, 128)
    matrix = jnp.where(iota(shape, 0) // 4 + first_lane == iota(shape, 1), 0.0625, 0.0)
    return jnp.dot(rows, matrix.astype(F32), precision=lax.Precision.HIGHEST)


def pack_rows(value, scratch):
    pairs = jnp.sum(value.reshape((2, 2) + value.shape[1:]), axis=1)
    pairs = pairs + swap(pairs, 1, 1)
    shape = (LANES, 128)
    out = jnp.zeros((8, 128), F32)
    for x in range(2):
        matrix = jnp.where(iota(shape, 0) // 4 + 64 * x == iota(shape, 1), 0.0625, 0.0)
        out = out + jnp.dot(pairs[x], matrix.astype(F32), precision=lax.Precision.HIGHEST)
    scratch[...] = out
    return scratch[pl.ds(0, 4, stride=2), :]


def split_two(ref, wide):
    return [[ref[pl.ds(2 * z + x, wide, stride=8), :] for z in range(4)] for x in range(2)]


def add(terms):
    return functools.reduce(lambda a, b: a + b, terms)


def before(value):
    return jnp.where(iota(value.shape, 0) > 0, roll(value, 1, 0), 0.0)


def after(value):
    last = value.shape[0] - 1
    return jnp.where(iota(value.shape, 0) < last, roll(value, -1, 0), 0.0)


def each(function, *lists):
    return [[function(*(a[x][z] for a in lists)) for z in range(4)] for x in range(2)]


def apply_two(v, d):
    out = [[], []]
    for x in range(2):
        for z in range(4):
            terms = [along_y(v[x][z], 1), v[1 - x][z]]
            terms += [before(v[1][z])] if x == 0 else [after(v[0][z])]
            terms += [v[x][k] for k in (z - 1, z + 1) if 0 <= k < 4]
            out[x].append(0.0625 * (6.0 * v[x][z] - add(terms)) + d[x][z] * v[x][z])
    return out


def restrict_two(v):
    out = []
    for z in range(2):
        total = v[0][2 * z] + v[0][2 * z + 1] + v[1][2 * z] + v[1][2 * z + 1]
        out.append(0.125 * (total + swap(total, 1, 1)))
    return out


def apply_three(v, d):
    out = []
    for z in range(2):
        beside = before(v[z]) + after(v[z]) + v[1 - z] + along_y(v[z], 2)
        out.append(0.015625 * (6.0 * v[z] - beside) + d[z] * v[z])
    return out


def solve_coarse(r2, d2, mine, narrow):
    shape = r2[0][0].shape
    lane = iota(shape, 1) % 64
    column = 32 * mine + jnp.where(lane < 48, lane, lane - 64)
    inside = (column >= 0) & (column < 32 * narrow)
    i2 = each(lambda d: jnp.where(inside, OMEGA / (0.375 + d), 0.0), d2)
    c2 = each(lambda i, r: i * r, i2, r2)
    left = each(lambda r, a: r - a, r2, apply_two(c2, d2))
    r3, d3 = restrict_two(left), restrict_two(d2)
    i3 = [jnp.where(inside, OMEGA / (0.09375 + d), 0.0) for d in d3]
    e3 = [i * r for i, r in zip(i3, r3)]
    for _ in range(3):
        a3 = apply_three(e3, d3)
        e3 = [e + i * (r - a) for e, i, r, a in zip(e3, i3, r3, a3)]
    one = inside[:1]
    for z in range(2):
        weight = jnp.where(one, jnp.sum(d3[z], axis=0, keepdims=True), 1.0)
        line = jnp.where(one, jnp.sum(r3[z], axis=0, keepdims=True) / weight, 0.0)
        e3[z] = e3[z] + line
    e2 = [[c2[x][z] + e3[z // 2] for z in range(4)] for x in range(2)]
    return each(lambda e, i, r, a: e + i * (r - a), e2, i2, r2, apply_two(e2, d2))


def rise(e2, scratch, at, reach, r1, d1, i1):
    wide = e2[0][0].shape[0]
    blank = jnp.zeros((8, 128), F32)
    for x in range(2):
        for z in range(4):
            scratch[2 * z + x, 0:8, :] = blank
            scratch[2 * z + x, 8 + wide : 16 + wide, :] = blank
            scratch[2 * z + x, 8 : 8 + wide, :] = e2[x][z]
    pair = iota((8, 128), 0) // 2
    rows = []
    for row in range(-reach, 2 + reach):
        x, step = row % 2, row // 2
        tile = blank
        for z in range(4):
            line = scratch[2 * z + x, pl.ds(at + (8 + step), 1), :]
            tile = jnp.where(pair == z, jnp.broadcast_to(line, (8, 128)), tile)
        rows.append(tile)
    shape = (128, LANES)
    matrix = jnp.where(iota(shape, 0) == iota(shape, 1) // 4, 1.0, 0.0).astype(F32)
    spread = jnp.dot(jnp.concatenate(rows, 0), matrix, precision=lax.Precision.HIGHEST)
    e1 = i1 * r1 + double_rows(spread.reshape(len(rows), 8, LANES))
    return e1[1:-1] + i1[1:-1] * (r1[1:-1] - apply_one(e1, d1[1:-1]))


def rows_of(pair, first, stop):
    return [pair[p][first:stop] for p in range(2)]


def finish(up, source, extra, inverse):
    e = [inverse[p] * source[p] + up for p in range(2)]
    a = apply_fine(e[0], e[1], extra[0][1:-1], extra[1][1:-1])
    z = [e[p][1:-1] + inverse[p][1:-1] * (source[p][1:-1] - a[p]) for p in range(2)]
    q = apply_fine(z[0], z[1], extra[0][2:-2], extra[1][2:-2])
    return z, q


def descend(source, extra, inverse):
    c = [i * s for i, s in zip(inverse, source)]
    a = apply_fine(c[0], c[1], extra[0][1:-1], extra[1][1:-1])
    left = [source[p][1:-1] - a[p] for p in range(2)]
    return restrict_fine(left[0], left[1])


def leave_one(r1, d1, i1):
    return r1[1:-1] - apply_one(i1 * r1, d1[1:-1])


def invert_one(d1, first, me_w, me_n, wide, narrow):
    lane = iota(d1.shape, 2)
    column = 128 * me_n + jnp.where(lane < 192, lane, lane - 256)
    line = 4 * me_w + first + iota(d1.shape, 0)
    inside = (column >= 0) & (column < 128 * narrow) & (line >= 0) & (line < 4 * wide)
    return jnp.where(inside, OMEGA / (1.5 + d1), 0.0)


def total(a, b):
    return jnp.sum(jnp.sum(a[0] * b[0] + a[1] * b[1], axis=0), keepdims=True)


def place(values, shape, first):
    lane = iota(shape, len(shape) - 1)
    out = jnp.zeros(shape, F32)
    for i, v in enumerate(values):
        out = jnp.where(lane == first + i, v, out)
    return out


def prepare_kernel(right_in, capacity_in, phase_in, flags_in, own, low, high, right, capacity, phase, flags, done):
    pairs = ((right_in, right), (capacity_in, capacity), (phase_in, phase), (flags_in, flags))
    copies = [pltpu.make_async_copy(a, b, done.at[i]) for i, (a, b) in enumerate(pairs)]
    for copy in copies:
        copy.start()
    for copy in copies:
        copy.wait()
    half = iota((8, 128), 1) < 64
    for p in range(2):
        for x in range(OWN):
            rows = pl.ds(x + 8 * p, 8, stride=16)
            r = right[rows, :]
            weight = jnp.where(phase[rows, :] == 1, 4.0, 1.0)
            d = 0.05 * capacity[rows, :] * weight + 0.5 * flags[rows, :].astype(F32)
            first = jnp.where(half, r, roll(d, 64, 1))
            second = jnp.where(half, roll(r, 64, 1), d)
            for side, value in ((0, first), (1, second)):
                own[side, p, x] = value
                if x < HALO:
                    low[side, p, x] = value
                if x >= OWN - HALO:
                    high[side, p, x - (OWN - HALO)] = value


def down_kernel(wide, narrow, a, b, from_left, from_right, r0, d0, i0, one, low, high, send):
    me_w, me_n = lax.axis_index("wide"), lax.axis_index("narrow")
    shape = (EXT, 8, 128)
    half = iota(shape, 2) < 64
    fine = (EXT, 8, LANES)
    lane, row = iota(fine, 2), iota(fine, 0)
    column = 128 * me_n + jnp.where(lane < 192, lane, lane - 256)
    line = 8 * me_w - HALO + row
    inside = (column >= 0) & (column < 128 * narrow) & (line >= 0) & (line < 8 * wide)
    source, extra, inverse = [], [], []
    for p in range(2):
        fa, fb, fl, fr = a[p], b[p], from_left[p], from_right[p]
        own_r = jnp.where(half, fa, roll(fb, 64, 2))
        own_d = jnp.where(half, roll(fa, 64, 2), fb)
        far_r = jnp.where(half, fr, roll(fl, 64, 2))
        far_d = jnp.where(half, roll(fr, 64, 2), fl)
        source.append(jnp.concatenate([own_r, far_r], axis=2))
        extra.append(jnp.concatenate([own_d, far_d], axis=2))
        inverse.append(jnp.where(inside, OMEGA / (6.0 + extra[p]), 0.0))
        r0[p] = source[p]
        d0[p] = extra[p]
        i0[p] = inverse[p]
    vr1 = descend(source, extra, inverse)
    vd1 = restrict_fine(extra[0][1:17], extra[1][1:17])
    vi1 = invert_one(vd1, -2, me_w, me_n, wide, narrow)
    for side, value in ((0, vr1), (1, vd1)):
        one[side] = value
        high[side] = value[2:4]
        low[side] = value[4:6]
    left = leave_one(vr1[1:7], vd1[1:7], vi1[1:7])
    tile = pack_two(left, 0) + pack_two(vd1[2:6], 64)
    send[...] = jnp.broadcast_to(tile, send.shape)


def both_halves(tile):
    half = iota(tile.shape, 1) < 64
    other = roll(tile, 64, 1)
    return jnp.where(half, tile, other), jnp.where(half, other, tile)


def turn_kernel(wide, narrow, got, r0, d0, i0, one, below, above, z, q, r1, d1, i1, low, high, send, scratch, small):
    me_w, me_n = lax.axis_index("wide"), lax.axis_index("narrow")
    tiles = split_two(got, wide)
    r2 = each(lambda t: both_halves(t)[0], tiles)
    d2 = each(lambda t: both_halves(t)[1], tiles)
    e2 = solve_coarse(r2, d2, me_n, narrow)
    vr1 = jnp.concatenate([below[0], one[0], above[0]], axis=0)
    vd1 = jnp.concatenate([below[1], one[1], above[1]], axis=0)
    vi1 = invert_one(vd1, -4, me_w, me_n, wide, narrow)
    e1 = rise(e2, scratch, me_w, 2, vr1, vd1, vi1)
    up = double_rows(e1)[1:-1]
    source, extra, inverse = (rows_of(ref, 0, EXT) for ref in (r0, d0, i0))
    vz, vq = finish(up, source, extra, inverse)
    own_z = [v[4:12, :, :128] for v in vz]
    own_q = [v[3:11, :, :128] for v in vq]
    own_r = [v[HALO : HALO + OWN, :, :128] for v in source]
    for p in range(2):
        z[p] = own_z[p]
        q[p] = vq[p]
    below_two = descend(vq, rows_of(d0, 2, 16), rows_of(i0, 2, 16))
    r1[...] = below_two
    d1[...] = vd1[2:10]
    i1[...] = vi1[2:10]
    low[...] = below_two[2:3]
    high[...] = below_two[3:4]
    rows = pack_rows(leave_one(below_two, vd1[3:9], vi1[3:9]), small)
    sums = place([total(own_r, own_z), total(own_z, own_q)], rows.shape, SUMS)
    lane = iota(rows.shape, 1)
    send[0:4, :] = jnp.where((lane == SUMS) | (lane == SUMS + 1), sums, rows)
    send[4:8, :] = jnp.zeros(rows.shape, F32)


def window_kernel(own, right, left, send):
    lane = iota(own.shape, 1)
    cell = lane % 64
    halo = jnp.where(cell < 48, roll(right[...], 32, 1), roll(left[...], 32, 1))
    keep = (cell < 32) | (lane == SUMS) | (lane == SUMS + 1)
    send[...] = jnp.broadcast_to(jnp.where(keep, own[...], halo)[0:4], send.shape)


def split_rows(ref, wide):
    sides = [[], []]
    for z in range(4):
        for side, value in zip(sides, both_halves(ref[pl.ds(z, wide, stride=4), :])):
            side.append(value)
    return sides


def up_again_kernel(wide, narrow, got, first, source, r0, d0, i0, below, r1, above, d1, i1, z0, w0, y0, sums, scratch):
    me_w, me_n = lax.axis_index("wide"), lax.axis_index("narrow")
    r2 = split_rows(got, wide)
    d2 = each(lambda t: both_halves(t)[1], split_two(first, wide))
    e2 = solve_coarse(r2, d2, me_n, narrow)
    vr1 = jnp.concatenate([below[...], r1[...], above[...]], axis=0)
    e1 = rise(e2, scratch, me_w, 1, vr1, d1[...], i1[...])
    extra, inverse = rows_of(d0, 3, 15), rows_of(i0, 3, 15)
    vw, vy = finish(double_rows(e1), rows_of(source, 1, 13), extra, inverse)
    w = [v[1:-1, :, :128] for v in vw]
    y = [v[:, :, :128] for v in vy]
    scalars = jnp.sum(got[pl.ds(0, wide, stride=4), :], axis=0, keepdims=True)
    lane = iota((1, 128), 1)
    rho = jnp.sum(jnp.where(lane == SUMS, scalars, 0.0), keepdims=True)
    curve = jnp.sum(jnp.where(lane == SUMS + 1, scalars, 0.0), keepdims=True)
    ratio = rho / jnp.where(curve > 0.0, curve, 1.0)
    shift = jnp.where(curve > 0.0, jnp.minimum(jnp.maximum(ratio, 0.0), 8.0), 0.0)
    s = shift.reshape(1, 1, 1)
    z = [z0[p] for p in range(2)]
    q = [source[p, 3:11, :, :128] for p in range(2)]
    r = [r0[p, HALO : HALO + OWN, :, :128] for p in range(2)]
    for p in range(2):
        w0[p] = w[p]
        y0[p] = y[p]
    rs = [r[p] - s * q[p] for p in range(2)]
    zs = [z[p] - s * w[p] for p in range(2)]
    ys = [q[p] - s * y[p] for p in range(2)]
    values = [
        shift,
        total(r, z),
        total(z, q),
        total(rs, zs),
        total(rs, w) + total(q, zs),
        total(q, w),
        total(zs, ys),
        total(w, ys) + total(zs, y),
        total(w, y),
        total(zs, q) + total(z, ys),
        total(w, q) + total(z, y),
    ]
    sums[...] = jnp.broadcast_to(place(values, (1, 128), 0), sums.shape)


def last_kernel(got, z0, source, w0, y0, r0, field, residual):
    lane = iota(got.shape, 1)

    def pick(at):
        return jnp.sum(jnp.where(lane == at, got[...], 0.0), axis=1, keepdims=True)

    def whole(columns):
        return jnp.sum(columns, axis=0, keepdims=True)

    shift, g = pick(0), [pick(i) for i in range(1, 11)]
    rho, curve = whole(g[0]), whole(g[1])
    alpha = rho / curve
    t = alpha - shift
    rho_next = whole(g[2] - t * (g[3] - t * g[4]))
    square = whole(g[5] - t * (g[6] - t * g[7]))
    cross = whole(g[8] - t * g[9])
    beta = rho_next / rho
    alpha_next = rho_next / (square + beta * cross + beta * beta * curve)
    for p in range(2):
        for x in range(OWN):
            rows = pl.ds(x + 8 * p, 8, stride=16)
            z, q = z0[p, x], source[p, 3 + x, :, :128]
            step = (z - alpha * w0[p, x]) + beta * z
            image = (q - alpha * y0[p, x]) + beta * q
            field[rows, :] = alpha * z + alpha_next * step
            residual[rows, :] = (r0[p, HALO + x, :, :128] - alpha * q) - alpha_next * image


def call(kernel, outs, *args, scratch=(), space=pltpu.VMEM, limit=40):
    return pl.pallas_call(
        kernel,
        out_shape=tuple(jax.ShapeDtypeStruct(s, F32) for s in outs),
        in_specs=[pl.BlockSpec(memory_space=space)] * len(args),
        out_specs=tuple(pl.BlockSpec(memory_space=pltpu.VMEM) for _ in outs),
        scratch_shapes=scratch,
        compiler_params=pltpu.CompilerParams(vmem_limit_bytes=limit * 1024 * 1024),
    )(*args)


def exchange(slots, axis, groups=None):
    return lax.all_to_all(slots, axis, 0, 0, axis_index_groups=groups)


def to_next(array, axis):
    n = lax.axis_size(axis)
    return lax.ppermute(array, axis, [(i, i + 1) for i in range(n - 1)])


def to_previous(array, axis):
    n = lax.axis_size(axis)
    return lax.ppermute(array, axis, [(i + 1, i) for i in range(n - 1)])


def around(array, axis, step):
    n = lax.axis_size(axis)
    return lax.ppermute(array, axis, [(i, (i + step) % n) for i in range(n)])


def on_device(right_side, capacity, phase, mold_flags):
    wide, narrow = lax.axis_size("wide"), lax.axis_size("narrow")
    flat = [v.reshape(128, 128) for v in (right_side, capacity, phase, mold_flags)]
    edge = (2, 2, HALO, 8, 128)
    staged = [pltpu.VMEM((128, 128), v.dtype) for v in flat]
    own, low, high = call(
        prepare_kernel,
        [(2, 2, OWN, 8, 128), edge, edge],
        *flat,
        scratch=staged + [pltpu.SemaphoreType.DMA((4,))],
        space=pl.ANY,
        limit=63,
    )
    below, above = to_next(high, "wide"), to_previous(low, "wide")
    a = jnp.concatenate([below[0], own[0], above[0]], axis=1)
    b = jnp.concatenate([below[1], own[1], above[1]], axis=1)
    from_left, from_right = around(b, "narrow", 1), around(a, "narrow", -1)
    fine, pair = (2, EXT, 8, LANES), (2, 2, 8, LANES)
    r0, d0, i0, one, low, high, send = call(
        functools.partial(down_kernel, wide, narrow),
        [fine, fine, fine, (2, 8, 8, LANES), pair, pair, (wide, 8, 128)],
        a, b, from_left, from_right,
    )
    below, above = to_next(high, "wide"), to_previous(low, "wide")
    first = exchange(send, "wide").reshape(8 * wide, 128)
    block, coarse, line = (2, OWN, 8, 128), (8, 8, LANES), (1, 8, LANES)
    scratch = [pltpu.VMEM((8, wide + 16, 128), F32)]
    z0, source, r1, d1, i1, low, high, send = call(
        functools.partial(turn_kernel, wide, narrow),
        [block, (2, 14, 8, LANES), (6, 8, LANES), coarse, coarse, line, line, (8, 128)],
        first, r0, d0, i0, one, below, above,
        scratch=scratch + [pltpu.VMEM((8, 128), F32)],
    )
    below, above = to_next(high, "wide"), to_previous(low, "wide")
    from_left, from_right = around(send, "narrow", 1), around(send, "narrow", -1)
    (send,) = call(window_kernel, [(wide, 4, 128)], send, from_right, from_left)
    second = exchange(send, "wide").reshape(4 * wide, 128)
    w0, y0, sums = call(
        functools.partial(up_again_kernel, wide, narrow),
        [block, block, (DEEP, 1, 128)],
        second, first, source, r0, d0, i0, below, r1, above, d1, i1, z0,
        scratch=scratch,
    )
    across = wide // DEEP
    far = [[DEEP * y + z for z in range(DEEP)] for y in range(across)]
    near = [
        [(DEEP * y + z) * narrow + n for y in range(across) for n in range(narrow)]
        for z in range(DEEP)
    ]
    parts = exchange(sums, "wide", far)
    sums = jnp.where(jnp.arange(128) == 0, parts[0], jnp.sum(parts, axis=0))
    sums = jnp.broadcast_to(sums[None], (across * narrow,) + sums.shape)
    third = exchange(sums, ("wide", "narrow"), near).reshape(across * narrow, 128)
    field, residual = call(
        last_kernel, [(128, 128), (128, 128)], third, z0, source, w0, y0, r0
    )
    return field.reshape(right_side.shape), residual.reshape(right_side.shape)


def solution(mesh):
    spec = P(None, "wide", "narrow")
    return jax.shard_map(
        on_device, mesh=mesh, in_specs=(spec,) * 4, out_specs=(spec, spec), check_vma=False
    )
```

```python
import functools

import jax
import jax.numpy as jnp
from jax import lax
from jax.experimental import pallas as pl
from jax.experimental.pallas import tpu as pltpu
from jax.sharding import PartitionSpec as P

OMEGA = 0.8
HALO = 5
OWN = 8
EXT = OWN + 2 * HALO
LANES = 256
F32 = jnp.float32
DEEP = 16
SUMS = 44


def iota(shape, dim):
    return lax.broadcasted_iota(jnp.int32, shape, dim)


def roll(value, shift, axis):
    return pltpu.roll(value, shift % value.shape[axis], axis)


def swap(value, width, axis):
    at = iota(value.shape, axis)
    lower = (at // width) % 2 == 0
    return jnp.where(lower, roll(value, -width, axis), roll(value, width, axis))


def along_y(value, width):
    axis = value.ndim - 1
    return roll(value, width, axis) + roll(value, -width, axis)


def apply_fine(even, odd, extra_even, extra_odd):
    e, o = even[1:-1], odd[1:-1]
    k = iota(e.shape, 1)
    by_e = o + jnp.where(k > 0, roll(o, 1, 1), 0.0) + even[2:] + even[:-2] + along_y(e, 1)
    by_o = e + jnp.where(k < 7, roll(e, -1, 1), 0.0) + odd[2:] + odd[:-2] + along_y(o, 1)
    return 6.0 * e - by_e + extra_even * e, 6.0 * o - by_o + extra_odd * o


def restrict_fine(even, odd):
    both = even + odd
    both = jnp.sum(both.reshape((both.shape[0] // 2, 2) + both.shape[1:]), axis=1)
    return 0.125 * (both + swap(both, 1, 2))


def double_rows(value):
    wide = jnp.broadcast_to(value[:, None], (value.shape[0], 2) + value.shape[1:])
    return wide.reshape((2 * value.shape[0],) + value.shape[1:])


def apply_one(value, extra):
    v = value[1:-1]
    k = iota(v.shape, 1)
    beside = jnp.where(k > 0, roll(v, 1, 1), 0.0) + jnp.where(k < 7, roll(v, -1, 1), 0.0)
    beside = beside + value[2:] + value[:-2] + along_y(v, 2)
    return 0.25 * (6.0 * v - beside) + extra * v


def pack_two(value, first_lane):
    pairs = jnp.sum(value.reshape((2, 2) + value.shape[1:]), axis=1)
    pairs = pairs + swap(pairs, 1, 1)
    rows = jnp.where(iota(pairs.shape[1:], 0) % 2 == 0, pairs[0], pairs[1])
    shape = (LANES, 128)
    matrix = jnp.where(iota(shape, 0) // 4 + first_lane == iota(shape, 1), 0.0625, 0.0)
    return jnp.dot(rows, matrix.astype(F32), precision=lax.Precision.HIGHEST)


def pack_rows(value, scratch):
    pairs = jnp.sum(value.reshape((2, 2) + value.shape[1:]), axis=1)
    pairs = pairs + swap(pairs, 1, 1)
    shape = (LANES, 128)
    out = jnp.zeros((8, 128), F32)
    for x in range(2):
        matrix = jnp.where(iota(shape, 0) // 4 + 64 * x == iota(shape, 1), 0.0625, 0.0)
        out = out + jnp.dot(pairs[x], matrix.astype(F32), precision=lax.Precision.HIGHEST)
    scratch[...] = out
    return scratch[pl.ds(0, 4, stride=2), :]


def split_two(ref, wide):
    across = wide // DEEP

    def one(row):
        parts = [ref[pl.ds(8 * y + row, DEEP, stride=8 * across), :] for y in range(across)]
        return jnp.concatenate(parts, axis=0)

    return [[one(2 * z + x) for z in range(4)] for x in range(2)]


def add(terms):
    return functools.reduce(lambda a, b: a + b, terms)


def before(value):
    return jnp.where(iota(value.shape, 0) > 0, roll(value, 1, 0), 0.0)


def after(value):
    last = value.shape[0] - 1
    return jnp.where(iota(value.shape, 0) < last, roll(value, -1, 0), 0.0)


def each(function, *lists):
    return [[function(*(a[x][z] for a in lists)) for z in range(4)] for x in range(2)]


def apply_two(v, d):
    out = [[], []]
    for x in range(2):
        for z in range(4):
            terms = [along_y(v[x][z], 1), v[1 - x][z]]
            terms += [before(v[1][z])] if x == 0 else [after(v[0][z])]
            terms += [v[x][k] for k in (z - 1, z + 1) if 0 <= k < 4]
            out[x].append(0.0625 * (6.0 * v[x][z] - add(terms)) + d[x][z] * v[x][z])
    return out


def restrict_two(v):
    out = []
    for z in range(2):
        total = v[0][2 * z] + v[0][2 * z + 1] + v[1][2 * z] + v[1][2 * z + 1]
        out.append(0.125 * (total + swap(total, 1, 1)))
    return out


def apply_three(v, d):
    out = []
    for z in range(2):
        beside = before(v[z]) + after(v[z]) + v[1 - z] + along_y(v[z], 2)
        out.append(0.015625 * (6.0 * v[z] - beside) + d[z] * v[z])
    return out


def solve_coarse(r2, d2, mine, narrow):
    shape = r2[0][0].shape
    lane = iota(shape, 1) % 64
    column = 32 * mine + jnp.where(lane < 48, lane, lane - 64)
    inside = (column >= 0) & (column < 32 * narrow)
    i2 = each(lambda d: jnp.where(inside, OMEGA / (0.375 + d), 0.0), d2)
    c2 = each(lambda i, r: i * r, i2, r2)
    left = each(lambda r, a: r - a, r2, apply_two(c2, d2))
    r3, d3 = restrict_two(left), restrict_two(d2)
    i3 = [jnp.where(inside, OMEGA / (0.09375 + d), 0.0) for d in d3]
    e3 = [i * r for i, r in zip(i3, r3)]
    for _ in range(3):
        a3 = apply_three(e3, d3)
        e3 = [e + i * (r - a) for e, i, r, a in zip(e3, i3, r3, a3)]
    one = inside[:1]
    for z in range(2):
        weight = jnp.where(one, jnp.sum(d3[z], axis=0, keepdims=True), 1.0)
        line = jnp.where(one, jnp.sum(r3[z], axis=0, keepdims=True) / weight, 0.0)
        e3[z] = e3[z] + line
    e2 = [[c2[x][z] + e3[z // 2] for z in range(4)] for x in range(2)]
    return each(lambda e, i, r, a: e + i * (r - a), e2, i2, r2, apply_two(e2, d2))


def rise(e2, scratch, at, reach, r1, d1, i1):
    wide = e2[0][0].shape[0]
    blank = jnp.zeros((8, 128), F32)
    for x in range(2):
        for z in range(4):
            scratch[2 * z + x, 0:8, :] = blank
            scratch[2 * z + x, 8 + wide : 16 + wide, :] = blank
            scratch[2 * z + x, 8 : 8 + wide, :] = e2[x][z]
    pair = iota((8, 128), 0) // 2
    rows = []
    for row in range(-reach, 2 + reach):
        x, step = row % 2, row // 2
        tile = blank
        for z in range(4):
            line = scratch[2 * z + x, pl.ds(at + (8 + step), 1), :]
            tile = jnp.where(pair == z, jnp.broadcast_to(line, (8, 128)), tile)
        rows.append(tile)
    shape = (128, LANES)
    matrix = jnp.where(iota(shape, 0) == iota(shape, 1) // 4, 1.0, 0.0).astype(F32)
    spread = jnp.dot(jnp.concatenate(rows, 0), matrix, precision=lax.Precision.HIGHEST)
    e1 = i1 * r1 + double_rows(spread.reshape(len(rows), 8, LANES))
    return e1[1:-1] + i1[1:-1] * (r1[1:-1] - apply_one(e1, d1[1:-1]))


def rows_of(pair, first, stop):
    return [pair[p][first:stop] for p in range(2)]


def finish(up, source, extra, inverse):
    e = [inverse[p] * source[p] + up for p in range(2)]
    a = apply_fine(e[0], e[1], extra[0][1:-1], extra[1][1:-1])
    z = [e[p][1:-1] + inverse[p][1:-1] * (source[p][1:-1] - a[p]) for p in range(2)]
    q = apply_fine(z[0], z[1], extra[0][2:-2], extra[1][2:-2])
    return z, q


def descend(source, extra, inverse):
    c = [i * s for i, s in zip(inverse, source)]
    a = apply_fine(c[0], c[1], extra[0][1:-1], extra[1][1:-1])
    left = [source[p][1:-1] - a[p] for p in range(2)]
    return restrict_fine(left[0], left[1])


def leave_one(r1, d1, i1):
    return r1[1:-1] - apply_one(i1 * r1, d1[1:-1])


def invert_one(d1, first, me_w, me_n, wide, narrow):
    lane = iota(d1.shape, 2)
    column = 128 * me_n + jnp.where(lane < 192, lane, lane - 256)
    line = 4 * me_w + first + iota(d1.shape, 0)
    inside = (column >= 0) & (column < 128 * narrow) & (line >= 0) & (line < 4 * wide)
    return jnp.where(inside, OMEGA / (1.5 + d1), 0.0)


def total(a, b):
    return jnp.sum(jnp.sum(a[0] * b[0] + a[1] * b[1], axis=0), keepdims=True)


def place(values, shape, first):
    lane = iota(shape, len(shape) - 1)
    out = jnp.zeros(shape, F32)
    for i, v in enumerate(values):
        out = jnp.where(lane == first + i, v, out)
    return out


def prepare_kernel(right_in, capacity_in, phase_in, flags_in, own, low, high, right, capacity, phase, flags, done):
    pairs = ((right_in, right), (capacity_in, capacity), (phase_in, phase), (flags_in, flags))
    copies = [pltpu.make_async_copy(a, b, done.at[i]) for i, (a, b) in enumerate(pairs)]
    for copy in copies:
        copy.start()
    for copy in copies:
        copy.wait()
    half = iota((8, 128), 1) < 64
    for p in range(2):
        for x in range(OWN):
            rows = pl.ds(x + 8 * p, 8, stride=16)
            r = right[rows, :]
            weight = jnp.where(phase[rows, :] == 1, 4.0, 1.0)
            d = 0.05 * capacity[rows, :] * weight + 0.5 * flags[rows, :].astype(F32)
            first = jnp.where(half, r, roll(d, 64, 1))
            second = jnp.where(half, roll(r, 64, 1), d)
            for side, value in ((0, first), (1, second)):
                own[side, p, x] = value
                if x < HALO:
                    low[side, p, x] = value
                if x >= OWN - HALO:
                    high[side, p, x - (OWN - HALO)] = value


def down_kernel(wide, narrow, a, b, from_left, from_right, r0, d0, i0, one, low, high, send):
    me_w, me_n = lax.axis_index("wide"), lax.axis_index("narrow")
    shape = (EXT, 8, 128)
    half = iota(shape, 2) < 64
    fine = (EXT, 8, LANES)
    lane, row = iota(fine, 2), iota(fine, 0)
    column = 128 * me_n + jnp.where(lane < 192, lane, lane - 256)
    line = 8 * me_w - HALO + row
    inside = (column >= 0) & (column < 128 * narrow) & (line >= 0) & (line < 8 * wide)
    source, extra, inverse = [], [], []
    for p in range(2):
        fa, fb, fl, fr = a[p], b[p], from_left[p], from_right[p]
        own_r = jnp.where(half, fa, roll(fb, 64, 2))
        own_d = jnp.where(half, roll(fa, 64, 2), fb)
        far_r = jnp.where(half, fr, roll(fl, 64, 2))
        far_d = jnp.where(half, roll(fr, 64, 2), fl)
        source.append(jnp.concatenate([own_r, far_r], axis=2))
        extra.append(jnp.concatenate([own_d, far_d], axis=2))
        inverse.append(jnp.where(inside, OMEGA / (6.0 + extra[p]), 0.0))
        r0[p] = source[p]
        d0[p] = extra[p]
        i0[p] = inverse[p]
    vr1 = descend(source, extra, inverse)
    vd1 = restrict_fine(extra[0][1:17], extra[1][1:17])
    vi1 = invert_one(vd1, -2, me_w, me_n, wide, narrow)
    for side, value in ((0, vr1), (1, vd1)):
        one[side] = value
        high[side] = value[2:4]
        low[side] = value[4:6]
    left = leave_one(vr1[1:7], vd1[1:7], vi1[1:7])
    tile = pack_two(left, 0) + pack_two(vd1[2:6], 64)
    send[...] = jnp.broadcast_to(tile, send.shape)


def both_halves(tile):
    half = iota(tile.shape, 1) < 64
    other = roll(tile, 64, 1)
    return jnp.where(half, tile, other), jnp.where(half, other, tile)


def turn_kernel(wide, narrow, got, r0, d0, i0, one, below, above, z, q, r1, d1, i1, low, high, send, scratch, small):
    me_w, me_n = lax.axis_index("wide"), lax.axis_index("narrow")
    tiles = split_two(got, wide)
    r2 = each(lambda t: both_halves(t)[0], tiles)
    d2 = each(lambda t: both_halves(t)[1], tiles)
    e2 = solve_coarse(r2, d2, me_n, narrow)
    vr1 = jnp.concatenate([below[0], one[0], above[0]], axis=0)
    vd1 = jnp.concatenate([below[1], one[1], above[1]], axis=0)
    vi1 = invert_one(vd1, -4, me_w, me_n, wide, narrow)
    e1 = rise(e2, scratch, me_w, 2, vr1, vd1, vi1)
    up = double_rows(e1)[1:-1]
    source, extra, inverse = (rows_of(ref, 0, EXT) for ref in (r0, d0, i0))
    vz, vq = finish(up, source, extra, inverse)
    own_z = [v[4:12, :, :128] for v in vz]
    own_q = [v[3:11, :, :128] for v in vq]
    own_r = [v[HALO : HALO + OWN, :, :128] for v in source]
    for p in range(2):
        z[p] = own_z[p]
        q[p] = vq[p]
    below_two = descend(vq, rows_of(d0, 2, 16), rows_of(i0, 2, 16))
    r1[...] = below_two
    d1[...] = vd1[2:10]
    i1[...] = vi1[2:10]
    low[...] = below_two[2:3]
    high[...] = below_two[3:4]
    rows = pack_rows(leave_one(below_two, vd1[3:9], vi1[3:9]), small)
    sums = place([total(own_r, own_z), total(own_z, own_q)], rows.shape, SUMS)
    lane = iota(rows.shape, 1)
    send[0:4, :] = jnp.where((lane == SUMS) | (lane == SUMS + 1), sums, rows)
    send[4:8, :] = jnp.zeros(rows.shape, F32)


def window_kernel(own, right, left, send):
    lane = iota(own.shape, 1)
    cell = lane % 64
    halo = jnp.where(cell < 48, roll(right[...], 32, 1), roll(left[...], 32, 1))
    keep = (cell < 32) | (lane == SUMS) | (lane == SUMS + 1)
    send[...] = jnp.broadcast_to(jnp.where(keep, own[...], halo)[0:4], send.shape)


def split_rows(ref, wide):
    sides = [[], []]
    for z in range(4):
        for side, value in zip(sides, both_halves(ref[pl.ds(z, wide, stride=4), :])):
            side.append(value)
    return sides


def up_again_kernel(wide, narrow, got, first, source, r0, d0, i0, below, r1, above, d1, i1, z0, w0, y0, sums, scratch):
    me_w, me_n = lax.axis_index("wide"), lax.axis_index("narrow")
    r2 = split_rows(got, wide)
    d2 = each(lambda t: both_halves(t)[1], split_two(first, wide))
    e2 = solve_coarse(r2, d2, me_n, narrow)
    vr1 = jnp.concatenate([below[...], r1[...], above[...]], axis=0)
    e1 = rise(e2, scratch, me_w, 1, vr1, d1[...], i1[...])
    extra, inverse = rows_of(d0, 3, 15), rows_of(i0, 3, 15)
    vw, vy = finish(double_rows(e1), rows_of(source, 1, 13), extra, inverse)
    w = [v[1:-1, :, :128] for v in vw]
    y = [v[:, :, :128] for v in vy]
    scalars = jnp.sum(got[pl.ds(0, wide, stride=4), :], axis=0, keepdims=True)
    lane = iota((1, 128), 1)
    rho = jnp.sum(jnp.where(lane == SUMS, scalars, 0.0), keepdims=True)
    curve = jnp.sum(jnp.where(lane == SUMS + 1, scalars, 0.0), keepdims=True)
    ratio = rho / jnp.where(curve > 0.0, curve, 1.0)
    shift = jnp.where(curve > 0.0, jnp.minimum(jnp.maximum(ratio, 0.0), 8.0), 0.0)
    s = shift.reshape(1, 1, 1)
    z = [z0[p] for p in range(2)]
    q = [source[p, 3:11, :, :128] for p in range(2)]
    r = [r0[p, HALO : HALO + OWN, :, :128] for p in range(2)]
    for p in range(2):
        w0[p] = w[p]
        y0[p] = y[p]
    rs = [r[p] - s * q[p] for p in range(2)]
    zs = [z[p] - s * w[p] for p in range(2)]
    ys = [q[p] - s * y[p] for p in range(2)]
    values = [
        shift,
        total(r, z),
        total(z, q),
        total(rs, zs),
        total(rs, w) + total(q, zs),
        total(q, w),
        total(zs, ys),
        total(w, ys) + total(zs, y),
        total(w, y),
        total(zs, q) + total(z, ys),
        total(w, q) + total(z, y),
    ]
    sums[...] = jnp.broadcast_to(place(values, (1, 128), 0), sums.shape)


def last_kernel(got, z0, source, w0, y0, r0, field, residual):
    lane = iota(got.shape, 1)

    def pick(at):
        return jnp.sum(jnp.where(lane == at, got[...], 0.0), axis=1, keepdims=True)

    def whole(columns):
        return jnp.sum(columns, axis=0, keepdims=True)

    shift, g = pick(0), [pick(i) for i in range(1, 11)]
    rho, curve = whole(g[0]), whole(g[1])
    alpha = rho / curve
    t = alpha - shift
    rho_next = whole(g[2] - t * (g[3] - t * g[4]))
    square = whole(g[5] - t * (g[6] - t * g[7]))
    cross = whole(g[8] - t * g[9])
    beta = rho_next / rho
    alpha_next = rho_next / (square + beta * cross + beta * beta * curve)
    for p in range(2):
        for x in range(OWN):
            rows = pl.ds(x + 8 * p, 8, stride=16)
            z, q = z0[p, x], source[p, 3 + x, :, :128]
            step = (z - alpha * w0[p, x]) + beta * z
            image = (q - alpha * y0[p, x]) + beta * q
            field[rows, :] = alpha * z + alpha_next * step
            residual[rows, :] = (r0[p, HALO + x, :, :128] - alpha * q) - alpha_next * image


def call(kernel, outs, *args, scratch=(), space=pltpu.VMEM, limit=40):
    return pl.pallas_call(
        kernel,
        out_shape=tuple(jax.ShapeDtypeStruct(s, F32) for s in outs),
        in_specs=[pl.BlockSpec(memory_space=space)] * len(args),
        out_specs=tuple(pl.BlockSpec(memory_space=pltpu.VMEM) for _ in outs),
        scratch_shapes=scratch,
        compiler_params=pltpu.CompilerParams(vmem_limit_bytes=limit * 1024 * 1024),
    )(*args)


def exchange(slots, axis, groups=None):
    return lax.all_to_all(slots, axis, 0, 0, axis_index_groups=groups)


def to_next(array, axis):
    n = lax.axis_size(axis)
    return lax.ppermute(array, axis, [(i, i + 1) for i in range(n - 1)])


def to_previous(array, axis):
    n = lax.axis_size(axis)
    return lax.ppermute(array, axis, [(i + 1, i) for i in range(n - 1)])


def around(array, axis, step):
    n = lax.axis_size(axis)
    return lax.ppermute(array, axis, [(i, (i + step) % n) for i in range(n)])


def on_device(right_side, capacity, phase, mold_flags):
    wide, narrow = lax.axis_size("wide"), lax.axis_size("narrow")
    across = wide // DEEP
    far = [[DEEP * y + z for z in range(DEEP)] for y in range(across)]
    near = [
        [(DEEP * y + z) * narrow + n for y in range(across) for n in range(narrow)]
        for z in range(DEEP)
    ]
    side = [[DEEP * y + z for y in range(across)] for z in range(DEEP)]
    flat = [v.reshape(128, 128) for v in (right_side, capacity, phase, mold_flags)]
    edge = (2, 2, HALO, 8, 128)
    staged = [pltpu.VMEM((128, 128), v.dtype) for v in flat]
    own, low, high = call(
        prepare_kernel,
        [(2, 2, OWN, 8, 128), edge, edge],
        *flat,
        scratch=staged + [pltpu.SemaphoreType.DMA((4,))],
        space=pl.ANY,
        limit=63,
    )
    below, above = to_next(high, "wide"), to_previous(low, "wide")
    a = jnp.concatenate([below[0], own[0], above[0]], axis=1)
    b = jnp.concatenate([below[1], own[1], above[1]], axis=1)
    from_left, from_right = around(b, "narrow", 1), around(a, "narrow", -1)
    fine, pair = (2, EXT, 8, LANES), (2, 2, 8, LANES)
    r0, d0, i0, one, low, high, send = call(
        functools.partial(down_kernel, wide, narrow),
        [fine, fine, fine, (2, 8, 8, LANES), pair, pair, (across, 8, 128)],
        a, b, from_left, from_right,
    )
    below, above = to_next(high, "wide"), to_previous(low, "wide")
    send = exchange(send, "wide", side).reshape(8 * across, 128)
    send = jnp.broadcast_to(send[None], (DEEP,) + send.shape)
    first = exchange(send, "wide", far).reshape(8 * wide, 128)
    block, coarse, line = (2, OWN, 8, 128), (8, 8, LANES), (1, 8, LANES)
    scratch = [pltpu.VMEM((8, wide + 16, 128), F32)]
    z0, source, r1, d1, i1, low, high, send = call(
        functools.partial(turn_kernel, wide, narrow),
        [block, (2, 14, 8, LANES), (6, 8, LANES), coarse, coarse, line, line, (8, 128)],
        first, r0, d0, i0, one, below, above,
        scratch=scratch + [pltpu.VMEM((8, 128), F32)],
    )
    below, above = to_next(high, "wide"), to_previous(low, "wide")
    from_left, from_right = around(send, "narrow", 1), around(send, "narrow", -1)
    (send,) = call(window_kernel, [(wide, 4, 128)], send, from_right, from_left)
    second = exchange(send, "wide").reshape(4 * wide, 128)
    w0, y0, sums = call(
        functools.partial(up_again_kernel, wide, narrow),
        [block, block, (DEEP, 1, 128)],
        second, first, source, r0, d0, i0, below, r1, above, d1, i1, z0,
        scratch=scratch,
    )
    parts = exchange(sums, "wide", far)
    sums = jnp.where(jnp.arange(128) == 0, parts[0], jnp.sum(parts, axis=0))
    sums = jnp.broadcast_to(sums[None], (across * narrow,) + sums.shape)
    third = exchange(sums, ("wide", "narrow"), near).reshape(across * narrow, 128)
    field, residual = call(
        last_kernel, [(128, 128), (128, 128)], third, z0, source, w0, y0, r0
    )
    return field.reshape(right_side.shape), residual.reshape(right_side.shape)


def solution(mesh):
    spec = P(None, "wide", "narrow")
    return jax.shard_map(
        on_device, mesh=mesh, in_specs=(spec,) * 4, out_specs=(spec, spec), check_vma=False
    )
```

```python
import functools

import jax
import jax.numpy as jnp
from jax import lax
from jax.experimental import pallas as pl
from jax.experimental.pallas import tpu as pltpu
from jax.sharding import PartitionSpec as P

OMEGA = 0.8
HALO = 7
OWN = 8
EXT = OWN + 2 * HALO
LANES = 256
F32 = jnp.float32
DEEP = 16
SUMS = 44


def iota(shape, dim):
    return lax.broadcasted_iota(jnp.int32, shape, dim)


def roll(value, shift, axis):
    return pltpu.roll(value, shift % value.shape[axis], axis)


def swap(value, width, axis):
    at = iota(value.shape, axis)
    lower = (at // width) % 2 == 0
    return jnp.where(lower, roll(value, -width, axis), roll(value, width, axis))


def along_y(value, width):
    axis = value.ndim - 1
    return roll(value, width, axis) + roll(value, -width, axis)


def apply_fine(even, odd, extra_even, extra_odd):
    e, o = even[1:-1], odd[1:-1]
    k = iota(e.shape, 1)
    by_e = o + jnp.where(k > 0, roll(o, 1, 1), 0.0) + even[2:] + even[:-2] + along_y(e, 1)
    by_o = e + jnp.where(k < 7, roll(e, -1, 1), 0.0) + odd[2:] + odd[:-2] + along_y(o, 1)
    return 6.0 * e - by_e + extra_even * e, 6.0 * o - by_o + extra_odd * o


def restrict_fine(even, odd):
    both = even + odd
    both = jnp.sum(both.reshape((both.shape[0] // 2, 2) + both.shape[1:]), axis=1)
    return 0.125 * (both + swap(both, 1, 2))


def double_rows(value):
    wide = jnp.broadcast_to(value[:, None], (value.shape[0], 2) + value.shape[1:])
    return wide.reshape((2 * value.shape[0],) + value.shape[1:])


def apply_one(value, extra):
    v = value[1:-1]
    k = iota(v.shape, 1)
    beside = jnp.where(k > 0, roll(v, 1, 1), 0.0) + jnp.where(k < 7, roll(v, -1, 1), 0.0)
    beside = beside + value[2:] + value[:-2] + along_y(v, 2)
    return 0.25 * (6.0 * v - beside) + extra * v


def pack_two(value, first_lane):
    pairs = jnp.sum(value.reshape((2, 2) + value.shape[1:]), axis=1)
    pairs = pairs + swap(pairs, 1, 1)
    rows = jnp.where(iota(pairs.shape[1:], 0) % 2 == 0, pairs[0], pairs[1])
    shape = (LANES, 128)
    matrix = jnp.where(iota(shape, 0) // 4 + first_lane == iota(shape, 1), 0.0625, 0.0)
    return jnp.dot(rows, matrix.astype(F32), precision=lax.Precision.HIGHEST)


def pack_rows(value, scratch):
    pairs = jnp.sum(value.reshape((2, 2) + value.shape[1:]), axis=1)
    pairs = pairs + swap(pairs, 1, 1)
    shape = (LANES, 128)
    out = jnp.zeros((8, 128), F32)
    for x in range(2):
        matrix = jnp.where(iota(shape, 0) // 4 + 64 * x == iota(shape, 1), 0.0625, 0.0)
        out = out + jnp.dot(pairs[x], matrix.astype(F32), precision=lax.Precision.HIGHEST)
    scratch[...] = out
    return scratch[pl.ds(0, 4, stride=2), :]


def split_two(ref, wide):
    return [[ref[pl.ds(2 * z + x, wide, stride=8), :] for z in range(4)] for x in range(2)]


def add(terms):
    return functools.reduce(lambda a, b: a + b, terms)


def before(value):
    return jnp.where(iota(value.shape, 0) > 0, roll(value, 1, 0), 0.0)


def after(value):
    last = value.shape[0] - 1
    return jnp.where(iota(value.shape, 0) < last, roll(value, -1, 0), 0.0)


def each(function, *lists):
    return [[function(*(a[x][z] for a in lists)) for z in range(4)] for x in range(2)]


def apply_two(v, d):
    out = [[], []]
    for x in range(2):
        for z in range(4):
            terms = [along_y(v[x][z], 1), v[1 - x][z]]
            terms += [before(v[1][z])] if x == 0 else [after(v[0][z])]
            terms += [v[x][k] for k in (z - 1, z + 1) if 0 <= k < 4]
            out[x].append(0.0625 * (6.0 * v[x][z] - add(terms)) + d[x][z] * v[x][z])
    return out


def restrict_two(v):
    out = []
    for z in range(2):
        total = v[0][2 * z] + v[0][2 * z + 1] + v[1][2 * z] + v[1][2 * z + 1]
        out.append(0.125 * (total + swap(total, 1, 1)))
    return out


def apply_three(v, d):
    out = []
    for z in range(2):
        beside = before(v[z]) + after(v[z]) + v[1 - z] + along_y(v[z], 2)
        out.append(0.015625 * (6.0 * v[z] - beside) + d[z] * v[z])
    return out


def solve_coarse(r2, d2, mine, narrow):
    shape = r2[0][0].shape
    lane = iota(shape, 1) % 64
    column = 32 * mine + jnp.where(lane < 48, lane, lane - 64)
    inside = (column >= 0) & (column < 32 * narrow)
    i2 = each(lambda d: jnp.where(inside, OMEGA / (0.375 + d), 0.0), d2)
    c2 = each(lambda i, r: i * r, i2, r2)
    left = each(lambda r, a: r - a, r2, apply_two(c2, d2))
    r3, d3 = restrict_two(left), restrict_two(d2)
    i3 = [jnp.where(inside, OMEGA / (0.09375 + d), 0.0) for d in d3]
    e3 = [i * r for i, r in zip(i3, r3)]
    for _ in range(3):
        a3 = apply_three(e3, d3)
        e3 = [e + i * (r - a) for e, i, r, a in zip(e3, i3, r3, a3)]
    one = inside[:1]
    for z in range(2):
        weight = jnp.where(one, jnp.sum(d3[z], axis=0, keepdims=True), 1.0)
        line = jnp.where(one, jnp.sum(r3[z], axis=0, keepdims=True) / weight, 0.0)
        e3[z] = e3[z] + line
    e2 = [[c2[x][z] + e3[z // 2] for z in range(4)] for x in range(2)]
    return each(lambda e, i, r, a: e + i * (r - a), e2, i2, r2, apply_two(e2, d2))


def rise(e2, scratch, at, reach, r1, d1, i1):
    wide = e2[0][0].shape[0]
    blank = jnp.zeros((8, 128), F32)
    for x in range(2):
        for z in range(4):
            scratch[2 * z + x, 0:8, :] = blank
            scratch[2 * z + x, 8 + wide : 16 + wide, :] = blank
            scratch[2 * z + x, 8 : 8 + wide, :] = e2[x][z]
    pair = iota((8, 128), 0) // 2
    rows = []
    for row in range(-reach, 2 + reach):
        x, step = row % 2, row // 2
        tile = blank
        for z in range(4):
            line = scratch[2 * z + x, pl.ds(at + (8 + step), 1), :]
            tile = jnp.where(pair == z, jnp.broadcast_to(line, (8, 128)), tile)
        rows.append(tile)
    shape = (128, LANES)
    matrix = jnp.where(iota(shape, 0) == iota(shape, 1) // 4, 1.0, 0.0).astype(F32)
    spread = jnp.dot(jnp.concatenate(rows, 0), matrix, precision=lax.Precision.HIGHEST)
    up = double_rows(spread.reshape(len(rows), 8, LANES))
    trim = (up.shape[0] - r1.shape[0]) // 2
    e1 = i1 * r1 + up[trim : trim + r1.shape[0]]
    return e1[1:-1] + i1[1:-1] * (r1[1:-1] - apply_one(e1, d1[1:-1]))


def rows_of(pair, first, stop):
    return [pair[p][first:stop] for p in range(2)]


def finish(up, source, extra, inverse):
    e = [inverse[p] * source[p] + up for p in range(2)]
    a = apply_fine(e[0], e[1], extra[0][1:-1], extra[1][1:-1])
    z = [e[p][1:-1] + inverse[p][1:-1] * (source[p][1:-1] - a[p]) for p in range(2)]
    q = apply_fine(z[0], z[1], extra[0][2:-2], extra[1][2:-2])
    return z, q


def descend(source, extra, inverse):
    c = [i * s for i, s in zip(inverse, source)]
    a = apply_fine(c[0], c[1], extra[0][1:-1], extra[1][1:-1])
    left = [source[p][1:-1] - a[p] for p in range(2)]
    return restrict_fine(left[0], left[1])


def leave_one(r1, d1, i1):
    return r1[1:-1] - apply_one(i1 * r1, d1[1:-1])


def invert_one(d1, first, me_w, me_n, wide, narrow):
    lane = iota(d1.shape, 2)
    column = 128 * me_n + jnp.where(lane < 192, lane, lane - 256)
    line = 4 * me_w + first + iota(d1.shape, 0)
    inside = (column >= 0) & (column < 128 * narrow) & (line >= 0) & (line < 4 * wide)
    return jnp.where(inside, OMEGA / (1.5 + d1), 0.0)


def total(a, b):
    return jnp.sum(jnp.sum(a[0] * b[0] + a[1] * b[1], axis=0), keepdims=True)


def place(values, shape, first):
    lane = iota(shape, len(shape) - 1)
    out = jnp.zeros(shape, F32)
    for i, v in enumerate(values):
        out = jnp.where(lane == first + i, v, out)
    return out


def prepare_kernel(right_in, capacity_in, phase_in, flags_in, own, low, high, right, capacity, phase, flags, done):
    pairs = ((right_in, right), (capacity_in, capacity), (phase_in, phase), (flags_in, flags))
    copies = [pltpu.make_async_copy(a, b, done.at[i]) for i, (a, b) in enumerate(pairs)]
    for copy in copies:
        copy.start()
    for copy in copies:
        copy.wait()
    half = iota((8, 128), 1) < 64
    for p in range(2):
        for x in range(OWN):
            rows = pl.ds(x + 8 * p, 8, stride=16)
            r = right[rows, :]
            weight = jnp.where(phase[rows, :] == 1, 4.0, 1.0)
            d = 0.05 * capacity[rows, :] * weight + 0.5 * flags[rows, :].astype(F32)
            first = jnp.where(half, r, roll(d, 64, 1))
            second = jnp.where(half, roll(r, 64, 1), d)
            for side, value in ((0, first), (1, second)):
                own[side, p, x] = value
                if x < HALO:
                    low[side, p, x] = value
                if x >= OWN - HALO:
                    high[side, p, x - (OWN - HALO)] = value


def down_kernel(wide, narrow, a, b, from_left, from_right, r0, d0, i0, one, low, high, send):
    me_w, me_n = lax.axis_index("wide"), lax.axis_index("narrow")
    shape = (EXT, 8, 128)
    half = iota(shape, 2) < 64
    fine = (EXT, 8, LANES)
    lane, row = iota(fine, 2), iota(fine, 0)
    column = 128 * me_n + jnp.where(lane < 192, lane, lane - 256)
    line = 8 * me_w - HALO + row
    inside = (column >= 0) & (column < 128 * narrow) & (line >= 0) & (line < 8 * wide)
    source, extra, inverse = [], [], []
    for p in range(2):
        fa, fb, fl, fr = a[p], b[p], from_left[p], from_right[p]
        own_r = jnp.where(half, fa, roll(fb, 64, 2))
        own_d = jnp.where(half, roll(fa, 64, 2), fb)
        far_r = jnp.where(half, fr, roll(fl, 64, 2))
        far_d = jnp.where(half, roll(fr, 64, 2), fl)
        source.append(jnp.concatenate([own_r, far_r], axis=2))
        extra.append(jnp.concatenate([own_d, far_d], axis=2))
        inverse.append(jnp.where(inside, OMEGA / (6.0 + extra[p]), 0.0))
        r0[p] = source[p]
        d0[p] = extra[p]
        i0[p] = inverse[p]
    vr1 = descend(source, extra, inverse)
    vd1 = restrict_fine(extra[0][1:-1], extra[1][1:-1])
    vi1 = invert_one(vd1, -3, me_w, me_n, wide, narrow)
    for side, value in ((0, vr1), (1, vd1)):
        one[side] = value
        high[side] = value[2:4]
        low[side] = value[6:8]
    left = leave_one(vr1[2:8], vd1[2:8], vi1[2:8])
    tile = pack_two(left, 0) + pack_two(vd1[3:7], 64)
    send[...] = jnp.broadcast_to(tile, send.shape)


def both_halves(tile):
    half = iota(tile.shape, 1) < 64
    other = roll(tile, 64, 1)
    return jnp.where(half, tile, other), jnp.where(half, other, tile)


def turn_kernel(wide, narrow, got, r0, d0, i0, one, below, above, z, q, r1, d1, i1, send, scratch, small):
    me_w, me_n = lax.axis_index("wide"), lax.axis_index("narrow")
    tiles = split_two(got, wide)
    r2 = each(lambda t: both_halves(t)[0], tiles)
    d2 = each(lambda t: both_halves(t)[1], tiles)
    e2 = solve_coarse(r2, d2, me_n, narrow)
    vr1 = jnp.concatenate([below[0], one[0], above[0]], axis=0)
    vd1 = jnp.concatenate([below[1], one[1], above[1]], axis=0)
    vi1 = invert_one(vd1, -5, me_w, me_n, wide, narrow)
    e1 = rise(e2, scratch, me_w, 3, vr1, vd1, vi1)
    up = double_rows(e1)[1:-1]
    source, extra, inverse = (rows_of(ref, 0, EXT) for ref in (r0, d0, i0))
    vz, vq = finish(up, source, extra, inverse)
    own_z = [v[6:14, :, :128] for v in vz]
    own_q = [v[5:13, :, :128] for v in vq]
    own_r = [v[HALO : HALO + OWN, :, :128] for v in source]
    for p in range(2):
        z[p] = own_z[p]
        q[p] = vq[p]
    below_two = descend(vq, rows_of(d0, 2, 20), rows_of(i0, 2, 20))
    r1[...] = below_two
    d1[...] = vd1[3:11]
    i1[...] = vi1[3:11]
    rows = pack_rows(leave_one(below_two[1:7], vd1[4:10], vi1[4:10]), small)
    sums = place([total(own_r, own_z), total(own_z, own_q)], rows.shape, SUMS)
    lane = iota(rows.shape, 1)
    send[0:4, :] = jnp.where((lane == SUMS) | (lane == SUMS + 1), sums, rows)
    send[4:8, :] = jnp.zeros(rows.shape, F32)


def window_kernel(own, right, left, send):
    lane = iota(own.shape, 1)
    cell = lane % 64
    halo = jnp.where(cell < 48, roll(right[...], 32, 1), roll(left[...], 32, 1))
    keep = (cell < 32) | (lane == SUMS) | (lane == SUMS + 1)
    send[...] = jnp.broadcast_to(jnp.where(keep, own[...], halo)[0:4], send.shape)


def split_rows(ref, wide):
    sides = [[], []]
    for z in range(4):
        for side, value in zip(sides, both_halves(ref[pl.ds(z, wide, stride=4), :])):
            side.append(value)
    return sides


def up_again_kernel(wide, narrow, got, first, source, r0, d0, i0, r1, d1, i1, z0, w0, y0, sums, scratch):
    me_w, me_n = lax.axis_index("wide"), lax.axis_index("narrow")
    r2 = split_rows(got, wide)
    d2 = each(lambda t: both_halves(t)[1], split_two(first, wide))
    e2 = solve_coarse(r2, d2, me_n, narrow)
    e1 = rise(e2, scratch, me_w, 1, r1[...], d1[...], i1[...])
    extra, inverse = rows_of(d0, 5, 17), rows_of(i0, 5, 17)
    vw, vy = finish(double_rows(e1), rows_of(source, 3, 15), extra, inverse)
    w = [v[1:-1, :, :128] for v in vw]
    y = [v[:, :, :128] for v in vy]
    scalars = jnp.sum(got[pl.ds(0, wide, stride=4), :], axis=0, keepdims=True)
    lane = iota((1, 128), 1)
    rho = jnp.sum(jnp.where(lane == SUMS, scalars, 0.0), keepdims=True)
    curve = jnp.sum(jnp.where(lane == SUMS + 1, scalars, 0.0), keepdims=True)
    ratio = rho / jnp.where(curve > 0.0, curve, 1.0)
    shift = jnp.where(curve > 0.0, jnp.minimum(jnp.maximum(ratio, 0.0), 8.0), 0.0)
    s = shift.reshape(1, 1, 1)
    z = [z0[p] for p in range(2)]
    q = [source[p, 5:13, :, :128] for p in range(2)]
    r = [r0[p, HALO : HALO + OWN, :, :128] for p in range(2)]
    for p in range(2):
        w0[p] = w[p]
        y0[p] = y[p]
    rs = [r[p] - s * q[p] for p in range(2)]
    zs = [z[p] - s * w[p] for p in range(2)]
    ys = [q[p] - s * y[p] for p in range(2)]
    values = [
        shift,
        total(r, z),
        total(z, q),
        total(rs, zs),
        total(rs, w) + total(q, zs),
        total(q, w),
        total(zs, ys),
        total(w, ys) + total(zs, y),
        total(w, y),
        total(zs, q) + total(z, ys),
        total(w, q) + total(z, y),
    ]
    sums[...] = jnp.broadcast_to(place(values, (1, 128), 0), sums.shape)


def last_kernel(got, z0, source, w0, y0, r0, field, residual):
    lane = iota(got.shape, 1)

    def pick(at):
        return jnp.sum(jnp.where(lane == at, got[...], 0.0), axis=1, keepdims=True)

    def whole(columns):
        return jnp.sum(columns, axis=0, keepdims=True)

    shift, g = pick(0), [pick(i) for i in range(1, 11)]
    rho, curve = whole(g[0]), whole(g[1])
    alpha = rho / curve
    t = alpha - shift
    rho_next = whole(g[2] - t * (g[3] - t * g[4]))
    square = whole(g[5] - t * (g[6] - t * g[7]))
    cross = whole(g[8] - t * g[9])
    beta = rho_next / rho
    alpha_next = rho_next / (square + beta * cross + beta * beta * curve)
    for p in range(2):
        for x in range(OWN):
            rows = pl.ds(x + 8 * p, 8, stride=16)
            z, q = z0[p, x], source[p, 5 + x, :, :128]
            step = (z - alpha * w0[p, x]) + beta * z
            image = (q - alpha * y0[p, x]) + beta * q
            field[rows, :] = alpha * z + alpha_next * step
            residual[rows, :] = (r0[p, HALO + x, :, :128] - alpha * q) - alpha_next * image


def call(kernel, outs, *args, scratch=(), space=pltpu.VMEM, limit=40):
    return pl.pallas_call(
        kernel,
        out_shape=tuple(jax.ShapeDtypeStruct(s, F32) for s in outs),
        in_specs=[pl.BlockSpec(memory_space=space)] * len(args),
        out_specs=tuple(pl.BlockSpec(memory_space=pltpu.VMEM) for _ in outs),
        scratch_shapes=scratch,
        compiler_params=pltpu.CompilerParams(vmem_limit_bytes=limit * 1024 * 1024),
    )(*args)


def exchange(slots, axis, groups=None):
    return lax.all_to_all(slots, axis, 0, 0, axis_index_groups=groups)


def to_next(array, axis):
    n = lax.axis_size(axis)
    return lax.ppermute(array, axis, [(i, i + 1) for i in range(n - 1)])


def to_previous(array, axis):
    n = lax.axis_size(axis)
    return lax.ppermute(array, axis, [(i + 1, i) for i in range(n - 1)])


def around(array, axis, step):
    n = lax.axis_size(axis)
    return lax.ppermute(array, axis, [(i, (i + step) % n) for i in range(n)])


def on_device(right_side, capacity, phase, mold_flags):
    wide, narrow = lax.axis_size("wide"), lax.axis_size("narrow")
    flat = [v.reshape(128, 128) for v in (right_side, capacity, phase, mold_flags)]
    edge = (2, 2, HALO, 8, 128)
    staged = [pltpu.VMEM((128, 128), v.dtype) for v in flat]
    own, low, high = call(
        prepare_kernel,
        [(2, 2, OWN, 8, 128), edge, edge],
        *flat,
        scratch=staged + [pltpu.SemaphoreType.DMA((4,))],
        space=pl.ANY,
        limit=63,
    )
    below, above = to_next(high, "wide"), to_previous(low, "wide")
    a = jnp.concatenate([below[0], own[0], above[0]], axis=1)
    b = jnp.concatenate([below[1], own[1], above[1]], axis=1)
    from_left, from_right = around(b, "narrow", 1), around(a, "narrow", -1)
    fine, pair = (2, EXT, 8, LANES), (2, 2, 8, LANES)
    r0, d0, i0, one, low, high, send = call(
        functools.partial(down_kernel, wide, narrow),
        [fine, fine, fine, (2, 10, 8, LANES), pair, pair, (wide, 8, 128)],
        a, b, from_left, from_right,
    )
    below, above = to_next(high, "wide"), to_previous(low, "wide")
    first = exchange(send, "wide").reshape(8 * wide, 128)
    block, coarse = (2, OWN, 8, 128), (8, 8, LANES)
    scratch = [pltpu.VMEM((8, wide + 16, 128), F32)]
    z0, source, r1, d1, i1, send = call(
        functools.partial(turn_kernel, wide, narrow),
        [block, (2, 18, 8, LANES), coarse, coarse, coarse, (8, 128)],
        first, r0, d0, i0, one, below, above,
        scratch=scratch + [pltpu.VMEM((8, 128), F32)],
    )
    from_left, from_right = around(send, "narrow", 1), around(send, "narrow", -1)
    (send,) = call(window_kernel, [(wide, 4, 128)], send, from_right, from_left)
    second = exchange(send, "wide").reshape(4 * wide, 128)
    w0, y0, sums = call(
        functools.partial(up_again_kernel, wide, narrow),
        [block, block, (DEEP, 1, 128)],
        second, first, source, r0, d0, i0, r1, d1, i1, z0,
        scratch=scratch,
    )
    across = wide // DEEP
    far = [[DEEP * y + z for z in range(DEEP)] for y in range(across)]
    near = [
        [(DEEP * y + z) * narrow + n for y in range(across) for n in range(narrow)]
        for z in range(DEEP)
    ]
    parts = exchange(sums, "wide", far)
    sums = jnp.where(jnp.arange(128) == 0, parts[0], jnp.sum(parts, axis=0))
    sums = jnp.broadcast_to(sums[None], (across * narrow,) + sums.shape)
    third = exchange(sums, ("wide", "narrow"), near).reshape(across * narrow, 128)
    field, residual = call(
        last_kernel, [(128, 128), (128, 128)], third, z0, source, w0, y0, r0
    )
    return field.reshape(right_side.shape), residual.reshape(right_side.shape)


def solution(mesh):
    spec = P(None, "wide", "narrow")
    return jax.shard_map(
        on_device, mesh=mesh, in_specs=(spec,) * 4, out_specs=(spec, spec), check_vma=False
    )
```

```python
import functools

import jax
import jax.numpy as jnp
from jax import lax
from jax.experimental import pallas as pl
from jax.experimental.pallas import tpu as pltpu
from jax.sharding import PartitionSpec as P

OMEGA = 0.8
HALO = 7
OWN = 8
EXT = OWN + 2 * HALO
LANES = 256
F32 = jnp.float32
DEEP = 16
SUMS = 44


def iota(shape, dim):
    return lax.broadcasted_iota(jnp.int32, shape, dim)


def roll(value, shift, axis):
    return pltpu.roll(value, shift % value.shape[axis], axis)


def swap(value, width, axis):
    at = iota(value.shape, axis)
    lower = (at // width) % 2 == 0
    return jnp.where(lower, roll(value, -width, axis), roll(value, width, axis))


def along_y(value, width):
    axis = value.ndim - 1
    return roll(value, width, axis) + roll(value, -width, axis)


def apply_fine(even, odd, extra_even, extra_odd):
    e, o = even[1:-1], odd[1:-1]
    k = iota(e.shape, 1)
    by_e = o + jnp.where(k > 0, roll(o, 1, 1), 0.0) + even[2:] + even[:-2] + along_y(e, 1)
    by_o = e + jnp.where(k < 7, roll(e, -1, 1), 0.0) + odd[2:] + odd[:-2] + along_y(o, 1)
    return 6.0 * e - by_e + extra_even * e, 6.0 * o - by_o + extra_odd * o


def restrict_fine(even, odd):
    both = even + odd
    both = jnp.sum(both.reshape((both.shape[0] // 2, 2) + both.shape[1:]), axis=1)
    return 0.125 * (both + swap(both, 1, 2))


def double_rows(value):
    wide = jnp.broadcast_to(value[:, None], (value.shape[0], 2) + value.shape[1:])
    return wide.reshape((2 * value.shape[0],) + value.shape[1:])


def apply_one(value, extra):
    v = value[1:-1]
    k = iota(v.shape, 1)
    beside = jnp.where(k > 0, roll(v, 1, 1), 0.0) + jnp.where(k < 7, roll(v, -1, 1), 0.0)
    beside = beside + value[2:] + value[:-2] + along_y(v, 2)
    return 0.25 * (6.0 * v - beside) + extra * v


def pack_two(value, first_lane):
    pairs = jnp.sum(value.reshape((2, 2) + value.shape[1:]), axis=1)
    pairs = pairs + swap(pairs, 1, 1)
    rows = jnp.where(iota(pairs.shape[1:], 0) % 2 == 0, pairs[0], pairs[1])
    shape = (LANES, 128)
    matrix = jnp.where(iota(shape, 0) // 4 + first_lane == iota(shape, 1), 0.0625, 0.0)
    return jnp.dot(rows, matrix.astype(F32), precision=lax.Precision.HIGHEST)


def pack_rows(value, scratch):
    pairs = jnp.sum(value.reshape((2, 2) + value.shape[1:]), axis=1)
    pairs = pairs + swap(pairs, 1, 1)
    shape = (LANES, 128)
    out = jnp.zeros((8, 128), F32)
    for x in range(2):
        matrix = jnp.where(iota(shape, 0) // 4 + 64 * x == iota(shape, 1), 0.0625, 0.0)
        out = out + jnp.dot(pairs[x], matrix.astype(F32), precision=lax.Precision.HIGHEST)
    scratch[...] = out
    return scratch[pl.ds(0, 4, stride=2), :]


def split_two(ref, wide):
    return [[ref[pl.ds(2 * z + x, wide, stride=8), :] for z in range(4)] for x in range(2)]


def add(terms):
    return functools.reduce(lambda a, b: a + b, terms)


def before(value):
    return jnp.where(iota(value.shape, 0) > 0, roll(value, 1, 0), 0.0)


def after(value):
    last = value.shape[0] - 1
    return jnp.where(iota(value.shape, 0) < last, roll(value, -1, 0), 0.0)


def each(function, *lists):
    return [[function(*(a[x][z] for a in lists)) for z in range(4)] for x in range(2)]


def apply_two(v, d):
    out = [[], []]
    for x in range(2):
        for z in range(4):
            terms = [along_y(v[x][z], 1), v[1 - x][z]]
            terms += [before(v[1][z])] if x == 0 else [after(v[0][z])]
            terms += [v[x][k] for k in (z - 1, z + 1) if 0 <= k < 4]
            out[x].append(0.0625 * (6.0 * v[x][z] - add(terms)) + d[x][z] * v[x][z])
    return out


def restrict_two(v):
    out = []
    for z in range(2):
        total = v[0][2 * z] + v[0][2 * z + 1] + v[1][2 * z] + v[1][2 * z + 1]
        out.append(0.125 * (total + swap(total, 1, 1)))
    return out


def apply_three(v, d):
    out = []
    for z in range(2):
        beside = before(v[z]) + after(v[z]) + v[1 - z] + along_y(v[z], 2)
        out.append(0.015625 * (6.0 * v[z] - beside) + d[z] * v[z])
    return out


def solve_coarse(r2, d2, mine, narrow):
    shape = r2[0][0].shape
    lane = iota(shape, 1) % 64
    column = 32 * mine + jnp.where(lane < 48, lane, lane - 64)
    inside = (column >= 0) & (column < 32 * narrow)
    i2 = each(lambda d: jnp.where(inside, OMEGA / (0.375 + d), 0.0), d2)
    c2 = each(lambda i, r: i * r, i2, r2)
    left = each(lambda r, a: r - a, r2, apply_two(c2, d2))
    r3, d3 = restrict_two(left), restrict_two(d2)
    i3 = [jnp.where(inside, OMEGA / (0.09375 + d), 0.0) for d in d3]
    e3 = [i * r for i, r in zip(i3, r3)]
    for _ in range(3):
        a3 = apply_three(e3, d3)
        e3 = [e + i * (r - a) for e, i, r, a in zip(e3, i3, r3, a3)]
    one = inside[:1]
    for z in range(2):
        weight = jnp.where(one, jnp.sum(d3[z], axis=0, keepdims=True), 1.0)
        line = jnp.where(one, jnp.sum(r3[z], axis=0, keepdims=True) / weight, 0.0)
        e3[z] = e3[z] + line
    e2 = [[c2[x][z] + e3[z // 2] for z in range(4)] for x in range(2)]
    return each(lambda e, i, r, a: e + i * (r - a), e2, i2, r2, apply_two(e2, d2))


def rise(e2, scratch, at, reach, r1, d1, i1):
    wide = e2[0][0].shape[0]
    blank = jnp.zeros((8, 128), F32)
    for x in range(2):
        for z in range(4):
            scratch[2 * z + x, 0:8, :] = blank
            scratch[2 * z + x, 8 + wide : 16 + wide, :] = blank
            scratch[2 * z + x, 8 : 8 + wide, :] = e2[x][z]
    pair = iota((8, 128), 0) // 2
    rows = []
    for row in range(-reach, 2 + reach):
        x, step = row % 2, row // 2
        tile = blank
        for z in range(4):
            line = scratch[2 * z + x, pl.ds(at + (8 + step), 1), :]
            tile = jnp.where(pair == z, jnp.broadcast_to(line, (8, 128)), tile)
        rows.append(tile)
    shape = (128, LANES)
    matrix = jnp.where(iota(shape, 0) == iota(shape, 1) // 4, 1.0, 0.0).astype(F32)
    spread = jnp.dot(jnp.concatenate(rows, 0), matrix, precision=lax.Precision.HIGHEST)
    up = double_rows(spread.reshape(len(rows), 8, LANES))
    trim = (up.shape[0] - r1.shape[0]) // 2
    e1 = i1 * r1 + up[trim : trim + r1.shape[0]]
    return e1[1:-1] + i1[1:-1] * (r1[1:-1] - apply_one(e1, d1[1:-1]))


def rows_of(pair, first, stop):
    return [pair[p][first:stop] for p in range(2)]


def finish(up, source, extra, inverse):
    e = [inverse[p] * source[p] + up for p in range(2)]
    a = apply_fine(e[0], e[1], extra[0][1:-1], extra[1][1:-1])
    z = [e[p][1:-1] + inverse[p][1:-1] * (source[p][1:-1] - a[p]) for p in range(2)]
    q = apply_fine(z[0], z[1], extra[0][2:-2], extra[1][2:-2])
    return z, q


def descend(source, extra, inverse):
    c = [i * s for i, s in zip(inverse, source)]
    a = apply_fine(c[0], c[1], extra[0][1:-1], extra[1][1:-1])
    left = [source[p][1:-1] - a[p] for p in range(2)]
    return restrict_fine(left[0], left[1])


def leave_one(r1, d1, i1):
    return r1[1:-1] - apply_one(i1 * r1, d1[1:-1])


def invert_one(d1, first, me_w, me_n, wide, narrow):
    lane = iota(d1.shape, 2)
    column = 128 * me_n + jnp.where(lane < 192, lane, lane - 256)
    line = 4 * me_w + first + iota(d1.shape, 0)
    inside = (column >= 0) & (column < 128 * narrow) & (line >= 0) & (line < 4 * wide)
    return jnp.where(inside, OMEGA / (1.5 + d1), 0.0)


def total(a, b):
    return jnp.sum(jnp.sum(a[0] * b[0] + a[1] * b[1], axis=0), keepdims=True)


def place(values, shape, first):
    lane = iota(shape, len(shape) - 1)
    out = jnp.zeros(shape, F32)
    for i, v in enumerate(values):
        out = jnp.where(lane == first + i, v, out)
    return out


def prepare_kernel(right, diagonal, own, low, high):
    half = iota((8, 128), 1) < 64
    for p in range(2):
        for x in range(OWN):
            rows = pl.ds(x + 8 * p, 8, stride=16)
            r, d = right[rows, :], diagonal[rows, :]
            first = jnp.where(half, r, roll(d, 64, 1))
            second = jnp.where(half, roll(r, 64, 1), d)
            for side, value in ((0, first), (1, second)):
                own[side, p, x] = value
                if x < HALO:
                    low[side, p, x] = value
                if x >= OWN - HALO:
                    high[side, p, x - (OWN - HALO)] = value


def down_kernel(wide, narrow, a, b, from_left, from_right, r0, d0, i0, one, low, high, send):
    me_w, me_n = lax.axis_index("wide"), lax.axis_index("narrow")
    shape = (EXT, 8, 128)
    half = iota(shape, 2) < 64
    fine = (EXT, 8, LANES)
    lane, row = iota(fine, 2), iota(fine, 0)
    column = 128 * me_n + jnp.where(lane < 192, lane, lane - 256)
    line = 8 * me_w - HALO + row
    inside = (column >= 0) & (column < 128 * narrow) & (line >= 0) & (line < 8 * wide)
    source, extra, inverse = [], [], []
    for p in range(2):
        fa, fb, fl, fr = a[p], b[p], from_left[p], from_right[p]
        own_r = jnp.where(half, fa, roll(fb, 64, 2))
        own_d = jnp.where(half, roll(fa, 64, 2), fb)
        far_r = jnp.where(half, fr, roll(fl, 64, 2))
        far_d = jnp.where(half, roll(fr, 64, 2), fl)
        source.append(jnp.concatenate([own_r, far_r], axis=2))
        extra.append(jnp.concatenate([own_d, far_d], axis=2))
        inverse.append(jnp.where(inside, OMEGA / (6.0 + extra[p]), 0.0))
        r0[p] = source[p]
        d0[p] = extra[p]
        i0[p] = inverse[p]
    vr1 = descend(source, extra, inverse)
    vd1 = restrict_fine(extra[0][1:-1], extra[1][1:-1])
    vi1 = invert_one(vd1, -3, me_w, me_n, wide, narrow)
    for side, value in ((0, vr1), (1, vd1)):
        one[side] = value
        high[side] = value[2:4]
        low[side] = value[6:8]
    left = leave_one(vr1[2:8], vd1[2:8], vi1[2:8])
    tile = pack_two(left, 0) + pack_two(vd1[3:7], 64)
    send[...] = jnp.broadcast_to(tile, send.shape)


def both_halves(tile):
    half = iota(tile.shape, 1) < 64
    other = roll(tile, 64, 1)
    return jnp.where(half, tile, other), jnp.where(half, other, tile)


def turn_kernel(wide, narrow, got, r0, d0, i0, one, below, above, z, q, r1, d1, i1, send, scratch, small):
    me_w, me_n = lax.axis_index("wide"), lax.axis_index("narrow")
    tiles = split_two(got, wide)
    r2 = each(lambda t: both_halves(t)[0], tiles)
    d2 = each(lambda t: both_halves(t)[1], tiles)
    e2 = solve_coarse(r2, d2, me_n, narrow)
    vr1 = jnp.concatenate([below[0], one[0], above[0]], axis=0)
    vd1 = jnp.concatenate([below[1], one[1], above[1]], axis=0)
    vi1 = invert_one(vd1, -5, me_w, me_n, wide, narrow)
    e1 = rise(e2, scratch, me_w, 3, vr1, vd1, vi1)
    up = double_rows(e1)[1:-1]
    source, extra, inverse = (rows_of(ref, 0, EXT) for ref in (r0, d0, i0))
    vz, vq = finish(up, source, extra, inverse)
    own_z = [v[6:14, :, :128] for v in vz]
    own_q = [v[5:13, :, :128] for v in vq]
    own_r = [v[HALO : HALO + OWN, :, :128] for v in source]
    for p in range(2):
        z[p] = own_z[p]
        q[p] = vq[p]
    below_two = descend(vq, rows_of(d0, 2, 20), rows_of(i0, 2, 20))
    r1[...] = below_two
    d1[...] = vd1[3:11]
    i1[...] = vi1[3:11]
    rows = pack_rows(leave_one(below_two[1:7], vd1[4:10], vi1[4:10]), small)
    sums = place([total(own_r, own_z), total(own_z, own_q)], rows.shape, SUMS)
    lane = iota(rows.shape, 1)
    send[0:4, :] = jnp.where((lane == SUMS) | (lane == SUMS + 1), sums, rows)
    send[4:8, :] = jnp.zeros(rows.shape, F32)


def window_kernel(own, right, left, send):
    lane = iota(own.shape, 1)
    cell = lane % 64
    halo = jnp.where(cell < 48, roll(right[...], 32, 1), roll(left[...], 32, 1))
    keep = (cell < 32) | (lane == SUMS) | (lane == SUMS + 1)
    send[...] = jnp.broadcast_to(jnp.where(keep, own[...], halo)[0:4], send.shape)


def split_rows(ref, wide):
    sides = [[], []]
    for z in range(4):
        for side, value in zip(sides, both_halves(ref[pl.ds(z, wide, stride=4), :])):
            side.append(value)
    return sides


def up_again_kernel(wide, narrow, got, first, source, r0, d0, i0, r1, d1, i1, z0, w0, y0, sums, scratch):
    me_w, me_n = lax.axis_index("wide"), lax.axis_index("narrow")
    r2 = split_rows(got, wide)
    d2 = each(lambda t: both_halves(t)[1], split_two(first, wide))
    e2 = solve_coarse(r2, d2, me_n, narrow)
    e1 = rise(e2, scratch, me_w, 1, r1[...], d1[...], i1[...])
    extra, inverse = rows_of(d0, 5, 17), rows_of(i0, 5, 17)
    vw, vy = finish(double_rows(e1), rows_of(source, 3, 15), extra, inverse)
    w = [v[1:-1, :, :128] for v in vw]
    y = [v[:, :, :128] for v in vy]
    scalars = jnp.sum(got[pl.ds(0, wide, stride=4), :], axis=0, keepdims=True)
    lane = iota((1, 128), 1)
    rho = jnp.sum(jnp.where(lane == SUMS, scalars, 0.0), keepdims=True)
    curve = jnp.sum(jnp.where(lane == SUMS + 1, scalars, 0.0), keepdims=True)
    ratio = rho / jnp.where(curve > 0.0, curve, 1.0)
    shift = jnp.where(curve > 0.0, jnp.minimum(jnp.maximum(ratio, 0.0), 8.0), 0.0)
    s = shift.reshape(1, 1, 1)
    z = [z0[p] for p in range(2)]
    q = [source[p, 5:13, :, :128] for p in range(2)]
    r = [r0[p, HALO : HALO + OWN, :, :128] for p in range(2)]
    for p in range(2):
        w0[p] = w[p]
        y0[p] = y[p]
    rs = [r[p] - s * q[p] for p in range(2)]
    zs = [z[p] - s * w[p] for p in range(2)]
    ys = [q[p] - s * y[p] for p in range(2)]
    values = [
        shift,
        total(r, z),
        total(z, q),
        total(rs, zs),
        total(rs, w) + total(q, zs),
        total(q, w),
        total(zs, ys),
        total(w, ys) + total(zs, y),
        total(w, y),
        total(zs, q) + total(z, ys),
        total(w, q) + total(z, y),
    ]
    sums[...] = jnp.broadcast_to(place(values, (1, 128), 0), sums.shape)


def last_kernel(got, z0, source, w0, y0, r0, field, residual):
    lane = iota(got.shape, 1)

    def pick(at):
        return jnp.sum(jnp.where(lane == at, got[...], 0.0), axis=1, keepdims=True)

    def whole(columns):
        return jnp.sum(columns, axis=0, keepdims=True)

    shift, g = pick(0), [pick(i) for i in range(1, 11)]
    rho, curve = whole(g[0]), whole(g[1])
    alpha = rho / curve
    t = alpha - shift
    rho_next = whole(g[2] - t * (g[3] - t * g[4]))
    square = whole(g[5] - t * (g[6] - t * g[7]))
    cross = whole(g[8] - t * g[9])
    beta = rho_next / rho
    alpha_next = rho_next / (square + beta * cross + beta * beta * curve)
    for p in range(2):
        for x in range(OWN):
            rows = pl.ds(x + 8 * p, 8, stride=16)
            z, q = z0[p, x], source[p, 5 + x, :, :128]
            step = (z - alpha * w0[p, x]) + beta * z
            image = (q - alpha * y0[p, x]) + beta * q
            field[rows, :] = alpha * z + alpha_next * step
            residual[rows, :] = (r0[p, HALO + x, :, :128] - alpha * q) - alpha_next * image


def call(kernel, outs, *args, scratch=()):
    return pl.pallas_call(
        kernel,
        out_shape=tuple(jax.ShapeDtypeStruct(s, F32) for s in outs),
        in_specs=[pl.BlockSpec(memory_space=pltpu.VMEM)] * len(args),
        out_specs=tuple(pl.BlockSpec(memory_space=pltpu.VMEM) for _ in outs),
        scratch_shapes=scratch,
        compiler_params=pltpu.CompilerParams(vmem_limit_bytes=40 * 1024 * 1024),
    )(*args)


def exchange(slots, axis, groups=None):
    return lax.all_to_all(slots, axis, 0, 0, axis_index_groups=groups)


def to_next(array, axis):
    n = lax.axis_size(axis)
    return lax.ppermute(array, axis, [(i, i + 1) for i in range(n - 1)])


def to_previous(array, axis):
    n = lax.axis_size(axis)
    return lax.ppermute(array, axis, [(i + 1, i) for i in range(n - 1)])


def around(array, axis, step):
    n = lax.axis_size(axis)
    return lax.ppermute(array, axis, [(i, (i + step) % n) for i in range(n)])


def on_device(right_side, capacity, phase, mold_flags):
    wide, narrow = lax.axis_size("wide"), lax.axis_size("narrow")
    edge = (2, 2, HALO, 8, 128)
    weight = jnp.where(phase == 1, jnp.float32(4.0), jnp.float32(1.0))
    diagonal = 0.05 * capacity * weight + 0.5 * mold_flags.astype(F32)
    own, low, high = call(
        prepare_kernel,
        [(2, 2, OWN, 8, 128), edge, edge],
        right_side.reshape(128, 128), diagonal.reshape(128, 128),
    )
    below, above = to_next(high, "wide"), to_previous(low, "wide")
    a = jnp.concatenate([below[0], own[0], above[0]], axis=1)
    b = jnp.concatenate([below[1], own[1], above[1]], axis=1)
    from_left, from_right = around(b, "narrow", 1), around(a, "narrow", -1)
    fine, pair = (2, EXT, 8, LANES), (2, 2, 8, LANES)
    r0, d0, i0, one, low, high, send = call(
        functools.partial(down_kernel, wide, narrow),
        [fine, fine, fine, (2, 10, 8, LANES), pair, pair, (wide, 8, 128)],
        a, b, from_left, from_right,
    )
    below, above = to_next(high, "wide"), to_previous(low, "wide")
    first = exchange(send, "wide").reshape(8 * wide, 128)
    block, coarse = (2, OWN, 8, 128), (8, 8, LANES)
    scratch = [pltpu.VMEM((8, wide + 16, 128), F32)]
    z0, source, r1, d1, i1, send = call(
        functools.partial(turn_kernel, wide, narrow),
        [block, (2, 18, 8, LANES), coarse, coarse, coarse, (8, 128)],
        first, r0, d0, i0, one, below, above,
        scratch=scratch + [pltpu.VMEM((8, 128), F32)],
    )
    from_left, from_right = around(send, "narrow", 1), around(send, "narrow", -1)
    (send,) = call(window_kernel, [(wide, 4, 128)], send, from_right, from_left)
    second = exchange(send, "wide").reshape(4 * wide, 128)
    w0, y0, sums = call(
        functools.partial(up_again_kernel, wide, narrow),
        [block, block, (DEEP, 1, 128)],
        second, first, source, r0, d0, i0, r1, d1, i1, z0,
        scratch=scratch,
    )
    across = wide // DEEP
    far = [[DEEP * y + z for z in range(DEEP)] for y in range(across)]
    near = [
        [(DEEP * y + z) * narrow + n for y in range(across) for n in range(narrow)]
        for z in range(DEEP)
    ]
    parts = exchange(sums, "wide", far)
    sums = jnp.where(jnp.arange(128) == 0, parts[0], jnp.sum(parts, axis=0))
    sums = jnp.broadcast_to(sums[None], (across * narrow,) + sums.shape)
    third = exchange(sums, ("wide", "narrow"), near).reshape(across * narrow, 128)
    field, residual = call(
        last_kernel, [(128, 128), (128, 128)], third, z0, source, w0, y0, r0
    )
    return field.reshape(right_side.shape), residual.reshape(right_side.shape)


def solution(mesh):
    spec = P(None, "wide", "narrow")
    return jax.shard_map(
        on_device, mesh=mesh, in_specs=(spec,) * 4, out_specs=(spec, spec), check_vma=False
    )
```

```python
import functools

import jax
import jax.numpy as jnp
from jax import lax
from jax.experimental import pallas as pl
from jax.experimental.pallas import tpu as pltpu
from jax.sharding import PartitionSpec as P

OMEGA = 0.8
HALO = 7
OWN = 8
EXT = OWN + 2 * HALO
LANES = 256
F32 = jnp.float32
DEEP = 16
SUMS = 44


def iota(shape, dim):
    return lax.broadcasted_iota(jnp.int32, shape, dim)


def roll(value, shift, axis):
    return pltpu.roll(value, shift % value.shape[axis], axis)


def swap(value, width, axis):
    at = iota(value.shape, axis)
    lower = (at // width) % 2 == 0
    return jnp.where(lower, roll(value, -width, axis), roll(value, width, axis))


def along_y(value, width):
    axis = value.ndim - 1
    return roll(value, width, axis) + roll(value, -width, axis)


def apply_fine(even, odd, extra_even, extra_odd):
    e, o = even[1:-1], odd[1:-1]
    k = iota(e.shape, 1)
    by_e = o + jnp.where(k > 0, roll(o, 1, 1), 0.0) + even[2:] + even[:-2] + along_y(e, 1)
    by_o = e + jnp.where(k < 7, roll(e, -1, 1), 0.0) + odd[2:] + odd[:-2] + along_y(o, 1)
    return 6.0 * e - by_e + extra_even * e, 6.0 * o - by_o + extra_odd * o


def restrict_fine(even, odd):
    both = even + odd
    both = jnp.sum(both.reshape((both.shape[0] // 2, 2) + both.shape[1:]), axis=1)
    return 0.125 * (both + swap(both, 1, 2))


def double_rows(value):
    wide = jnp.broadcast_to(value[:, None], (value.shape[0], 2) + value.shape[1:])
    return wide.reshape((2 * value.shape[0],) + value.shape[1:])


def apply_one(value, extra):
    v = value[1:-1]
    k = iota(v.shape, 1)
    beside = jnp.where(k > 0, roll(v, 1, 1), 0.0) + jnp.where(k < 7, roll(v, -1, 1), 0.0)
    beside = beside + value[2:] + value[:-2] + along_y(v, 2)
    return 0.25 * (6.0 * v - beside) + extra * v


def pair_rows(value):
    pairs = jnp.sum(value.reshape((2, 2) + value.shape[1:]), axis=1)
    return pairs + swap(pairs, 1, 1)


def pack(first, second):
    shape = (LANES, 128)
    matrix = jnp.where(iota(shape, 0) // 4 == iota(shape, 1), 0.0625, 0.0).astype(F32)
    both = jnp.concatenate([first, second], axis=0)
    out = jnp.dot(both, matrix, precision=lax.Precision.HIGHEST)
    return out[:8] + roll(out[8:], 64, 1)


def pack_two(first, second):
    rows = []
    for value in (first, second):
        pairs = pair_rows(value)
        rows.append(jnp.where(iota(pairs.shape[1:], 0) % 2 == 0, pairs[0], pairs[1]))
    return pack(*rows)


def pack_rows(value, scratch):
    pairs = pair_rows(value)
    scratch[...] = pack(pairs[0], pairs[1])
    return scratch[pl.ds(0, 4, stride=2), :]


def split_two(ref, wide):
    return [[ref[pl.ds(2 * z + x, wide, stride=8), :] for z in range(4)] for x in range(2)]


def add(terms):
    return functools.reduce(lambda a, b: a + b, terms)


def before(value):
    return jnp.where(iota(value.shape, 0) > 0, roll(value, 1, 0), 0.0)


def after(value):
    last = value.shape[0] - 1
    return jnp.where(iota(value.shape, 0) < last, roll(value, -1, 0), 0.0)


def each(function, *lists):
    return [[function(*(a[x][z] for a in lists)) for z in range(4)] for x in range(2)]


def apply_two(v, d):
    out = [[], []]
    for x in range(2):
        for z in range(4):
            terms = [along_y(v[x][z], 1), v[1 - x][z]]
            terms += [before(v[1][z])] if x == 0 else [after(v[0][z])]
            terms += [v[x][k] for k in (z - 1, z + 1) if 0 <= k < 4]
            out[x].append(0.0625 * (6.0 * v[x][z] - add(terms)) + d[x][z] * v[x][z])
    return out


def restrict_two(v):
    out = []
    for z in range(2):
        total = v[0][2 * z] + v[0][2 * z + 1] + v[1][2 * z] + v[1][2 * z + 1]
        out.append(0.125 * (total + swap(total, 1, 1)))
    return out


def apply_three(v, d):
    out = []
    for z in range(2):
        beside = before(v[z]) + after(v[z]) + v[1 - z] + along_y(v[z], 2)
        out.append(0.015625 * (6.0 * v[z] - beside) + d[z] * v[z])
    return out


def solve_coarse(r2, d2, mine, narrow):
    shape = r2[0][0].shape
    lane = iota(shape, 1) % 64
    column = 32 * mine + jnp.where(lane < 48, lane, lane - 64)
    inside = (column >= 0) & (column < 32 * narrow)
    i2 = each(lambda d: jnp.where(inside, OMEGA / (0.375 + d), 0.0), d2)
    c2 = each(lambda i, r: i * r, i2, r2)
    left = each(lambda r, a: r - a, r2, apply_two(c2, d2))
    r3, d3 = restrict_two(left), restrict_two(d2)
    i3 = [jnp.where(inside, OMEGA / (0.09375 + d), 0.0) for d in d3]
    e3 = [i * r for i, r in zip(i3, r3)]
    for _ in range(3):
        a3 = apply_three(e3, d3)
        e3 = [e + i * (r - a) for e, i, r, a in zip(e3, i3, r3, a3)]
    one = inside[:1]
    for z in range(2):
        weight = jnp.where(one, jnp.sum(d3[z], axis=0, keepdims=True), 1.0)
        line = jnp.where(one, jnp.sum(r3[z], axis=0, keepdims=True) / weight, 0.0)
        e3[z] = e3[z] + line
    e2 = [[c2[x][z] + e3[z // 2] for z in range(4)] for x in range(2)]
    return each(lambda e, i, r, a: e + i * (r - a), e2, i2, r2, apply_two(e2, d2))


def rise(e2, scratch, at, reach, r1, d1, i1):
    wide = e2[0][0].shape[0]
    blank = jnp.zeros((8, 128), F32)
    for x in range(2):
        for z in range(4):
            scratch[2 * z + x, 0:8, :] = blank
            scratch[2 * z + x, 8 + wide : 16 + wide, :] = blank
            scratch[2 * z + x, 8 : 8 + wide, :] = e2[x][z]
    pair = iota((8, 128), 0) // 2
    rows = []
    for row in range(-reach, 2 + reach):
        x, step = row % 2, row // 2
        tile = blank
        for z in range(4):
            line = scratch[2 * z + x, pl.ds(at + (8 + step), 1), :]
            tile = jnp.where(pair == z, jnp.broadcast_to(line, (8, 128)), tile)
        rows.append(tile)
    shape = (128, LANES)
    matrix = jnp.where(iota(shape, 0) == iota(shape, 1) // 4, 1.0, 0.0).astype(F32)
    spread = jnp.dot(jnp.concatenate(rows, 0), matrix, precision=lax.Precision.HIGHEST)
    up = double_rows(spread.reshape(len(rows), 8, LANES))
    trim = (up.shape[0] - r1.shape[0]) // 2
    e1 = i1 * r1 + up[trim : trim + r1.shape[0]]
    return e1[1:-1] + i1[1:-1] * (r1[1:-1] - apply_one(e1, d1[1:-1]))


def rows_of(pair, first, stop):
    return [pair[p][first:stop] for p in range(2)]


def finish(up, source, extra, inverse):
    e = [inverse[p] * source[p] + up for p in range(2)]
    a = apply_fine(e[0], e[1], extra[0][1:-1], extra[1][1:-1])
    z = [e[p][1:-1] + inverse[p][1:-1] * (source[p][1:-1] - a[p]) for p in range(2)]
    q = apply_fine(z[0], z[1], extra[0][2:-2], extra[1][2:-2])
    return z, q


def descend(source, extra, inverse):
    c = [i * s for i, s in zip(inverse, source)]
    a = apply_fine(c[0], c[1], extra[0][1:-1], extra[1][1:-1])
    left = [source[p][1:-1] - a[p] for p in range(2)]
    return restrict_fine(left[0], left[1])


def leave_one(r1, d1, i1):
    return r1[1:-1] - apply_one(i1 * r1, d1[1:-1])


def invert_one(d1, first, me_w, me_n, wide, narrow):
    lane = iota(d1.shape, 2)
    column = 128 * me_n + jnp.where(lane < 192, lane, lane - 256)
    line = 4 * me_w + first + iota(d1.shape, 0)
    inside = (column >= 0) & (column < 128 * narrow) & (line >= 0) & (line < 4 * wide)
    return jnp.where(inside, OMEGA / (1.5 + d1), 0.0)


def total(a, b):
    return jnp.sum(jnp.sum(a[0] * b[0] + a[1] * b[1], axis=0), keepdims=True)


def place(values, shape, first):
    lane = iota(shape, len(shape) - 1)
    out = jnp.zeros(shape, F32)
    for i, v in enumerate(values):
        out = jnp.where(lane == first + i, v, out)
    return out


def prepare_kernel(right, diagonal, own, low, high):
    half = iota((8, 128), 1) < 64
    for p in range(2):
        for x in range(OWN):
            rows = pl.ds(x + 8 * p, 8, stride=16)
            r, d = right[rows, :], diagonal[rows, :]
            first = jnp.where(half, r, roll(d, 64, 1))
            second = jnp.where(half, roll(r, 64, 1), d)
            for side, value in ((0, first), (1, second)):
                own[side, p, x] = value
                if x < HALO:
                    low[side, p, x] = value
                if x >= OWN - HALO:
                    high[side, p, x - (OWN - HALO)] = value


def down_kernel(wide, narrow, a, b, from_left, from_right, r0, d0, i0, one, low, high, send):
    me_w, me_n = lax.axis_index("wide"), lax.axis_index("narrow")
    shape = (EXT, 8, 128)
    half = iota(shape, 2) < 64
    fine = (EXT, 8, LANES)
    lane, row = iota(fine, 2), iota(fine, 0)
    column = 128 * me_n + jnp.where(lane < 192, lane, lane - 256)
    line = 8 * me_w - HALO + row
    inside = (column >= 0) & (column < 128 * narrow) & (line >= 0) & (line < 8 * wide)
    source, extra, inverse = [], [], []
    for p in range(2):
        fa, fb, fl, fr = a[p], b[p], from_left[p], from_right[p]
        own_r = jnp.where(half, fa, roll(fb, 64, 2))
        own_d = jnp.where(half, roll(fa, 64, 2), fb)
        far_r = jnp.where(half, fr, roll(fl, 64, 2))
        far_d = jnp.where(half, roll(fr, 64, 2), fl)
        source.append(jnp.concatenate([own_r, far_r], axis=2))
        extra.append(jnp.concatenate([own_d, far_d], axis=2))
        inverse.append(jnp.where(inside, OMEGA / (6.0 + extra[p]), 0.0))
        r0[p] = source[p]
        d0[p] = extra[p]
        i0[p] = inverse[p]
    vr1 = descend(source, extra, inverse)
    vd1 = restrict_fine(extra[0][1:-1], extra[1][1:-1])
    vi1 = invert_one(vd1, -3, me_w, me_n, wide, narrow)
    for side, value in ((0, vr1), (1, vd1)):
        one[side] = value
        high[side] = value[2:4]
        low[side] = value[6:8]
    left = leave_one(vr1[2:8], vd1[2:8], vi1[2:8])
    tile = pack_two(left, vd1[3:7])
    send[...] = jnp.broadcast_to(tile, send.shape)


def both_halves(tile):
    half = iota(tile.shape, 1) < 64
    other = roll(tile, 64, 1)
    return jnp.where(half, tile, other), jnp.where(half, other, tile)


def turn_kernel(wide, narrow, got, r0, d0, i0, one, below, above, z, q, r1, d1, i1, send, scratch, small):
    me_w, me_n = lax.axis_index("wide"), lax.axis_index("narrow")
    tiles = split_two(got, wide)
    r2 = each(lambda t: both_halves(t)[0], tiles)
    d2 = each(lambda t: both_halves(t)[1], tiles)
    e2 = solve_coarse(r2, d2, me_n, narrow)
    vr1 = jnp.concatenate([below[0], one[0], above[0]], axis=0)
    vd1 = jnp.concatenate([below[1], one[1], above[1]], axis=0)
    vi1 = invert_one(vd1, -5, me_w, me_n, wide, narrow)
    e1 = rise(e2, scratch, me_w, 3, vr1, vd1, vi1)
    up = double_rows(e1)[1:-1]
    source, extra, inverse = (rows_of(ref, 0, EXT) for ref in (r0, d0, i0))
    vz, vq = finish(up, source, extra, inverse)
    own_z = [v[6:14, :, :128] for v in vz]
    own_q = [v[5:13, :, :128] for v in vq]
    own_r = [v[HALO : HALO + OWN, :, :128] for v in source]
    for p in range(2):
        z[p] = own_z[p]
        q[p] = vq[p]
    below_two = descend(vq, rows_of(d0, 2, 20), rows_of(i0, 2, 20))
    r1[...] = below_two
    d1[...] = vd1[3:11]
    i1[...] = vi1[3:11]
    rows = pack_rows(leave_one(below_two[1:7], vd1[4:10], vi1[4:10]), small)
    sums = place([total(own_r, own_z), total(own_z, own_q)], rows.shape, SUMS)
    lane = iota(rows.shape, 1)
    send[0:4, :] = jnp.where((lane == SUMS) | (lane == SUMS + 1), sums, rows)
    send[4:8, :] = jnp.zeros(rows.shape, F32)


def window_kernel(own, right, left, send):
    lane = iota(own.shape, 1)
    cell = lane % 64
    halo = jnp.where(cell < 48, roll(right[...], 32, 1), roll(left[...], 32, 1))
    keep = (cell < 32) | (lane == SUMS) | (lane == SUMS + 1)
    send[...] = jnp.broadcast_to(jnp.where(keep, own[...], halo)[0:4], send.shape)


def split_rows(ref, wide):
    sides = [[], []]
    for z in range(4):
        for side, value in zip(sides, both_halves(ref[pl.ds(z, wide, stride=4), :])):
            side.append(value)
    return sides


def up_again_kernel(wide, narrow, got, first, source, r0, d0, i0, r1, d1, i1, z0, w0, y0, sums, scratch):
    me_w, me_n = lax.axis_index("wide"), lax.axis_index("narrow")
    r2 = split_rows(got, wide)
    d2 = each(lambda t: both_halves(t)[1], split_two(first, wide))
    e2 = solve_coarse(r2, d2, me_n, narrow)
    e1 = rise(e2, scratch, me_w, 1, r1[...], d1[...], i1[...])
    extra, inverse = rows_of(d0, 5, 17), rows_of(i0, 5, 17)
    vw, vy = finish(double_rows(e1), rows_of(source, 3, 15), extra, inverse)
    w = [v[1:-1, :, :128] for v in vw]
    y = [v[:, :, :128] for v in vy]
    scalars = jnp.sum(got[pl.ds(0, wide, stride=4), :], axis=0, keepdims=True)
    lane = iota((1, 128), 1)
    rho = jnp.sum(jnp.where(lane == SUMS, scalars, 0.0), keepdims=True)
    curve = jnp.sum(jnp.where(lane == SUMS + 1, scalars, 0.0), keepdims=True)
    ratio = rho / jnp.where(curve > 0.0, curve, 1.0)
    shift = jnp.where(curve > 0.0, jnp.minimum(jnp.maximum(ratio, 0.0), 8.0), 0.0)
    s = shift.reshape(1, 1, 1)
    z = [z0[p] for p in range(2)]
    q = [source[p, 5:13, :, :128] for p in range(2)]
    r = [r0[p, HALO : HALO + OWN, :, :128] for p in range(2)]
    for p in range(2):
        w0[p] = w[p]
        y0[p] = y[p]
    rs = [r[p] - s * q[p] for p in range(2)]
    zs = [z[p] - s * w[p] for p in range(2)]
    ys = [q[p] - s * y[p] for p in range(2)]
    values = [
        shift,
        total(r, z),
        total(z, q),
        total(rs, zs),
        total(rs, w) + total(q, zs),
        total(q, w),
        total(zs, ys),
        total(w, ys) + total(zs, y),
        total(w, y),
        total(zs, q) + total(z, ys),
        total(w, q) + total(z, y),
    ]
    sums[...] = jnp.broadcast_to(place(values, (1, 128), 0), sums.shape)


def last_kernel(got, z0, source, w0, y0, r0, field, residual):
    lane = iota(got.shape, 1)

    def pick(at):
        return jnp.sum(jnp.where(lane == at, got[...], 0.0), axis=1, keepdims=True)

    def whole(columns):
        return jnp.sum(columns, axis=0, keepdims=True)

    shift, g = pick(0), [pick(i) for i in range(1, 11)]
    rho, curve = whole(g[0]), whole(g[1])
    alpha = rho / curve
    t = alpha - shift
    rho_next = whole(g[2] - t * (g[3] - t * g[4]))
    square = whole(g[5] - t * (g[6] - t * g[7]))
    cross = whole(g[8] - t * g[9])
    beta = rho_next / rho
    alpha_next = rho_next / (square + beta * cross + beta * beta * curve)
    for p in range(2):
        for x in range(OWN):
            rows = pl.ds(x + 8 * p, 8, stride=16)
            z, q = z0[p, x], source[p, 5 + x, :, :128]
            step = (z - alpha * w0[p, x]) + beta * z
            image = (q - alpha * y0[p, x]) + beta * q
            field[rows, :] = alpha * z + alpha_next * step
            residual[rows, :] = (r0[p, HALO + x, :, :128] - alpha * q) - alpha_next * image


def call(kernel, outs, *args, scratch=()):
    return pl.pallas_call(
        kernel,
        out_shape=tuple(jax.ShapeDtypeStruct(s, F32) for s in outs),
        in_specs=[pl.BlockSpec(memory_space=pltpu.VMEM)] * len(args),
        out_specs=tuple(pl.BlockSpec(memory_space=pltpu.VMEM) for _ in outs),
        scratch_shapes=scratch,
        compiler_params=pltpu.CompilerParams(vmem_limit_bytes=40 * 1024 * 1024),
    )(*args)


def exchange(slots, axis, groups=None):
    return lax.all_to_all(slots, axis, 0, 0, axis_index_groups=groups)


def to_next(array, axis):
    n = lax.axis_size(axis)
    return lax.ppermute(array, axis, [(i, i + 1) for i in range(n - 1)])


def to_previous(array, axis):
    n = lax.axis_size(axis)
    return lax.ppermute(array, axis, [(i + 1, i) for i in range(n - 1)])


def around(array, axis, step):
    n = lax.axis_size(axis)
    return lax.ppermute(array, axis, [(i, (i + step) % n) for i in range(n)])


def on_device(right_side, capacity, phase, mold_flags):
    wide, narrow = lax.axis_size("wide"), lax.axis_size("narrow")
    edge = (2, 2, HALO, 8, 128)
    weight = jnp.where(phase == 1, jnp.float32(4.0), jnp.float32(1.0))
    diagonal = 0.05 * capacity * weight + 0.5 * mold_flags.astype(F32)
    own, low, high = call(
        prepare_kernel,
        [(2, 2, OWN, 8, 128), edge, edge],
        right_side.reshape(128, 128), diagonal.reshape(128, 128),
    )
    below, above = to_next(high, "wide"), to_previous(low, "wide")
    a = jnp.concatenate([below[0], own[0], above[0]], axis=1)
    b = jnp.concatenate([below[1], own[1], above[1]], axis=1)
    from_left, from_right = around(b, "narrow", 1), around(a, "narrow", -1)
    fine, pair = (2, EXT, 8, LANES), (2, 2, 8, LANES)
    r0, d0, i0, one, low, high, send = call(
        functools.partial(down_kernel, wide, narrow),
        [fine, fine, fine, (2, 10, 8, LANES), pair, pair, (wide, 8, 128)],
        a, b, from_left, from_right,
    )
    below, above = to_next(high, "wide"), to_previous(low, "wide")
    first = exchange(send, "wide").reshape(8 * wide, 128)
    block, coarse = (2, OWN, 8, 128), (8, 8, LANES)
    scratch = [pltpu.VMEM((8, wide + 16, 128), F32)]
    z0, source, r1, d1, i1, send = call(
        functools.partial(turn_kernel, wide, narrow),
        [block, (2, 18, 8, LANES), coarse, coarse, coarse, (8, 128)],
        first, r0, d0, i0, one, below, above,
        scratch=scratch + [pltpu.VMEM((8, 128), F32)],
    )
    from_left, from_right = around(send, "narrow", 1), around(send, "narrow", -1)
    (send,) = call(window_kernel, [(wide, 4, 128)], send, from_right, from_left)
    second = exchange(send, "wide").reshape(4 * wide, 128)
    w0, y0, sums = call(
        functools.partial(up_again_kernel, wide, narrow),
        [block, block, (DEEP, 1, 128)],
        second, first, source, r0, d0, i0, r1, d1, i1, z0,
        scratch=scratch,
    )
    across = wide // DEEP
    far = [[DEEP * y + z for z in range(DEEP)] for y in range(across)]
    near = [
        [(DEEP * y + z) * narrow + n for y in range(across) for n in range(narrow)]
        for z in range(DEEP)
    ]
    parts = exchange(sums, "wide", far)
    sums = jnp.where(jnp.arange(128) == 0, parts[0], jnp.sum(parts, axis=0))
    sums = jnp.broadcast_to(sums[None], (across * narrow,) + sums.shape)
    third = exchange(sums, ("wide", "narrow"), near).reshape(across * narrow, 128)
    field, residual = call(
        last_kernel, [(128, 128), (128, 128)], third, z0, source, w0, y0, r0
    )
    return field.reshape(right_side.shape), residual.reshape(right_side.shape)


def solution(mesh):
    spec = P(None, "wide", "narrow")
    return jax.shard_map(
        on_device, mesh=mesh, in_specs=(spec,) * 4, out_specs=(spec, spec), check_vma=False
    )
```
